32 devices in a mesh: dp: 8 (over z, x), blk: 4 (over y, core).
Axes of the slice: x: 2, y: 2, z: 4, core: 2. Of those that a mesh axis runs over, the one named last changes fastest.
Arguments:
- tokens: bfloat16 [64, 1024, 768], P('dp', 'blk'), may hold values from -6 to 6
- cotangent: bfloat16 [64, 1024, 768], P('dp', 'blk'), may hold values from -6 to 6
- lengths: int32 [64], P('dp'), may hold values from 32 to 1024, as said below
- query_weight: bfloat16 [768, 768], replicated, may hold values from -0.21875 to 0.21875
- query_bias: bfloat16 [768], replicated, may hold values from -3 to 3
- key_weight: bfloat16 [768, 768], replicated, may hold values from -0.21875 to 0.21875
- value_weight: bfloat16 [768, 768], replicated, may hold values from -0.21875 to 0.21875
- value_bias: bfloat16 [768], replicated, may hold values from -3 to 3
- out_weight: bfloat16 [768, 768], replicated, may hold values from -1.75 to 1.75
- out_bias: bfloat16 [768], replicated, may hold values from -3 to 3
- attention_gain: bfloat16 [768], replicated, may hold values from 0.25 to 1.75
- attention_shift: bfloat16 [768], replicated, may hold values from -3 to 3
- inner_weight: bfloat16 [768, 3072], replicated, may hold values from -0.21875 to 0.21875
- inner_bias: bfloat16 [3072], replicated, may hold values from -3 to 3
- outer_weight: bfloat16 [3072, 768], replicated, may hold values from -0.109375 to 0.109375
- outer_bias: bfloat16 [768], replicated, may hold values from -3 to 3
- final_gain: bfloat16 [768], replicated, may hold values from 0.25 to 1.75
- final_shift: bfloat16 [768], replicated, may hold values from -3 to 3
Outputs:
- layer_output: bfloat16 [64, 1024, 768], P('dp', 'blk')
- input_grad: float32 [64, 1024, 768], P('dp', 'blk')
- query_weight_grad: float32 [768, 768], P('blk')
- query_bias_grad: float32 [768], P('blk')
- key_weight_grad: float32 [768, 768], P('blk')
- value_weight_grad: float32 [768, 768], P('blk')
- value_bias_grad: float32 [768], P('blk')
- out_weight_grad: float32 [768, 768], P('blk')
- out_bias_grad: float32 [768], P('blk')
- attention_gain_grad: float32 [768], P('blk')
- attention_shift_grad: float32 [768], P('blk')
- inner_weight_grad: float32 [768, 3072], P('blk')
- inner_bias_grad: float32 [3072], P('blk')
- outer_weight_grad: float32 [3072, 768], P('blk')
- outer_bias_grad: float32 [768], P('blk')
- final_gain_grad: float32 [768], P('blk')
- final_shift_grad: float32 [768], P('blk')
The draws below stay inside these ranges and needn't reach their ends.
Inputs may be any that keep to these rules, and one draw needn't show every extreme that they name: `lengths`: lengths lean toward short ones; among the 8 slots of each index of dp one, chosen at random, has length 1024.
All inputs are finite; a program needn't handle non-finite values.
Results may differ from the reference program's by a relative error of at most 0.03.
Values may be sent and summed in bfloat16 or wider, within the bound.
No kernel may reach another device: no remote copies, remote signals or barrier semaphores. Data moves between devices by JAX's collectives and lax.ppermute only.
A program may use at most 448 MiB of HBM per device.

```python
import jax
import jax.numpy as jnp
from jax import lax

D = 768
HEAD_DIM = 64
FF = 3072
SLOT = 1024
SLOTS_GRP = 8
MIN_LEN = 32
SLOTS = 64


def draw_lengths(key, part):
    key = jax.random.fold_in(key, 11)
    first_key, second_key = jax.random.split(key)
    rolled = jax.random.randint(first_key, (SLOTS,), 0, 64)
    added_len = (SLOT - MIN_LEN) * (rolled * (rolled + 63)) // (63 * 126)
    chosen = jax.random.randint(second_key, (SLOTS // SLOTS_GRP,), 0, SLOTS_GRP)
    slot_ids = jnp.arange(SLOTS, dtype=jnp.int32)
    longest = slot_ids % SLOTS_GRP == chosen[slot_ids // SLOTS_GRP]
    return jnp.where(longest, SLOT, MIN_LEN + added_len).astype(jnp.int32)


def levels(own_key, dims, cuts, least, high):
    def one(position, parts):
        heights = jax.random.uniform(jax.random.fold_in(jax.random.fold_in(own_key, 6), position), (parts,), jnp.float32, least / len(cuts), high / len(cuts))
        return jnp.repeat(jnp.exp(heights), dims[position] // parts).reshape((-1,) + (1,) * (len(dims) - position - 1))

    factor_of = one(*cuts[0])
    for cut in cuts[1:]:
        factor_of = factor_of * one(*cut)
    return factor_of


def noise(rng, shape, width, bound, shards=(), kind=jnp.bfloat16):
    values = jax.random.normal(rng, shape, jnp.float32) * width
    if len(shards) > 0:
        values = levels(rng, shape, shards, -0.22, 0.18) * values
    return jnp.clip(values, min=-bound, max=bound).astype(kind)


def setup_inputs(seed: int = 0) -> dict:
    key_list = jax.random.split(jax.random.key(seed), 19)
    return {
        "tokens": noise(key_list[0], (SLOTS, SLOT, D), 1.0, 6.0, ((0, 8), (1, 4))),
        "cotangent": noise(key_list[1], (SLOTS, SLOT, D), 1.0, 6.0, ((0, 8), (1, 4))),
        "lengths": draw_lengths(jax.random.fold_in(key_list[18], 71), 0),
        "query_weight": noise(key_list[3], (D, D), D ** -0.5, 0.21875),
        "query_bias": noise(key_list[4], (D,), 0.5, 3.0),
        "key_weight": noise(key_list[5], (D, D), D ** -0.5, 0.21875),
        "value_weight": noise(key_list[6], (D, D), D ** -0.5, 0.21875),
        "value_bias": noise(key_list[7], (D,), 0.5, 3.0),
        "out_weight": noise(key_list[8], (D, D), (max(1, D // 64)) ** -0.5, 1.75),
        "out_bias": noise(key_list[9], (D,), 0.3, 3.0),
        "attention_gain": jnp.clip(1.0 + 0.15 * jax.random.normal(key_list[10], (D,), jnp.float32), 0.25, 1.75).astype(jnp.bfloat16),
        "attention_shift": noise(key_list[11], (D,), 0.3, 3.0),
        "inner_weight": noise(key_list[12], (D, FF), D ** -0.5, 0.21875),
        "inner_bias": noise(key_list[13], (FF,), 0.3, 3.0),
        "outer_weight": noise(key_list[14], (FF, D), FF ** -0.5, 0.109375),
        "outer_bias": noise(key_list[15], (D,), 0.3, 3.0),
        "final_gain": jnp.clip(1.0 + 0.15 * jax.random.normal(key_list[16], (D,), jnp.float32), 0.25, 1.75).astype(jnp.bfloat16),
        "final_shift": noise(key_list[17], (D,), 0.3, 3.0),
    }


@jax.custom_vjp
def low(v):
    return lax.optimization_barrier(v.astype(jnp.bfloat16)).astype(jnp.float32)

@jax.custom_vjp
def low_back(v):
    return v

def low_keep(v):
    return (low(v), None)

def low_pass(kept, grad):
    return (grad,)

def back_keep(v):
    return (v, None)

def back_low(kept, grad):
    return (low(grad),)
low.defvjp(low_keep, low_pass)
low_back.defvjp(back_keep, back_low)
EPSILON = 1e-06
NEGATIVE = -1e+30
HIGHEST = lax.Precision.HIGHEST

def rounded(values):
    return low(low_back(values))

def layer_norm(values, norm_gain, norm_shift):
    center = values - lax.optimization_barrier(jnp.mean(values, axis=-1, keepdims=True))
    return center * lax.rsqrt(lax.optimization_barrier(jnp.mean(center * center, axis=-1, keepdims=True)) + EPSILON) * norm_gain + norm_shift

def attend(pieces):
    queries, key_rows, value_rows, allowed = pieces
    scores = jnp.einsum('qhd,khd->hqk', queries, key_rows, precision=HIGHEST) * HEAD_DIM ** (-0.5)
    scores = low_back(scores)
    scores = jnp.where(allowed[None, None, :], scores, NEGATIVE)
    peak_score = lax.optimization_barrier(jnp.max(scores, axis=-1, keepdims=True))
    weights = jnp.where(allowed[None, None, :], jnp.exp(scores - peak_score), 0.0)
    probs = weights / lax.optimization_barrier(jnp.sum(weights, axis=-1, keepdims=True))
    return jnp.einsum('hqk,khd->qhd', low(probs), value_rows, precision=HIGHEST)

def layer(inputs, allowed, params):
    query_weight, query_bias, key_weight, value_weight, value_bias, out_weight, out_bias, attention_gain, attention_shift, inner_weight, inner_bias, outer_weight, outer_bias, final_gain, final_shift = params
    slot_count, slot_len, features = inputs.shape
    head_count = features // HEAD_DIM
    split_shape = (slot_count, slot_len, head_count, HEAD_DIM)
    flat = inputs.reshape(slot_count * slot_len, features)
    lowered = low(flat)
    queries = rounded(jnp.dot(lowered, query_weight, precision=HIGHEST) + query_bias)
    key_rows = rounded(jnp.dot(lowered, key_weight, precision=HIGHEST))
    value_rows = rounded(jnp.dot(lowered, value_weight, precision=HIGHEST) + value_bias)
    context = lax.map(jax.checkpoint(attend), (queries.reshape(split_shape), key_rows.reshape(split_shape), value_rows.reshape(split_shape), allowed))
    context = rounded(context.reshape(slot_count * slot_len, features))
    branch = low_back(jnp.dot(context, out_weight, precision=HIGHEST) + out_bias)
    middle = layer_norm(flat + branch, attention_gain, attention_shift)
    hidden = low_back(jnp.dot(low(middle), inner_weight, precision=HIGHEST) + inner_bias)
    activated = low(jax.nn.gelu(hidden, approximate=True))
    feed_out = low_back(jnp.dot(activated, outer_weight, precision=HIGHEST) + outer_bias)
    return layer_norm(middle + feed_out, final_gain, final_shift).reshape(slot_count, slot_len, features)

def reference(tokens, cotangent, lengths, query_weight, query_bias, key_weight, value_weight, value_bias, out_weight, out_bias, attention_gain, attention_shift, inner_weight, inner_bias, outer_weight, outer_bias, final_gain, final_shift):
    params = (query_weight.astype(jnp.float32), query_bias.astype(jnp.float32), key_weight.astype(jnp.float32), value_weight.astype(jnp.float32), value_bias.astype(jnp.float32), out_weight.astype(jnp.float32), out_bias.astype(jnp.float32), attention_gain.astype(jnp.float32), attention_shift.astype(jnp.float32), inner_weight.astype(jnp.float32), inner_bias.astype(jnp.float32), outer_weight.astype(jnp.float32), outer_bias.astype(jnp.float32), final_gain.astype(jnp.float32), final_shift.astype(jnp.float32))
    group_count = SLOTS // SLOTS_GRP
    grouped = (group_count, SLOTS_GRP, SLOT, D)
    positions = jnp.arange(SLOT, dtype=jnp.int32)

    def run(running_totals, pieces):
        inputs, incoming, group_lengths = pieces
        allowed = positions[None, :] < group_lengths[:, None]
        keep = allowed[:, :, None].astype(jnp.float32)

        def forward_apply(start, weights):
            return layer(layer(start, allowed, weights), allowed, weights) * keep
        result, pullback = jax.vjp(forward_apply, inputs.astype(jnp.float32), params)
        grad_input, grad_params = pullback(incoming.astype(jnp.float32))
        running_totals = jax.tree.map(jnp.add, running_totals, grad_params)
        return (running_totals, (result.astype(jnp.bfloat16), grad_input))
    start_totals = jax.tree.map(jnp.zeros_like, params)
    running_totals, (results, grad_inputs) = lax.scan(run, start_totals, (tokens.reshape(grouped), cotangent.reshape(grouped), lengths.reshape(group_count, SLOTS_GRP)))
    return (results.reshape(SLOTS, SLOT, D), grad_inputs.reshape(SLOTS, SLOT, D), running_totals[0], running_totals[1], running_totals[2], running_totals[3], running_totals[4], running_totals[5], running_totals[6], running_totals[7], running_totals[8], running_totals[9], running_totals[10], running_totals[11], running_totals[12], running_totals[13], running_totals[14])
```

```python
from functools import partial
import math

import jax
import jax.numpy as jnp
from jax import lax
from jax.experimental import pallas as pl
from jax.experimental.pallas import tpu as pltpu
from jax.sharding import PartitionSpec as P

HEAD_DIM = 64
EPSILON = 1e-06
NEGATIVE = -1e30
LOG2E = math.log2(math.e)
LN2 = math.log(2.0)
SCORE_SCALE = HEAD_DIM ** (-0.5)
GELU_C = math.sqrt(2.0 / math.pi)
VMEM_LIMIT = 60 * 2**20
BF = jnp.bfloat16
F32 = jnp.float32
(P_QB, P_VB, P_OB, P_AG, P_AS, P_UB, P_FG, P_FS) = range(8)


def dot_nt(a, b):
    return lax.dot_general(a, b, (((1,), (1,)), ((), ())), preferred_element_type=F32)


def dot_nn(a, b):
    return lax.dot_general(a, b, (((1,), (0,)), ((), ())), preferred_element_type=F32)


def dot_tn(a, b):
    return lax.dot_general(a, b, (((0,), (0,)), ((), ())), preferred_element_type=F32)


def params_of(**extra):
    return pltpu.CompilerParams(vmem_limit_bytes=VMEM_LIMIT, **extra)


def plan_kernel(own, devices, tile, len_ref, me_ref, out_ref):
    slots = len_ref.shape[0]
    me = me_ref[0]
    total = own * devices
    order = 2 * own + 2
    for r in range(total):
        out_ref[order + r] = -1
    for i in range(slots):
        n = len_ref[i]
        rank = jnp.int32(0)
        for j in range(slots):
            if j != i:
                m = len_ref[j]
                before = (m >= n) if j < i else (m > n)
                rank = rank + before.astype(jnp.int32)
        row = lax.div(rank, devices)
        col = lax.rem(rank, devices)
        owner = jnp.where(lax.rem(row, 2) == 0, col, devices - 1 - col)
        out_ref[order + owner * own + row] = i
    start = jnp.int32(0)
    for j in range(own):
        s = out_ref[order + me * own + j]
        n = jnp.where(s >= 0, len_ref[jnp.maximum(s, 0)], 0)
        out_ref[2 * j] = start
        out_ref[2 * j + 1] = n
        start = start + lax.div(n + 127, 128) * 128
    out_ref[2 * own] = jnp.maximum(lax.div(start + tile - 1, tile), 1)
    out_ref[2 * own + 1] = me


def make_plan(lengths, me, own, devices, tile):
    return pl.pallas_call(
        partial(plan_kernel, own, devices, tile),
        in_specs=[pl.BlockSpec(memory_space=pltpu.SMEM)] * 2,
        out_specs=pl.BlockSpec(memory_space=pltpu.SMEM),
        out_shape=jax.ShapeDtypeStruct((2 * own + 2 + own * devices,), jnp.int32),
    )(lengths, me)


def copy_kernel(plan, source, out):
    out[...] = source[...]


def gather_slots(plan, source, own, devices):
    slots, span, features = source.shape
    block = (1, span, features)
    order = 2 * own + 2
    return pl.pallas_call(
        copy_kernel,
        grid_spec=pltpu.PrefetchScalarGridSpec(
            num_scalar_prefetch=1,
            grid=(own * devices,),
            in_specs=[
                pl.BlockSpec(block, lambda i, plan: (jnp.maximum(plan[order + i], 0), 0, 0))
            ],
            out_specs=pl.BlockSpec(block, lambda i, plan: (i, 0, 0)),
        ),
        out_shape=jax.ShapeDtypeStruct((own * devices, span, features), source.dtype),
    )(plan, source)


def pack_kernel(own, devices, chunk, plan, parts, packed, sems):
    span = parts.shape[1]
    pieces = span // chunk

    def each(action):
        for s in range(devices):
            for j in range(own):
                for c in range(pieces):
                    first = s * span + c * chunk
                    at = pl.multiple_of(plan[2 * j] + first, chunk)

                    @pl.when(first < plan[2 * j + 1])
                    def _():
                        action(
                            pltpu.make_async_copy(
                                parts.at[s * own + j, pl.ds(c * chunk, chunk)],
                                packed.at[pl.ds(at, chunk)],
                                sems.at[(s * own + j) * pieces + c],
                            )
                        )

    each(lambda copy: copy.start())
    each(lambda copy: copy.wait())


def pack_rows(plan, parts, own, devices, rows):
    total, span, features = parts.shape
    chunk = min(128, span)
    return pl.pallas_call(
        partial(pack_kernel, own, devices, chunk),
        grid_spec=pltpu.PrefetchScalarGridSpec(
            num_scalar_prefetch=1,
            grid=(1,),
            in_specs=[pl.BlockSpec(memory_space=pl.ANY)],
            out_specs=pl.BlockSpec((rows, features), lambda i, plan: (0, 0)),
            scratch_shapes=[pltpu.SemaphoreType.DMA((total * (span // chunk),))],
        ),
        out_shape=jax.ShapeDtypeStruct((rows, features), parts.dtype),
        compiler_params=params_of(),
    )(plan, parts)


def unpack_kernel(own, devices, span, plan, packed, parts, sems):
    copies = []
    for d in range(devices):
        for j in range(own):
            at = pl.multiple_of(plan[2 * j] + d * span, min(128, span))
            i = d * own + j
            copies.append(
                pltpu.make_async_copy(packed.at[pl.ds(at, span)], parts.at[i], sems.at[i])
            )
    for copy in copies:
        copy.start()
    for copy in copies:
        copy.wait()


def unpack_rows(plan, packed, own, devices, span):
    total = own * devices
    rows, features = packed.shape
    return pl.pallas_call(
        partial(unpack_kernel, own, devices, span),
        grid_spec=pltpu.PrefetchScalarGridSpec(
            num_scalar_prefetch=1,
            grid=(1,),
            in_specs=[pl.BlockSpec((rows, features), lambda i, plan: (0, 0))],
            out_specs=pl.BlockSpec(memory_space=pl.ANY),
            scratch_shapes=[pltpu.SemaphoreType.DMA((total,))],
        ),
        out_shape=jax.ShapeDtypeStruct((total, span, features), packed.dtype),
        compiler_params=params_of(),
    )(plan, packed)


def place_kernel(own, devices, plan, lengths, parts, out):
    total, span, features = parts.shape
    order = 2 * own + 2
    row = lax.broadcasted_iota(jnp.int32, (span, features), 0) + plan[2 * own + 1] * span
    for i in range(total):
        slot = plan[order + i]

        @pl.when(slot >= 0)
        def _():
            keep = row < lengths[slot]
            out[slot] = jnp.where(keep, parts[i].astype(F32), 0.0).astype(out.dtype)


def place_slots(plan, lengths, parts, own, devices, out_type):
    total, span, features = parts.shape
    slots = lengths.shape[0]
    return pl.pallas_call(
        partial(place_kernel, own, devices),
        grid_spec=pltpu.PrefetchScalarGridSpec(
            num_scalar_prefetch=2,
            grid=(1,),
            in_specs=[pl.BlockSpec((total, span, features), lambda i, *_: (0, 0, 0))],
            out_specs=pl.BlockSpec((slots, span, features), lambda i, *_: (0, 0, 0)),
        ),
        out_shape=jax.ShapeDtypeStruct((slots, span, features), out_type),
        compiler_params=params_of(),
    )(plan, lengths, parts)


def exchanged(parts, devices):
    total, span, features = parts.shape
    parts = parts.reshape(devices, total // devices * span, features)
    parts = lax.all_to_all(parts, "blk", 0, 0)
    return parts.reshape(total, span, features)


def rows_valid(plan, own, tile, shape):
    row = lax.broadcasted_iota(jnp.int32, shape, 0) + pl.program_id(0) * tile
    valid = None
    for j in range(own):
        start = plan[2 * j]
        inside = (row >= start) & (row < start + plan[2 * j + 1])
        valid = inside if valid is None else valid | inside
    return valid


def normed_rows(values):
    center = values - jnp.mean(values, axis=-1, keepdims=True)
    inverse = lax.rsqrt(jnp.mean(center * center, axis=-1, keepdims=True) + EPSILON)
    return center * inverse, inverse


def norm_back(grad_out, normed, inverse, gain):
    scaled = grad_out * gain
    mean_part = jnp.mean(scaled, axis=-1, keepdims=True)
    along_part = jnp.mean(scaled * normed, axis=-1, keepdims=True)
    return inverse * (scaled - mean_part - normed * along_part)


def column_sum(values):
    return jnp.sum(values, axis=0, keepdims=True)


def project_qkv(low, wq, wk, wv, small, out):
    features = low.shape[1]
    out[:, :features] = (
        (dot_nn(low, wq[...]) + small[P_QB : P_QB + 1]) * (SCORE_SCALE * LOG2E)
    ).astype(BF)
    out[:, features : 2 * features] = dot_nn(low, wk[...]).astype(BF)
    out[:, 2 * features :] = (dot_nn(low, wv[...]) + small[P_VB : P_VB + 1]).astype(BF)


def qkv_kernel(own, tile, plan, x, wq, wk, wv, small, out):
    valid = rows_valid(plan, own, tile, x.shape)
    project_qkv(jnp.where(valid, x[...], 0), wq, wk, wv, small, out)


def gelu_parts(u):
    square = u * u
    t = jnp.tanh(u * (GELU_C + (GELU_C * 0.044715) * square))
    half = 0.5 + 0.5 * t
    slope = half + (0.5 * u) * (1.0 - t * t) * (GELU_C + (3 * GELU_C * 0.044715) * square)
    return u * half, slope


def feed_forward(context, x, wo, wi, wu, small, inner_bias, act, slope, width):
    pre = x + (dot_nn(context, wo[...]) + small[P_OB : P_OB + 1])
    normed1, inverse1 = normed_rows(pre)
    middle = normed1 * small[P_AG : P_AG + 1] + small[P_AS : P_AS + 1]
    low = middle.astype(BF)
    hidden_features = wi.shape[1]
    feed = None
    for c in range(0, hidden_features, width):
        cols = slice(c, c + width)
        hidden = dot_nn(low, wi[:, cols]) + inner_bias[:, cols]
        activated, grad = gelu_parts(hidden)
        activated = activated.astype(BF)
        act[:, cols] = activated
        slope[:, cols] = grad.astype(BF)
        part = dot_nn(activated, wu[cols, :])
        feed = part if feed is None else feed + part
    normed2, inverse2 = normed_rows(middle + (feed + small[P_UB : P_UB + 1]))
    return normed1, inverse1, low, normed2, inverse2


def post_kernel(
    own, tile, width, plan, context, x, wo, wi, wu, wq, wk, wv, small, inner_bias,
    normed1_out, normed2_out, inverse_out, act_out, slope_out, qkv_out,
):
    valid = rows_valid(plan, own, tile, x.shape)
    ctx = jnp.where(valid, context[...], 0)
    rows = jnp.where(valid, x[...], 0).astype(F32)
    normed1, inverse1, _, normed2, inverse2 = feed_forward(
        ctx, rows, wo, wi, wu, small, inner_bias, act_out, slope_out, width
    )
    normed1_out[...] = normed1
    normed2_out[...] = normed2
    lane = lax.broadcasted_iota(jnp.int32, inverse_out.shape, 1)
    inverse_out[...] = jnp.where(lane < 64, inverse1, inverse2)
    low = (normed2 * small[P_FG : P_FG + 1] + small[P_FS : P_FS + 1]).astype(BF)
    project_qkv(low, wq, wk, wv, small, qkv_out)


def feed_back(
    grad, ctx, low, normed1, inverse1, normed2, inverse2, act, slope, wo, wi, wu, small,
    width, acc_inner, acc_outer, acc_out, sums, inner_sum,
):
    sums[5:6] += column_sum(grad * normed2)
    sums[6:7] += column_sum(grad)
    dsum = norm_back(grad, normed2, inverse2, small[P_FG : P_FG + 1])
    dfeed = dsum.astype(BF)
    sums[4:5] += column_sum(dfeed.astype(F32))
    hidden_features = wi.shape[1]
    dmiddle = dsum
    for c in range(0, hidden_features, width):
        cols = slice(c, c + width)
        acc_outer[cols, :] += dot_tn(act[:, cols], dfeed)
        dhidden = (dot_nt(dfeed, wu[cols, :]) * slope[:, cols].astype(F32)).astype(BF)
        inner_sum[:, cols] += column_sum(dhidden.astype(F32))
        acc_inner[:, cols] += dot_tn(low, dhidden)
        dmiddle = dmiddle + dot_nt(dhidden, wi[:, cols])
    sums[2:3] += column_sum(dmiddle * normed1)
    sums[3:4] += column_sum(dmiddle)
    dpre = norm_back(dmiddle, normed1, inverse1, small[P_AG : P_AG + 1])
    dbranch = dpre.astype(BF)
    sums[1:2] += column_sum(dbranch.astype(F32))
    acc_out[...] += dot_tn(ctx, dbranch)
    return dpre, dot_nt(dbranch, wo[...]).astype(BF)


def flush_pieces(pieces, earlier, result, stage, stage_in, sems, sems_in):
    devices = result.shape[0]

    def shape_of(rows):
        return (devices, rows // devices, result.shape[2])

    def out_copy(i):
        _, at, rows = pieces[i]
        each = rows // devices
        return pltpu.make_async_copy(
            stage.at[i % 2, :, pl.ds(0, each)], result.at[:, pl.ds(at, each)], sems.at[i % 2]
        )

    def in_copy(i):
        _, at, rows = pieces[i]
        each = rows // devices
        return pltpu.make_async_copy(
            earlier.at[:, pl.ds(at, each)], stage_in.at[i % 2, :, pl.ds(0, each)], sems_in.at[i % 2]
        )

    if earlier is not None:
        in_copy(0).start()
    for i, (load, at, rows) in enumerate(pieces):
        each = rows // devices
        if earlier is not None:
            if i + 1 < len(pieces):
                in_copy(i + 1).start()
            in_copy(i).wait()
        if i >= 2:
            out_copy(i - 2).wait()
        value = load().reshape(shape_of(rows))
        if earlier is not None:
            value = value + stage_in[i % 2, :, :each].astype(F32)
        stage[i % 2, :, :each] = value.astype(BF)
        out_copy(i).start()
    for i in range(max(0, len(pieces) - 2), len(pieces)):
        out_copy(i).wait()


def feed_pieces(acc_inner, acc_outer, acc_out, devices):
    features, hidden_features = acc_inner.shape
    pieces = []
    at = 0
    for c in range(0, hidden_features, features):
        pieces.append((lambda c=c: acc_inner[:, c : c + features], at, features))
        at += features // devices
    each = hidden_features // devices
    for c in range(0, hidden_features, features):
        rows = features // devices
        def load(c=c, rows=rows):
            first = c // devices
            return jnp.concatenate(
                [acc_outer[b * each + first : b * each + first + rows, :] for b in range(devices)], 0
            )
        pieces.append((load, at, features))
        at += rows
    pieces.append((lambda: acc_out[...], at, features))
    return pieces


def second_kernel(
    own, tile, width, plan, context, normed_in, cotangent, wo, wi, wu, small, inner_bias,
    layer_out, dctx_out, dpre_out, grads_out, sums_out, inner_sum_out,
    act, slope, acc_inner, acc_outer, acc_out, sums, inner_sum, stage, sems,
):
    step = pl.program_id(0)

    @pl.when(step == 0)
    def _():
        for ref in (acc_inner, acc_outer, acc_out, sums, inner_sum):
            ref[...] = jnp.zeros_like(ref)

    valid = rows_valid(plan, own, tile, context.shape)
    ctx = jnp.where(valid, context[...], 0)
    x = normed_in[...] * small[P_FG : P_FG + 1] + small[P_FS : P_FS + 1]
    normed1, inverse1, low, normed2, inverse2 = feed_forward(
        ctx, x, wo, wi, wu, small, inner_bias, act, slope, width
    )
    layer_out[...] = (normed2 * small[P_FG : P_FG + 1] + small[P_FS : P_FS + 1]).astype(BF)
    grad = jnp.where(valid, cotangent[...], 0).astype(F32)
    dpre_out[...], dctx_out[...] = feed_back(
        grad, ctx, low, normed1, inverse1, normed2, inverse2, act, slope, wo, wi, wu, small,
        width, acc_inner, acc_outer, acc_out, sums, inner_sum,
    )

    @pl.when(step == plan[2 * own] - 1)
    def _():
        sums_out[...] = sums[...]
        inner_sum_out[...] = inner_sum[...]
        pieces = feed_pieces(acc_inner, acc_outer, acc_out, grads_out.shape[0])
        flush_pieces(pieces, None, grads_out, stage, None, sems, None)


def first_kernel(
    own, tile, width, plan, context, normed1_in, normed2_in, inverse_in, act, slope, grad,
    wo, wi, wu, small, earlier, sums_in, inner_sum_in,
    dctx_out, dpre_out, grads_out, sums_out, inner_sum_out,
    acc_inner, acc_outer, acc_out, sums, inner_sum, stage, sems, stage_in, sems_in,
):
    step = pl.program_id(0)

    @pl.when(step == 0)
    def _():
        for ref in (acc_inner, acc_outer, acc_out):
            ref[...] = jnp.zeros_like(ref)
        sums[...] = sums_in[...]
        inner_sum[...] = inner_sum_in[...]

    valid = rows_valid(plan, own, tile, context.shape)
    ctx = jnp.where(valid, context[...], 0)
    normed1 = normed1_in[...]
    low = (normed1 * small[P_AG : P_AG + 1] + small[P_AS : P_AS + 1]).astype(BF)
    inverse = inverse_in[...]
    dpre_out[...], dctx_out[...] = feed_back(
        grad[...], ctx, low, normed1, inverse[:, 0:1], normed2_in[...], inverse[:, 64:65],
        act, slope, wo, wi, wu, small, width, acc_inner, acc_outer, acc_out, sums, inner_sum,
    )

    @pl.when(step == plan[2 * own] - 1)
    def _():
        sums_out[...] = sums[...]
        inner_sum_out[...] = inner_sum[...]
        pieces = feed_pieces(acc_inner, acc_outer, acc_out, grads_out.shape[0])
        flush_pieces(pieces, earlier, grads_out, stage, stage_in, sems, sems_in)


def qkv_back_kernel(
    own, tile, from_norm, plan, dq, dk, dv, x, dpre, wq, wk, wv, small, *rest
):
    if from_norm:
        dx_out, grads_out, sums_out, acc, sums, stage, sems = rest
        earlier, stage_in, sems_in = None, None, None
    else:
        earlier, sums_in, dx_out, grads_out, sums_out, acc, sums, stage, sems, stage_in, sems_in = rest
    step = pl.program_id(0)

    @pl.when(step == 0)
    def _():
        acc[...] = jnp.zeros_like(acc)
        sums[...] = jnp.zeros_like(sums) if from_norm else sums_in[...]

    valid = rows_valid(plan, own, tile, dpre.shape)
    gq = jnp.where(valid, dq[...], 0)
    gk = jnp.where(valid, dk[...], 0)
    gv = jnp.where(valid, dv[...], 0)
    if from_norm:
        low = (x[...] * small[P_FG : P_FG + 1] + small[P_FS : P_FS + 1]).astype(BF)
    else:
        low = jnp.where(valid, x[...], 0)
    dx = dpre[...] + dot_nt(gq, wq[...]) + dot_nt(gk, wk[...]) + dot_nt(gv, wv[...])
    dx_out[...] = dx.astype(dx_out.dtype)
    acc[0] += dot_tn(low, gq)
    acc[1] += dot_tn(low, gk)
    acc[2] += dot_tn(low, gv)
    sums[0:1] += column_sum(gq.astype(F32))
    sums[1:2] += column_sum(gv.astype(F32))

    @pl.when(step == plan[2 * own] - 1)
    def _():
        sums_out[...] = sums[...]
        features = acc.shape[1]
        each = features // grads_out.shape[0]
        pieces = [(lambda i=i: acc[i], i * each, features) for i in range(3)]
        flush_pieces(pieces, earlier, grads_out, stage, stage_in, sems, sems_in)


class Rows:
    def __init__(self, plan, own, rows, tile, steps):
        self.plan, self.own, self.rows, self.tile, self.steps = plan, own, rows, tile, steps

    def tile_spec(self, width):
        last = 2 * self.own
        return pl.BlockSpec((self.tile, width), lambda i, plan: (jnp.minimum(i, plan[last] - 1), 0))

    def call(self, kernel, tiled, whole, far, tiled_out, whole_out, far_out, scratch):
        def whole_spec(shape):
            return pl.BlockSpec(shape, lambda i, *_: (0,) * len(shape), pipeline_mode=pl.Buffered(1))

        def whole_out_spec(shape):
            return pl.BlockSpec(shape, lambda i, *_: (0,) * len(shape))

        in_specs = [self.tile_spec(a.shape[1]) for a in tiled]
        in_specs += [whole_spec(a.shape) for a in whole]
        in_specs += [
            pl.BlockSpec(memory_space=pl.ANY) if is_far else whole_out_spec(a.shape)
            for a, is_far in far
        ]
        out_specs = [self.tile_spec(width) for width, _ in tiled_out]
        out_specs += [pl.BlockSpec(memory_space=pl.ANY) for _ in far_out]
        out_specs += [whole_out_spec(shape) for shape, _ in whole_out]
        out_shape = [jax.ShapeDtypeStruct((self.rows, width), kind) for width, kind in tiled_out]
        out_shape += [jax.ShapeDtypeStruct(shape, kind) for shape, kind in far_out]
        out_shape += [jax.ShapeDtypeStruct(shape, kind) for shape, kind in whole_out]
        def guarded(plan, *refs):
            @pl.when(pl.program_id(0) < plan[2 * self.own])
            def _():
                kernel(plan, *refs)

        return pl.pallas_call(
            guarded,
            grid_spec=pltpu.PrefetchScalarGridSpec(
                num_scalar_prefetch=1,
                grid=(self.steps,),
                in_specs=in_specs,
                out_specs=out_specs,
                scratch_shapes=scratch,
            ),
            out_shape=out_shape,
            compiler_params=params_of(),
        )(self.plan, *tiled, *whole, *[a for a, _ in far])


def forward_attention(own, slot_len, step_keys, tq, plan, q_ref, k_ref, v_ref, o_ref, of_ref, li_ref, m_ref, ka, va):
    lane_q = lax.broadcasted_iota(jnp.int32, (tq, 128), 1)
    low_q = lane_q < 64
    one0 = jnp.where(lane_q == 64, 1.0, 0.0).astype(BF)
    one1 = jnp.where(lane_q == 0, 1.0, 0.0).astype(BF)

    def slot(j, keys):
        start = pl.multiple_of(plan[2 * j], 128)
        n = plan[2 * j + 1]
        lane = lax.broadcasted_iota(jnp.int32, (keys, 128), 1)
        real = lax.broadcasted_iota(jnp.int32, (keys, 128), 0) < n
        low = lane < 64
        k = jnp.where(real, k_ref[pl.ds(start, keys), :], 0)
        v = jnp.where(real, v_ref[pl.ds(start, keys), :], 0)
        bias = jnp.where(real, 0.0, NEGATIVE).astype(BF)
        ka[0, :keys] = jnp.where(low, k, jnp.where(lane == 64, bias, 0))
        ka[1, :keys] = jnp.where(low, jnp.where(lane == 0, bias, 0), k)
        va[0, :keys] = jnp.where(low, v, 1.0)
        va[1, :keys] = jnp.where(low, 1.0, v)

        def scores(r):
            q = q_ref[pl.ds(r, tq), :]
            s0 = dot_nt(jnp.where(low_q, q, one0), ka[0, :keys])
            s1 = dot_nt(jnp.where(low_q, one1, q), ka[1, :keys])
            return s0, s1

        def finish(r, e0, e1):
            o0 = dot_nn(e0.astype(BF), va[0, :keys])
            o1 = dot_nn(e1.astype(BF), va[1, :keys])
            total = jnp.where(low_q, pltpu.roll(o0, 64, 1), pltpu.roll(o1, 64, 1))
            li = 1.0 / total
            out = jnp.where(low_q, o0, o1) * li
            o_ref[pl.ds(r, tq), :] = out.astype(BF)
            of_ref[pl.ds(r, tq), :] = out
            li_ref[pl.ds(r, tq), :] = li
            return total

        def plain_tile(i, bad):
            r = pl.multiple_of(start + i * tq, 128)
            s0, s1 = scores(r)
            total = finish(r, jnp.exp2(s0), jnp.exp2(s1))
            m_ref[pl.ds(r, tq), :] = jnp.zeros((tq, 128), F32)
            good = (total > 2.0**-60) & (total < 2.0**80)
            return jnp.maximum(bad, jnp.where(good, 0.0, 1.0))

        tiles = lax.div(n + tq - 1, tq)
        bad = lax.fori_loop(0, tiles, plain_tile, jnp.zeros((tq, 128), F32))

        @pl.when(jnp.max(bad) > 0.0)
        def _():
            def safe_tile(i, c):
                r = pl.multiple_of(start + i * tq, 128)
                s0, s1 = scores(r)
                m0 = jnp.max(s0, axis=1, keepdims=True)
                m1 = jnp.max(s1, axis=1, keepdims=True)
                finish(r, jnp.exp2(s0 - m0), jnp.exp2(s1 - m1))
                m_ref[pl.ds(r, tq), :] = jnp.where(low_q, m0, m1)
                return c

            lax.fori_loop(0, tiles, safe_tile, 0)

    for j in range(own):
        n = plan[2 * j + 1]
        for keys in range(step_keys, slot_len + 1, step_keys):

            @pl.when((n > keys - step_keys) & (n <= keys))
            def _():
                slot(j, keys)


def backward_attention(
    own, slot_len, step_keys, tq, plan, q_ref, k_ref, v_ref, o_ref, do_ref, li_ref, m_ref,
    dq_ref, dk_ref, dv_ref, ka, km, va, dka, dva,
):
    lane_q = lax.broadcasted_iota(jnp.int32, (tq, 128), 1)
    low_q = lane_q < 64
    place = lax.rem(lane_q, 64)

    def slot(j, keys):
        start = pl.multiple_of(plan[2 * j], 128)
        n = plan[2 * j + 1]
        lane = lax.broadcasted_iota(jnp.int32, (keys, 128), 1)
        real = lax.broadcasted_iota(jnp.int32, (keys, 128), 0) < n
        low = lane < 64
        k = jnp.where(real, k_ref[pl.ds(start, keys), :], 0)
        v = jnp.where(real, v_ref[pl.ds(start, keys), :], 0)
        bias = jnp.where(real, 0.0, NEGATIVE).astype(BF)

        def beside_k(base):
            return jnp.where(
                lane == base, bias, jnp.where((lane > base) & (lane <= base + 3), 1.0, 0.0).astype(BF)
            )

        def beside_v(base):
            return jnp.where((lane >= base) & (lane < base + 2), 1.0, 0.0).astype(BF)

        ka[0, :keys] = jnp.where(low, k, beside_k(64))
        ka[1, :keys] = jnp.where(low, beside_k(0), k)
        km[0, :keys] = jnp.where(low, k, 0)
        km[1, :keys] = jnp.where(low, 0, k)
        va[0, :keys] = jnp.where(low, v, beside_v(64))
        va[1, :keys] = jnp.where(low, beside_v(0), v)
        dka[:, :keys] = jnp.zeros((128, keys), F32)
        dva[:, :keys] = jnp.zeros((128, keys), F32)

        def tile(i, c):
            r = pl.multiple_of(start + i * tq, 128)
            real_q = lax.broadcasted_iota(jnp.int32, (tq, 128), 0) + i * tq < n
            q = jnp.where(real_q, q_ref[pl.ds(r, tq), :], 0)
            li = jnp.where(real_q, li_ref[pl.ds(r, tq), :], 0.0)
            m = jnp.where(real_q, m_ref[pl.ds(r, tq), :], 0.0)
            do = (jnp.where(real_q, do_ref[pl.ds(r, tq), :].astype(F32), 0.0) * li).astype(BF)
            product = jnp.where(real_q, do.astype(F32) * o_ref[pl.ds(r, tq), :], 0.0)
            delta0 = -jnp.sum(jnp.where(low_q, product, 0.0), axis=1, keepdims=True)
            delta1 = -jnp.sum(jnp.where(low_q, 0.0, product), axis=1, keepdims=True)
            m_other = -pltpu.roll(m, 64, 1)
            m_high = m_other.astype(BF).astype(F32)
            m_mid = (m_other - m_high).astype(BF).astype(F32)
            m_last = m_other - m_high - m_mid
            beside_q = jnp.where(
                place == 0,
                1.0,
                jnp.where(
                    place == 1, m_high, jnp.where(place == 2, m_mid, jnp.where(place == 3, m_last, 0.0))
                ),
            ).astype(BF)

            def beside_do(delta):
                high = delta.astype(BF).astype(F32)
                return jnp.where(place == 0, high, jnp.where(place == 1, delta - high, 0.0)).astype(BF)

            e0 = jnp.exp2(dot_nt(jnp.where(low_q, q, beside_q), ka[0, :keys]))
            e1 = jnp.exp2(dot_nt(jnp.where(low_q, beside_q, q), ka[1, :keys]))
            ds0 = (e0 * dot_nt(jnp.where(low_q, do, beside_do(delta0)), va[0, :keys])).astype(BF)
            ds1 = (e1 * dot_nt(jnp.where(low_q, beside_do(delta1), do), va[1, :keys])).astype(BF)
            dq = dot_nn(ds0, km[0, :keys]) + dot_nn(ds1, km[1, :keys])
            dq_ref[pl.ds(r, tq), :] = (dq * SCORE_SCALE).astype(BF)
            q_t = q.T
            do_t = do.T
            dva[:64, :keys] += dot_nn(do_t[:64], e0.astype(BF))
            dva[64:, :keys] += dot_nn(do_t[64:], e1.astype(BF))
            dka[:64, :keys] += dot_nn(q_t[:64], ds0)
            dka[64:, :keys] += dot_nn(q_t[64:], ds1)
            return c

        lax.fori_loop(0, lax.div(n + tq - 1, tq), tile, 0)
        dk_ref[pl.ds(start, keys), :] = (dka[:, :keys].T * LN2).astype(BF)
        dv_ref[pl.ds(start, keys), :] = dva[:, :keys].T.astype(BF)

    for j in range(own):
        n = plan[2 * j + 1]
        for keys in range(step_keys, slot_len + 1, step_keys):

            @pl.when((n > keys - step_keys) & (n <= keys))
            def _():
                slot(j, keys)


class Attention:
    def __init__(self, plan, own, slot_len, rows, features):
        self.plan, self.own, self.slot_len = plan, own, slot_len
        self.rows, self.features = rows, features
        self.pairs = features // 128
        self.step = min(256, slot_len)

    def spec(self, shift=0):
        return pl.BlockSpec((self.rows, 128), lambda p, *_: (0, p + shift))

    def call(self, kernel, in_specs, kinds, scratch, *args):
        return pl.pallas_call(
            partial(kernel, self.own, self.slot_len, self.step, self.step),
            grid_spec=pltpu.PrefetchScalarGridSpec(
                num_scalar_prefetch=1,
                grid=(self.pairs,),
                in_specs=in_specs,
                out_specs=[self.spec()] * len(kinds),
                scratch_shapes=scratch,
            ),
            out_shape=[jax.ShapeDtypeStruct((self.rows, self.features), kind) for kind in kinds],
            compiler_params=params_of(),
        )(self.plan, *args)

    def qkv_specs(self):
        return [self.spec(), self.spec(self.pairs), self.spec(2 * self.pairs)]

    def forward(self, qkv):
        scratch = [pltpu.VMEM((2, self.slot_len, 128), BF)] * 2
        return self.call(
            forward_attention, self.qkv_specs(), (BF, F32, F32, F32), scratch, qkv, qkv, qkv
        )

    def backward(self, qkv, out, inverse, peak, grad):
        scratch = [pltpu.VMEM((2, self.slot_len, 128), BF)] * 3
        scratch += [pltpu.VMEM((128, self.slot_len), F32)] * 2
        return self.call(
            backward_attention,
            self.qkv_specs() + [self.spec()] * 4,
            (BF, BF, BF),
            scratch,
            qkv,
            qkv,
            qkv,
            out,
            grad,
            inverse,
            peak,
        )


def summed_shares(grads):
    share = lax.psum_scatter(grads, "blk", scatter_dimension=0, tiled=True)
    return lax.psum(share, "dp")[0]


def on_device(
    tokens,
    cotangent,
    lengths,
    query_weight,
    query_bias,
    key_weight,
    value_weight,
    value_bias,
    out_weight,
    out_bias,
    attention_gain,
    attention_shift,
    inner_weight,
    inner_bias,
    outer_weight,
    outer_bias,
    final_gain,
    final_shift,
):
    devices = lax.axis_size("blk")
    slots, span, features = tokens.shape
    hidden_features = inner_weight.shape[1]
    slot_len = devices * span
    own = -(-slots // devices)
    tile = min(256, slot_len)
    rows = own * slot_len + tile
    width = features
    me = lax.axis_index("blk").astype(jnp.int32).reshape(1)
    plan = make_plan(lengths, me, own, devices, tile)

    def exchange_in(array):
        parts = exchanged(gather_slots(plan, array, own, devices), devices)
        return pack_rows(plan, parts, own, devices, rows)

    def exchange_out(packed, kind):
        parts = exchanged(unpack_rows(plan, packed, own, devices, span), devices)
        return place_slots(plan, lengths, parts, own, devices, kind)

    x1 = exchange_in(tokens)
    packed_cotangent = exchange_in(cotangent)
    small = jnp.concatenate(
        [
            query_bias, value_bias, out_bias, attention_gain,
            attention_shift, outer_bias, final_gain, final_shift,
        ]
    ).reshape(8, features).astype(F32)
    inner_row = inner_bias.reshape(1, hidden_features).astype(F32)
    wide = 3 * features
    tiles = Rows(plan, own, rows, tile, own * slot_len // tile)
    attention = Attention(plan, own, slot_len, rows, features)
    qkv_weights = (query_weight, key_weight, value_weight)
    feed_weights = (out_weight, inner_weight, outer_weight)

    (qkv1,) = tiles.call(
        partial(qkv_kernel, own, tile), [x1], (*qkv_weights, small), [], [(wide, BF)], [], [], []
    )
    context1, exact1, inverse_sum1, peak1 = attention.forward(qkv1)
    normed1, normed2, inverses, act, slope, qkv2 = tiles.call(
        partial(post_kernel, own, tile, width),
        [context1, x1],
        (*feed_weights, *qkv_weights, small, inner_row),
        [],
        [
            (features, F32), (features, F32), (128, F32),
            (hidden_features, BF), (hidden_features, BF), (wide, BF),
        ],
        [],
        [],
        [],
    )
    context2, exact2, inverse_sum2, peak2 = attention.forward(qkv2)

    share_rows = (2 * hidden_features + features) // devices
    feed_grads = ((devices, share_rows, features), BF)
    sums_out = [((8, features), F32), ((1, hidden_features), F32)]
    feed_scratch = [
        pltpu.VMEM((features, hidden_features), F32),
        pltpu.VMEM((hidden_features, features), F32),
        pltpu.VMEM((features, features), F32),
        pltpu.VMEM((8, features), F32),
        pltpu.VMEM((1, hidden_features), F32),
        pltpu.VMEM((2, devices, features // devices, features), BF),
        pltpu.SemaphoreType.DMA((2,)),
    ]
    stage_in = [
        pltpu.VMEM((2, devices, features // devices, features), BF),
        pltpu.SemaphoreType.DMA((2,)),
    ]
    packed_output, dcontext2, dpre2, feed_grads2, sums2, inner_sum2 = tiles.call(
        partial(second_kernel, own, tile, width),
        [context2, normed2, packed_cotangent],
        (*feed_weights, small, inner_row),
        [],
        [(features, BF), (features, BF), (features, F32)],
        sums_out,
        [feed_grads],
        [pltpu.VMEM((tile, hidden_features), BF)] * 2 + feed_scratch,
    )
    layer_output = exchange_out(packed_output, BF)
    dq2, dk2, dv2 = attention.backward(qkv2, exact2, inverse_sum2, peak2, dcontext2)

    qkv_grads = ((devices, 3 * features // devices, features), BF)
    qkv_scratch = [
        pltpu.VMEM((3, features, features), F32),
        pltpu.VMEM((8, features), F32),
        pltpu.VMEM((2, devices, features // devices, features), BF),
        pltpu.SemaphoreType.DMA((2,)),
    ]
    dx2, qkv_grads2, qkv_sums2 = tiles.call(
        partial(qkv_back_kernel, own, tile, True),
        [dq2, dk2, dv2, normed2, dpre2],
        (*qkv_weights, small),
        [],
        [(features, F32)],
        [((8, features), F32)],
        [qkv_grads],
        qkv_scratch,
    )
    dcontext1, dpre1, grads_feed, sums, inner_sum = tiles.call(
        partial(first_kernel, own, tile, width),
        [context1, normed1, normed2, inverses, act, slope, dx2],
        (*feed_weights, small),
        [(feed_grads2, True), (sums2, False), (inner_sum2, False)],
        [(features, BF), (features, F32)],
        sums_out,
        [feed_grads],
        feed_scratch + stage_in,
    )
    total_feed = summed_shares(grads_feed)
    dq1, dk1, dv1 = attention.backward(qkv1, exact1, inverse_sum1, peak1, dcontext1)
    packed_grad, grads_qkv, qkv_sums = tiles.call(
        partial(qkv_back_kernel, own, tile, False),
        [dq1, dk1, dv1, x1, dpre1],
        (*qkv_weights, small),
        [(qkv_grads2, True), (qkv_sums2, False)],
        [(features, BF)],
        [((8, features), F32)],
        [qkv_grads],
        qkv_scratch + stage_in,
    )
    input_grad = exchange_out(packed_grad, F32)

    each = features // devices
    vectors = jnp.concatenate([qkv_sums[:2], sums[1:7]], 0).reshape(8, devices, each)
    vectors = vectors.transpose(1, 0, 2).reshape(devices, 8 * each)
    vectors = jnp.concatenate([vectors, inner_sum.reshape(devices, hidden_features // devices)], 1)
    filled = vectors.shape[1]
    lines = -(-filled // features)
    vectors = jnp.pad(vectors, ((0, 0), (0, lines * features - filled)))
    vectors = vectors.reshape(devices, lines, features).astype(BF)
    total_qkv = summed_shares(jnp.concatenate([grads_qkv, vectors], 1)).astype(F32)
    total_feed = total_feed.astype(F32)
    vector = total_qkv[3 * each :].reshape(-1)
    query_b, value_b, out_b, gain_a, shift_a, outer_b, gain_f, shift_f = (
        vector[i * each : (i + 1) * each] for i in range(8)
    )
    inner_b = vector[8 * each : filled]
    inner = jnp.concatenate(
        [total_feed[i * each : (i + 1) * each] for i in range(hidden_features // features)], 1
    )
    after = hidden_features // devices
    outer = total_feed[after : 2 * after]
    return (
        layer_output,
        input_grad,
        total_qkv[:each],
        query_b,
        total_qkv[each : 2 * each],
        total_qkv[2 * each : 3 * each],
        value_b,
        total_feed[2 * after :],
        out_b,
        gain_a,
        shift_a,
        inner,
        inner_b,
        outer,
        outer_b,
        gain_f,
        shift_f,
    )


def solution(mesh):
    split = P("dp", "blk", None)
    in_specs = (split, split, P("dp")) + (P(),) * 15
    matrix, vector = P("blk", None), P("blk")
    out_specs = (
        split,
        split,
        matrix,
        vector,
        matrix,
        matrix,
        vector,
        matrix,
        vector,
        vector,
        vector,
        matrix,
        vector,
        matrix,
        vector,
        vector,
        vector,
    )
    return jax.shard_map(
        on_device, mesh=mesh, in_specs=in_specs, out_specs=out_specs, check_vma=False
    )
```

```python
from functools import partial
import math

import jax
import jax.numpy as jnp
from jax import lax
from jax.experimental import pallas as pl
from jax.experimental.pallas import tpu as pltpu
from jax.sharding import PartitionSpec as P

HEAD_DIM = 64
EPSILON = 1e-06
NEGATIVE = -1e30
LOG2E = math.log2(math.e)
LN2 = math.log(2.0)
SCORE_SCALE = HEAD_DIM ** (-0.5)
GELU_C = math.sqrt(2.0 / math.pi)
VMEM_LIMIT = 60 * 2**20
BF = jnp.bfloat16
F32 = jnp.float32
(P_QB, P_VB, P_OB, P_AG, P_AS, P_UB, P_FG, P_FS) = range(8)


def dot_nt(a, b):
    return lax.dot_general(a, b, (((1,), (1,)), ((), ())), preferred_element_type=F32)


def dot_nn(a, b):
    return lax.dot_general(a, b, (((1,), (0,)), ((), ())), preferred_element_type=F32)


def dot_tn(a, b):
    return lax.dot_general(a, b, (((0,), (0,)), ((), ())), preferred_element_type=F32)


def params_of(**extra):
    return pltpu.CompilerParams(vmem_limit_bytes=VMEM_LIMIT, **extra)


def estimate(multiply_adds):
    return pl.CostEstimate(flops=2 * int(multiply_adds), bytes_accessed=1024, transcendentals=0)


class Deal:
    def __init__(self, slots, span):
        self.span = span
        self.blocks = lax.axis_size("blk")
        self.groups = 2 if lax.axis_size("dp") % 2 == 0 else 1
        self.devices = self.groups * self.blocks
        self.turns = -(-slots // self.devices)
        self.own = self.groups * self.turns
        self.total = self.devices * self.turns

    def exchanged(self, parts):
        total, span, features = parts.shape
        parts = parts.reshape(self.devices, self.turns * span, features)
        if self.groups == 1:
            parts = lax.all_to_all(parts, "blk", 0, 0)
        else:
            everyone = lax.axis_size("dp") * self.blocks
            together = [
                list(range(i, i + self.devices)) for i in range(0, everyone, self.devices)
            ]
            parts = lax.all_to_all(parts, ("dp", "blk"), 0, 0, axis_index_groups=together)
        return parts.reshape(total, span, features)


def plan_kernel(deal, tile, len_ref, me_ref, out_ref):
    own, devices, turns = deal.own, deal.devices, deal.turns
    slots = len_ref.shape[0] // deal.groups
    side, place = me_ref[0], me_ref[1]
    me = side * deal.blocks + place
    order = 2 * own + 2
    for r in range(deal.total):
        out_ref[order + r] = -1
    for j in range(own):
        out_ref[2 * j + 1] = 0
    for g in range(deal.groups):
        group = side if g == 0 else 1 - side
        for i in range(slots):
            n = len_ref[g * slots + i]
            rank = jnp.int32(0)
            for j in range(slots):
                if j != i:
                    m = len_ref[g * slots + j]
                    before = (m >= n) if j < i else (m > n)
                    rank = rank + before.astype(jnp.int32)
            turn = lax.div(rank, devices)
            column = lax.rem(rank, devices)
            rising = lax.rem(turn + group, 2) == 1
            owner = jnp.where(rising, devices - 1 - column, column)
            if g == 0:
                out_ref[order + owner * turns + turn] = i

            @pl.when(owner == me)
            def _():
                out_ref[2 * (group * turns + turn) + 1] = n

    start = jnp.int32(0)
    for j in range(own):
        out_ref[2 * j] = start
        start = start + lax.div(out_ref[2 * j + 1] + 127, 128) * 128
    out_ref[2 * own] = jnp.maximum(lax.div(start + tile - 1, tile), 1)
    out_ref[2 * own + 1] = place


def make_plan(lengths, deal, tile):
    place = lax.axis_index("blk")
    side = lax.rem(lax.axis_index("dp"), deal.groups)
    if deal.groups == 2:
        lengths = jnp.concatenate([lengths, swapped(lengths, "dp", 1)])
    return pl.pallas_call(
        partial(plan_kernel, deal, tile),
        in_specs=[pl.BlockSpec(memory_space=pltpu.SMEM)] * 2,
        out_specs=pl.BlockSpec(memory_space=pltpu.SMEM),
        out_shape=jax.ShapeDtypeStruct((2 * deal.own + 2 + deal.total,), jnp.int32),
    )(lengths, jnp.stack([side, place]).astype(jnp.int32))


def gather_kernel(count, first, plan, source, out, held, sems_in, sems_out):
    incoming = [
        pltpu.make_async_copy(
            source.at[jnp.maximum(plan[first + i], 0)], held.at[i], sems_in.at[i]
        )
        for i in range(count)
    ]
    outgoing = [
        pltpu.make_async_copy(held.at[i], out.at[i], sems_out.at[i]) for i in range(count)
    ]
    for copy in incoming:
        copy.start()
    for i in range(count):
        incoming[i].wait()
        outgoing[i].start()
    for copy in outgoing:
        copy.wait()


def gather_slots(plan, source, deal):
    slots, span, features = source.shape
    count = deal.total
    return pl.pallas_call(
        partial(gather_kernel, count, 2 * deal.own + 2),
        grid_spec=pltpu.PrefetchScalarGridSpec(
            num_scalar_prefetch=1,
            grid=(1,),
            in_specs=[pl.BlockSpec(memory_space=pl.ANY)],
            out_specs=pl.BlockSpec(memory_space=pl.ANY),
            scratch_shapes=[
                pltpu.VMEM((count, span, features), source.dtype),
                pltpu.SemaphoreType.DMA((count,)),
                pltpu.SemaphoreType.DMA((count,)),
            ],
        ),
        out_shape=jax.ShapeDtypeStruct((count, span, features), source.dtype),
        compiler_params=params_of(),
    )(plan, source)


class Chunks:
    def __init__(self, deal, tile):
        self.own, self.span, self.tile, self.deal = deal.own, deal.span, tile, deal
        self.chunk = min(128, self.span)
        self.count = tile // self.chunk

    def place(self, plan, step, h):
        row = step * self.tile + h * self.chunk
        base, start, length = jnp.int32(0), plan[0], plan[1]
        turns = self.deal.turns
        for j in range(1, self.own):
            later = row >= plan[2 * j]
            base = jnp.where(later, j // turns * self.deal.blocks * turns + j % turns, base)
            start = jnp.where(later, plan[2 * j], start)
            length = jnp.where(later, plan[2 * j + 1], length)
        at = row - start
        valid = at < length
        at = jnp.where(valid, at, 0)
        block = base + lax.div(at, self.span) * turns
        return block, lax.div(lax.rem(at, self.span), self.chunk), valid

    def specs(self, features):
        def index(h):
            def at(i, plan):
                step = jnp.minimum(i, plan[2 * self.own] - 1)
                block, piece, _ = self.place(plan, step, h)
                return block, piece, 0

            return at

        return [
            pl.BlockSpec((1, self.chunk, features), index(h)) for h in range(self.count)
        ]

    def send(self, plan, step, held, out, sems, action):
        for h in range(self.count):
            block, piece, valid = self.place(plan, step, h)

            @pl.when(valid)
            def _():
                at = pl.multiple_of(piece * self.chunk, self.chunk)
                copy = pltpu.make_async_copy(
                    held.at[pl.ds(h * self.chunk, self.chunk)],
                    out.at[block, pl.ds(at, self.chunk)],
                    sems.at[h],
                )
                action(copy)

    def put(self, plan, step, value, held, out, sems):
        @pl.when(step > 0)
        def _():
            self.send(plan, step - 1, held, out, sems, lambda copy: copy.wait())

        held[...] = value
        self.send(plan, step, held, out, sems, lambda copy: copy.start())

        @pl.when(step == plan[2 * self.own] - 1)
        def _():
            self.send(plan, step, held, out, sems, lambda copy: copy.wait())

    def scratch(self, features, kind):
        return [pltpu.VMEM((self.tile, features), kind), pltpu.SemaphoreType.DMA((self.count,))]


def place_kernel(own, plan, lengths, parts, out):
    total, span, features = parts.shape
    order = 2 * own + 2
    row = lax.broadcasted_iota(jnp.int32, (span, features), 0) + plan[2 * own + 1] * span
    for i in range(total):
        slot = plan[order + i]

        @pl.when(slot >= 0)
        def _():
            keep = row < lengths[slot]
            out[slot] = jnp.where(keep, parts[i].astype(F32), 0.0).astype(out.dtype)


def place_slots(plan, lengths, parts, deal, out_type):
    total, span, features = parts.shape
    slots = lengths.shape[0]
    return pl.pallas_call(
        partial(place_kernel, deal.own),
        grid_spec=pltpu.PrefetchScalarGridSpec(
            num_scalar_prefetch=2,
            grid=(1,),
            in_specs=[pl.BlockSpec((total, span, features), lambda i, *_: (0, 0, 0))],
            out_specs=pl.BlockSpec((slots, span, features), lambda i, *_: (0, 0, 0)),
        ),
        out_shape=jax.ShapeDtypeStruct((slots, span, features), out_type),
        compiler_params=params_of(),
    )(plan, lengths, parts)


def rows_valid(plan, own, tile, shape):
    row = lax.broadcasted_iota(jnp.int32, shape, 0) + pl.program_id(0) * tile
    valid = None
    for j in range(own):
        start = plan[2 * j]
        inside = (row >= start) & (row < start + plan[2 * j + 1])
        valid = inside if valid is None else valid | inside
    return valid


def normed_rows(values):
    center = values - jnp.mean(values, axis=-1, keepdims=True)
    inverse = lax.rsqrt(jnp.mean(center * center, axis=-1, keepdims=True) + EPSILON)
    return center * inverse, inverse


def norm_back(grad_out, normed, inverse, gain):
    scaled = grad_out * gain
    mean_part = jnp.mean(scaled, axis=-1, keepdims=True)
    along_part = jnp.mean(scaled * normed, axis=-1, keepdims=True)
    return inverse * (scaled - mean_part - normed * along_part)


def column_sum(values):
    return jnp.sum(values, axis=0, keepdims=True)


def project_qkv(low, wq, wk, wv, small, out):
    features = low.shape[1]
    out[:, :features] = (
        (dot_nn(low, wq[...]) + small[P_QB : P_QB + 1]) * (SCORE_SCALE * LOG2E)
    ).astype(BF)
    out[:, features : 2 * features] = dot_nn(low, wk[...]).astype(BF)
    out[:, 2 * features :] = (dot_nn(low, wv[...]) + small[P_VB : P_VB + 1]).astype(BF)


SLOTS = 3


class Flush:
    def __init__(self, plan, own, devices, results, stage, sems, earlier, stage_in, sems_in):
        self.last = pl.program_id(0) == plan[2 * own] - 1
        self.core = lax.rem(plan[2 * own + 1], 2)
        self.devices, self.results, self.stage, self.sems = devices, results, stage, sems
        self.earlier, self.stage_in, self.sems_in = earlier, stage_in, sems_in
        self.pieces = []
        self.done = 0

    def plan(self, *pieces):
        self.pieces = pieces
        if self.earlier is not None:

            @pl.when(self.last)
            def _():
                for i in range(min(SLOTS, len(pieces))):
                    self.each_in(i, lambda copy: copy.start())

    def each(self, i, arrays, held, sems, outward, action):
        slot = i % SLOTS
        for same in (0, 1):

            @pl.when(self.core == same)
            def _():
                for n, (row, rows, device, at) in enumerate(self.pieces[i]):
                    far = arrays[int(device % 2 != same)].at[device // 2, pl.ds(at, rows)]
                    near = held.at[slot, pl.ds(row, rows)]
                    source, target = (near, far) if outward else (far, near)
                    action(pltpu.make_async_copy(source, target, sems.at[slot, n]))

    def each_in(self, i, action):
        self.each(i, self.earlier, self.stage_in, self.sems_in, False, action)

    def each_out(self, i, action):
        self.each(i, self.results, self.stage, self.sems, True, action)

    def finish(self, loads):
        @pl.when(self.last)
        def _():
            for i, load in enumerate(loads):
                if i >= SLOTS:
                    self.each_out(i - SLOTS, lambda copy: copy.wait())
                value = load()
                if self.earlier is not None:
                    self.each_in(i, lambda copy: copy.wait())
                    value = value + self.stage_in[i % SLOTS].astype(F32)
                self.stage[i % SLOTS] = value.astype(BF)
                self.each_out(i, lambda copy: copy.start())
                if self.earlier is not None and i + SLOTS < len(loads):
                    self.each_in(i + SLOTS, lambda copy: copy.start())
            for i in range(max(0, len(loads) - SLOTS), len(loads)):
                self.each_out(i, lambda copy: copy.wait())


def share_piece(features, devices, at):
    each = features // devices
    return [(b * each, each, b, at) for b in range(devices)]


def feed_layout(features, hidden_features, devices):
    each, share = features // devices, hidden_features // devices
    pieces = []
    for n, c in enumerate(range(0, hidden_features, features)):
        unit = min(features, share)
        pieces.append(
            [
                (row, unit, (c + row) // share, share + (c + row) % share)
                for row in range(0, features, unit)
            ]
        )
        pieces.append(share_piece(features, devices, n * each))
    pieces.append(share_piece(features, devices, 2 * share))
    return pieces


def qkv_kernel(own, tile, chunks, plan, *refs):
    refs = list(refs)
    parts, refs = refs[: chunks.count], refs[chunks.count :]
    wq, wk, wv, small, x_out, out = refs
    x = jnp.concatenate([part[0] for part in parts], 0)
    x = jnp.where(rows_valid(plan, own, tile, x.shape), x, 0)
    x_out[...] = x
    project_qkv(x, wq, wk, wv, small, out)


def project_qkv(low, wq, wk, wv, small, out):
    features = low.shape[1]
    out[:, :features] = (
        (dot_nn(low, wq[...]) + small[P_QB : P_QB + 1]) * (SCORE_SCALE * LOG2E)
    ).astype(BF)
    out[:, features : 2 * features] = dot_nn(low, wk[...]).astype(BF)
    out[:, 2 * features :] = (dot_nn(low, wv[...]) + small[P_VB : P_VB + 1]).astype(BF)


def gelu_parts(u):
    square = u * u
    t = jnp.tanh(u * (GELU_C + (GELU_C * 0.044715) * square))
    half = 0.5 + 0.5 * t
    slope = half + (0.5 * u) * (1.0 - t * t) * (GELU_C + (3 * GELU_C * 0.044715) * square)
    return u * half, slope


def feed_forward(context, x, wo, wi, wu, small, inner_bias, act, slope, width):
    pre = x + (dot_nn(context, wo[...]) + small[P_OB : P_OB + 1])
    normed1, inverse1 = normed_rows(pre)
    middle = normed1 * small[P_AG : P_AG + 1] + small[P_AS : P_AS + 1]
    low = middle.astype(BF)
    feed = None
    for c in range(0, act.shape[1], width):
        cols = slice(c, c + width)
        hidden = dot_nn(low, wi[:, cols]) + inner_bias[:, cols]
        activated, grad = gelu_parts(hidden)
        activated = activated.astype(BF)
        act[:, cols] = activated
        slope[:, cols] = grad.astype(BF)
        part = dot_nn(activated, wu[cols, :])
        feed = part if feed is None else feed + part
    normed2, inverse2 = normed_rows(middle + (feed + small[P_UB : P_UB + 1]))
    return normed1, inverse1, low, normed2, inverse2


def post_kernel(
    own, tile, width, plan, context, x, wo, wi, wu, wq, wk, wv, small, inner_bias,
    normed1_out, normed2_out, inverse_out, act_out, slope_out, qkv_out,
):
    valid = rows_valid(plan, own, tile, x.shape)
    ctx = jnp.where(valid, context[...], 0)
    normed1, inverse1, _, normed2, inverse2 = feed_forward(
        ctx, x[...].astype(F32), wo, wi, wu, small, inner_bias, act_out, slope_out, width
    )
    normed1_out[...] = normed1
    normed2_out[...] = normed2
    lane = lax.broadcasted_iota(jnp.int32, inverse_out.shape, 1)
    inverse_out[...] = jnp.where(lane < 64, inverse1, inverse2)
    low = (normed2 * small[P_FG : P_FG + 1] + small[P_FS : P_FS + 1]).astype(BF)
    project_qkv(low, wq, wk, wv, small, qkv_out)


def feed_back(
    grad, ctx, low, normed1, inverse1, normed2, inverse2, act, slope, wo, wi, wu, small,
    width, acc_inner, acc_outer, acc_out, sums, inner_sum, flush,
):
    flush.plan(*feed_layout(low.shape[1], act.shape[1], flush.devices))
    sums[5:6] += column_sum(grad * normed2)
    sums[6:7] += column_sum(grad)
    dsum = norm_back(grad, normed2, inverse2, small[P_FG : P_FG + 1])
    dfeed = dsum.astype(BF)
    sums[4:5] += column_sum(dfeed.astype(F32))
    dmiddle = dsum
    for c in range(0, act.shape[1], width):
        cols = slice(c, c + width)
        dactive = dot_nt(dfeed, wu[cols, :])
        acc_outer[cols, :] += dot_tn(act[:, cols], dfeed)
        dhidden = (dactive * slope[:, cols].astype(F32)).astype(BF)
        inner_sum[:, cols] += column_sum(dhidden.astype(F32))
        acc_inner[:, cols] += dot_tn(low, dhidden)
        dmiddle = dmiddle + dot_nt(dhidden, wi[:, cols])
    sums[2:3] += column_sum(dmiddle * normed1)
    sums[3:4] += column_sum(dmiddle)
    dpre = norm_back(dmiddle, normed1, inverse1, small[P_AG : P_AG + 1])
    dbranch = dpre.astype(BF)
    sums[1:2] += column_sum(dbranch.astype(F32))
    acc_out[...] += dot_tn(ctx, dbranch)
    dctx = dot_nt(dbranch, wo[...]).astype(BF)
    return dpre, dctx


def feed_loads(acc_inner, acc_outer, acc_out):
    features = acc_inner.shape[0]
    loads = []
    for c in range(0, acc_inner.shape[1], features):
        cols = slice(c, c + features)
        loads.append(lambda cols=cols: acc_outer[cols, :])
        loads.append(lambda cols=cols: acc_inner[:, cols])
    return [*loads, lambda: acc_out[...]]


def second_kernel(own, tile, chunks, devices, width, plan, context, normed_in, *refs):
    refs = list(refs)
    parts, refs = refs[: chunks.count], refs[chunks.count :]
    wo, wi, wu, small, inner_bias = refs[:5]
    dctx_out, dpre_out, layer_out, keep_out, send_out, sums_out, inner_sum_out = refs[5:12]
    act, slope, held, held_sems = refs[12:16]
    acc_inner, acc_outer, acc_out, sums, inner_sum, stage, sems = refs[16:]
    step = pl.program_id(0)

    @pl.when(step == 0)
    def _():
        for ref in (acc_inner, acc_outer, acc_out, sums, inner_sum):
            ref[...] = jnp.zeros_like(ref)

    valid = rows_valid(plan, own, tile, context.shape)
    ctx = jnp.where(valid, context[...], 0)
    x = normed_in[...] * small[P_FG : P_FG + 1] + small[P_FS : P_FS + 1]
    normed1, inverse1, low, normed2, inverse2 = feed_forward(
        ctx, x, wo, wi, wu, small, inner_bias, act, slope, width
    )
    result = (normed2 * small[P_FG : P_FG + 1] + small[P_FS : P_FS + 1]).astype(BF)
    chunks.put(plan, step, result, held, layer_out, held_sems)
    cotangent = jnp.concatenate([part[0] for part in parts], 0)
    grad = jnp.where(valid, cotangent, 0).astype(F32)
    flush = Flush(plan, own, devices, (keep_out, send_out), stage, sems, None, None, None)
    dpre_out[...], dctx_out[...] = feed_back(
        grad, ctx, low, normed1, inverse1, normed2, inverse2, act, slope, wo, wi, wu, small,
        width, acc_inner, acc_outer, acc_out, sums, inner_sum, flush,
    )
    flush.finish(feed_loads(acc_inner, acc_outer, acc_out))
    sums_out[...] = sums[...]
    inner_sum_out[...] = inner_sum[...]


def first_kernel(
    own, tile, devices, width, plan, context, normed1_in, normed2_in, inverse_in, act, slope, grad,
    wo, wi, wu, small, keep_in, send_in, sums_in, inner_sum_in,
    dctx_out, dpre_out, keep_out, send_out, sums_out, inner_sum_out,
    acc_inner, acc_outer, acc_out, sums, inner_sum, stage, sems, stage_in, sems_in,
):
    step = pl.program_id(0)

    @pl.when(step == 0)
    def _():
        for ref in (acc_inner, acc_outer, acc_out):
            ref[...] = jnp.zeros_like(ref)
        sums[...] = sums_in[...]
        inner_sum[...] = inner_sum_in[...]

    valid = rows_valid(plan, own, tile, context.shape)
    ctx = jnp.where(valid, context[...], 0)
    normed1 = normed1_in[...]
    low = (normed1 * small[P_AG : P_AG + 1] + small[P_AS : P_AS + 1]).astype(BF)
    inverse = inverse_in[...]
    flush = Flush(
        plan, own, devices, (keep_out, send_out), stage, sems, (keep_in, send_in), stage_in, sems_in
    )
    dpre_out[...], dctx_out[...] = feed_back(
        grad[...], ctx, low, normed1, inverse[:, 0:1], normed2_in[...], inverse[:, 64:65],
        act, slope, wo, wi, wu, small, width, acc_inner, acc_outer, acc_out, sums, inner_sum, flush,
    )
    flush.finish(feed_loads(acc_inner, acc_outer, acc_out))
    sums_out[...] = sums[...]
    inner_sum_out[...] = inner_sum[...]


def qkv_back_kernel(own, tile, chunks, devices, groups, plan, *refs):
    refs = list(refs)
    dqkv, refs = refs[: 3 * groups], refs[3 * groups :]
    x, dpre, wq, wk, wv, small = refs[:6]
    if chunks is None:
        earlier, stage_in, sems_in = None, None, None
        dx_out, keep_out, send_out, sums_out = refs[6:10]
        rest = refs[10:]
    else:
        keep_in, send_in, sums_in = refs[6:9]
        earlier = (keep_in, send_in)
        dx_out, keep_out, send_out, sums_out = refs[9:13]
        rest = refs[13:]
    acc, sums, stage, sems = rest[:4]
    if chunks is not None:
        stage_in, sems_in, held, held_sems = rest[4:]
    step = pl.program_id(0)

    @pl.when(step == 0)
    def _():
        acc[...] = jnp.zeros_like(acc)
        sums[...] = jnp.zeros_like(sums) if chunks is None else sums_in[...]

    features = acc.shape[1]
    flush = Flush(plan, own, devices, (keep_out, send_out), stage, sems, earlier, stage_in, sems_in)
    flush.plan(*[share_piece(features, devices, i * (features // devices)) for i in range(3)])
    if chunks is None:
        low = (x[...] * small[P_FG : P_FG + 1] + small[P_FS : P_FS + 1]).astype(BF)
    else:
        low = x[...]
    dx = dpre[...]
    for i, (weight, row) in enumerate(((wq, 0), (wk, None), (wv, 1))):
        grad = jnp.concatenate([ref[...] for ref in dqkv[i * groups : (i + 1) * groups]], 1)
        grad = jnp.where(rows_valid(plan, own, tile, grad.shape), grad, 0)
        acc[i] += dot_tn(low, grad)
        if row is not None:
            sums[row : row + 1] += column_sum(grad.astype(F32))
        dx = dx + dot_nt(grad, weight[...])
    if chunks is None:
        dx_out[...] = dx
    else:
        chunks.put(plan, step, dx.astype(BF), held, dx_out, held_sems)
    flush.finish([lambda i=i: acc[i] for i in range(3)])
    sums_out[...] = sums[...]


class Rows:
    def __init__(self, plan, own, rows, tile, steps):
        self.plan, self.own, self.rows, self.tile, self.steps = plan, own, rows, tile, steps

    def tile_spec(self, width, past=False):
        tiles = 2 * self.own
        beyond = 0 if past else 1
        return pl.BlockSpec((self.tile, width), lambda i, plan: (jnp.minimum(i, plan[tiles] - beyond), 0))

    def call(
        self, kernel, work, tiled, weights, whole, far=(), tiled_out=(), far_out=(), whole_out=(), scratch=(), past=None
    ):
        def whole_spec(shape):
            return pl.BlockSpec(shape, lambda i, *_: (0,) * len(shape))

        operands, in_specs = [], []
        for item in tiled:
            if isinstance(item, tuple):
                operands += [item[0]] * len(item[1])
                in_specs += item[1]
            else:
                operands.append(item)
                in_specs.append(self.tile_spec(item.shape[1]))
        operands += [*weights, *whole, *[array for array, _ in far]]
        in_specs += [
            pl.BlockSpec(array.shape, lambda i, *_: (0, 0), pipeline_mode=pl.Buffered(1))
            for array in weights
        ]
        in_specs += [whole_spec(array.shape) for array in whole]
        in_specs += [
            pl.BlockSpec(memory_space=pl.ANY) if is_far else whole_spec(array.shape)
            for array, is_far in far
        ]
        out_specs = [self.tile_spec(width, i == past) for i, (width, _) in enumerate(tiled_out)]
        out_specs += [pl.BlockSpec(memory_space=pl.ANY) for _ in far_out]
        out_specs += [whole_spec(shape) for shape, _ in whole_out]
        out_shape = [jax.ShapeDtypeStruct((self.rows, width), kind) for width, kind in tiled_out]
        out_shape += [jax.ShapeDtypeStruct(shape, kind) for shape, kind in (*far_out, *whole_out)]

        def guarded(plan, *refs):
            @pl.when(pl.program_id(0) < plan[2 * self.own])
            def _():
                kernel(plan, *refs)

            if past is not None:
                ref = refs[len(operands) + past]

                @pl.when(pl.program_id(0) == plan[2 * self.own])
                def _():
                    ref[...] = jnp.zeros_like(ref)

        return pl.pallas_call(
            guarded,
            grid_spec=pltpu.PrefetchScalarGridSpec(
                num_scalar_prefetch=1,
                grid=(self.steps,),
                in_specs=in_specs,
                out_specs=out_specs,
                scratch_shapes=scratch,
            ),
            out_shape=out_shape,
            compiler_params=params_of(),
            cost_estimate=estimate(work * self.steps * self.tile // 2),
        )(self.plan, *operands)


def lane_mask(rows, first, end):
    lane = lax.broadcasted_iota(jnp.int32, (rows, 128), 1)
    return jnp.where((lane >= first) & (lane < end), 1.0, 0.0).astype(BF)


def halves(rows):
    return lane_mask(rows, 0, 64), lane_mask(rows, 64, 128)


def row_mask(rows, end, inside, outside):
    row = lax.broadcasted_iota(jnp.int32, (rows, 128), 0)
    return jnp.where(row < end, inside, outside).astype(BF)


def by_keys(plan, own, slot_len, step_keys, slot):
    for j in range(own):
        n = plan[2 * j + 1]
        for keys in range(step_keys, slot_len + 1, step_keys):

            @pl.when((n > keys - step_keys) & (n <= keys))
            def _():
                slot(j, keys)


def forward_attention(
    own, slot_len, tq, plan, q_ref, k_ref, v_ref, o_ref, of_ref, li_ref, m_ref, ka, va, bad_ref
):
    low_q = lax.broadcasted_iota(jnp.int32, (tq, 128), 1) < 64
    first_q, second_q = halves(tq)
    one0 = lane_mask(tq, 64, 65)
    one1 = lane_mask(tq, 0, 1)

    def slot(safe, j, keys):
        start = pl.multiple_of(plan[2 * j], 128)
        n = plan[2 * j + 1]
        first, second = halves(keys)
        bias = row_mask(keys, n, 0.0, NEGATIVE)
        k = k_ref[pl.ds(start, keys), :]
        v = v_ref[pl.ds(start, keys), :]
        ka[0, :keys] = k * first + bias * lane_mask(keys, 64, 65)
        ka[1, :keys] = k * second + bias * lane_mask(keys, 0, 1)
        va[0, :keys] = v * first + second
        va[1, :keys] = v * second + first

        def tile(i, c):
            r = pl.multiple_of(start + i * tq, 128)
            q = q_ref[pl.ds(r, tq), :]
            s0 = dot_nt(q * first_q + one0, ka[0, :keys])
            s1 = dot_nt(q * second_q + one1, ka[1, :keys])
            m = jnp.zeros((tq, 128), F32)
            if safe:
                m0 = jnp.max(s0, axis=1, keepdims=True)
                m1 = jnp.max(s1, axis=1, keepdims=True)
                s0, s1 = s0 - m0, s1 - m1
                m = jnp.where(low_q, m0, m1)
            o0 = dot_nn(jnp.exp2(s0).astype(BF), va[0, :keys])
            o1 = dot_nn(jnp.exp2(s1).astype(BF), va[1, :keys])
            total = jnp.where(low_q, pltpu.roll(o0, 64, 1), pltpu.roll(o1, 64, 1))
            li = 1.0 / total
            out = jnp.where(low_q, o0, o1) * li
            o_ref[pl.ds(r, tq), :] = out.astype(BF)
            of_ref[pl.ds(r, tq), :] = out
            li_ref[pl.ds(r, tq), :] = li
            m_ref[pl.ds(r, tq), :] = m
            if not safe:
                good = (total > 2.0**-60) & (total < 2.0**80)
                bad_ref[...] = jnp.where(good, bad_ref[...], 1.0)
            return c

        lax.fori_loop(0, lax.div(n + tq - 1, tq), tile, 0)

    bad_ref[...] = jnp.zeros_like(bad_ref)
    by_keys(plan, own, slot_len, tq, partial(slot, False))

    @pl.when(jnp.max(bad_ref[...]) > 0.0)
    def _():
        by_keys(plan, own, slot_len, tq, partial(slot, True))


def backward_attention(
    own, slot_len, tq, plan, q_ref, k_ref, v_ref, o_ref, do_ref, li_ref, m_ref,
    dq_ref, dk_ref, dv_ref, ka, km, va, dka, dva,
):
    lane_q = lax.broadcasted_iota(jnp.int32, (tq, 128), 1)
    low_q = lane_q < 64
    place = lax.rem(lane_q, 64)
    first_q, second_q = halves(tq)

    def slot(j, keys):
        start = pl.multiple_of(plan[2 * j], 128)
        n = plan[2 * j + 1]
        first, second = halves(keys)
        bias = row_mask(keys, n, 0.0, NEGATIVE)
        k = k_ref[pl.ds(start, keys), :]
        v = v_ref[pl.ds(start, keys), :]
        km[0, :keys] = k * first
        km[1, :keys] = k * second
        ka[0, :keys] = k * first + (bias * lane_mask(keys, 64, 65) + lane_mask(keys, 65, 68))
        ka[1, :keys] = k * second + (bias * lane_mask(keys, 0, 1) + lane_mask(keys, 1, 4))
        va[0, :keys] = v * first + lane_mask(keys, 64, 66)
        va[1, :keys] = v * second + lane_mask(keys, 0, 2)
        dka[:, :keys] = jnp.zeros((128, keys), F32)
        dva[:, :keys] = jnp.zeros((128, keys), F32)

        def tile(i, c):
            r = pl.multiple_of(start + i * tq, 128)
            real_q = lax.broadcasted_iota(jnp.int32, (tq, 128), 0) + i * tq < n
            q = q_ref[pl.ds(r, tq), :] * row_mask(tq, n - i * tq, 1.0, 0.0)
            li = jnp.where(real_q, li_ref[pl.ds(r, tq), :], 0.0)
            m = jnp.where(real_q, m_ref[pl.ds(r, tq), :], 0.0)
            do = (do_ref[pl.ds(r, tq), :].astype(F32) * li).astype(BF)
            product = do.astype(F32) * o_ref[pl.ds(r, tq), :]
            delta0 = -jnp.sum(jnp.where(low_q, product, 0.0), axis=1, keepdims=True)
            delta1 = -jnp.sum(jnp.where(low_q, 0.0, product), axis=1, keepdims=True)
            m_other = -pltpu.roll(m, 64, 1)
            m_high = m_other.astype(BF).astype(F32)
            m_mid = (m_other - m_high).astype(BF).astype(F32)
            m_last = m_other - m_high - m_mid
            beside_q = jnp.where(
                place == 0,
                1.0,
                jnp.where(
                    place == 1, m_high, jnp.where(place == 2, m_mid, jnp.where(place == 3, m_last, 0.0))
                ),
            ).astype(BF)
            delta = jnp.where(low_q, delta1, delta0)
            high = delta.astype(BF).astype(F32)
            beside_do = jnp.where(
                place == 0, high, jnp.where(place == 1, delta - high, 0.0)
            ).astype(BF)
            e0 = jnp.exp2(dot_nt(q * first_q + beside_q * second_q, ka[0, :keys]))
            e1 = jnp.exp2(dot_nt(q * second_q + beside_q * first_q, ka[1, :keys]))
            ds0 = (e0 * dot_nt(do * first_q + beside_do * second_q, va[0, :keys])).astype(BF)
            ds1 = (e1 * dot_nt(do * second_q + beside_do * first_q, va[1, :keys])).astype(BF)
            dq = dot_nn(ds0, km[0, :keys]) + dot_nn(ds1, km[1, :keys])
            dq_ref[pl.ds(r, tq), :] = (dq * SCORE_SCALE).astype(BF)
            q_t = q.T
            do_t = do.T
            dva[:64, :keys] += dot_nn(do_t[:64], e0.astype(BF))
            dva[64:, :keys] += dot_nn(do_t[64:], e1.astype(BF))
            dka[:64, :keys] += dot_nn(q_t[:64], ds0)
            dka[64:, :keys] += dot_nn(q_t[64:], ds1)
            return c

        lax.fori_loop(0, lax.div(n + tq - 1, tq), tile, 0)
        dk_ref[pl.ds(start, keys), :] = (dka[:, :keys].T * LN2).astype(BF)
        dv_ref[pl.ds(start, keys), :] = dva[:, :keys].T.astype(BF)

    by_keys(plan, own, slot_len, tq, slot)


class Attention:
    def __init__(self, plan, own, slot_len, rows, features):
        self.plan, self.own, self.slot_len = plan, own, slot_len
        self.rows, self.features = rows, features
        self.pairs = features // 128
        self.step = min(256, slot_len)

    def spec(self, shift=0):
        return pl.BlockSpec((self.rows, 128), lambda p, *_: (0, p + shift))

    def call(self, kernel, pairs, in_specs, kinds, scratch, work, *args):
        return pl.pallas_call(
            partial(kernel, self.own, self.slot_len, self.step),
            grid_spec=pltpu.PrefetchScalarGridSpec(
                num_scalar_prefetch=1,
                grid=(pairs,),
                in_specs=in_specs,
                out_specs=[self.spec()] * len(kinds),
                scratch_shapes=scratch,
            ),
            out_shape=[jax.ShapeDtypeStruct((self.rows, pairs * 128), kind) for kind in kinds],
            compiler_params=params_of(),
            cost_estimate=estimate(work * pairs * self.own * self.slot_len**2 * 128),
        )(self.plan, *args)

    def qkv_specs(self, first=0):
        return [self.spec(first), self.spec(self.pairs + first), self.spec(2 * self.pairs + first)]

    def forward(self, qkv):
        scratch = [pltpu.VMEM((2, self.slot_len, 128), BF)] * 2
        scratch += [pltpu.VMEM((self.step, 128), F32)]
        return self.call(
            forward_attention, self.pairs, self.qkv_specs(), (BF, F32, F32, F32), scratch, 3, qkv, qkv, qkv
        )

    def backward(self, first, pairs, qkv, out, inverse, peak, grad):
        scratch = [pltpu.VMEM((2, self.slot_len, 128), BF)] * 3
        scratch += [pltpu.VMEM((128, self.slot_len), F32)] * 2
        return self.call(
            backward_attention,
            pairs,
            self.qkv_specs(first) + [self.spec(first)] * 4,
            (BF, BF, BF),
            scratch,
            6,
            qkv,
            qkv,
            qkv,
            out,
            grad,
            inverse,
            peak,
        )


def swapped(array, axis, distance):
    count = lax.axis_size(axis)
    return lax.ppermute(array, axis, [(i, i ^ distance) for i in range(count)])


def my_bit(axis, distance):
    return lax.rem(lax.div(lax.axis_index(axis), distance), 2)


def halved(array, axis, distance, dim=0):
    size = array.shape[dim] // 2
    mine = my_bit(axis, distance) * size
    theirs = size - mine
    received = swapped(lax.dynamic_slice_in_dim(array, theirs, size, dim), axis, distance)
    return lax.dynamic_slice_in_dim(array, mine, size, dim) + received


def doubled(arrays, axis, distance):
    low = my_bit(axis, distance) == 0
    received = swapped(jnp.concatenate(arrays, 0), axis, distance)
    result, at = [], 0
    for array in arrays:
        other = received[at : at + array.shape[0]]
        at += array.shape[0]
        first = jnp.where(low, array, other)
        result.append(jnp.concatenate([first, jnp.where(low, other, array)], 0))
    return result


def bits(count):
    distances = []
    while count > 1:
        count //= 2
        distances.append(count)
    return distances


class Sum:
    def __init__(self, kept, sent, extra=None):
        self.parts = (kept, sent)
        self.extra = extra
        across = lax.axis_size("dp")
        self.near = [distance for distance in bits(across) if distance == 1]
        self.far = sorted(distance for distance in bits(across) if distance > 1)
        self.blocks = [2 * distance for distance in bits(kept.shape[0])]

    def over_core(self):
        kept, sent = self.parts
        total = kept + swapped(sent, "blk", 1)
        if self.extra is not None:
            total = jnp.concatenate([total, self.extra], 1)
        self.parts = (total,)

    def over_chips(self):
        (total,) = self.parts
        half = total.shape[1] // 2
        one, two = total[:, :half], total[:, half:]
        for distance in self.blocks[:1]:
            one = halved(one, "blk", distance)
        for distance in self.near:
            two = halved(two, "dp", distance, 1)
        self.parts = one, two

    def over_both(self):
        one, two = self.parts
        for distance in self.blocks[1:]:
            one = halved(one, "blk", distance)
        one = one[0]
        for distance in self.near:
            one = halved(one, "dp", distance)
        for distance in self.blocks:
            two = halved(two, "blk", distance)
        self.cut = one.shape[0]
        self.parts = (jnp.concatenate([one, two[0]], 0),)

    def over_next(self):
        for distance in self.far[:1]:
            self.parts = (halved(self.parts[0], "dp", distance),)

    def over_rest(self):
        for distance in self.far[1:]:
            self.parts = (halved(self.parts[0], "dp", distance),)

    def back_from_rest(self):
        for distance in reversed(self.far[1:]):
            self.parts = tuple(doubled(self.parts, "dp", distance))

    def back_from_next(self):
        for distance in self.far[:1]:
            self.parts = tuple(doubled(self.parts, "dp", distance))

    def back(self):
        (both,) = self.parts
        parts = [both[: self.cut], both[self.cut :]]
        for distance in self.near:
            parts = doubled(parts, "dp", distance)
        return jnp.concatenate(parts, 0).astype(F32)


def tied(sums, others):
    parts, others = lax.optimization_barrier(([item.parts for item in sums], others))
    for item, part in zip(sums, parts):
        item.parts = tuple(part)
    return others


def on_device(
    tokens,
    cotangent,
    lengths,
    query_weight,
    query_bias,
    key_weight,
    value_weight,
    value_bias,
    out_weight,
    out_bias,
    attention_gain,
    attention_shift,
    inner_weight,
    inner_bias,
    outer_weight,
    outer_bias,
    final_gain,
    final_shift,
):
    devices = lax.axis_size("blk")
    slots, span, features = tokens.shape
    hidden_features = inner_weight.shape[1]
    slot_len = devices * span
    deal = Deal(slots, span)
    own = deal.own
    tile = min(256, slot_len)
    rows = own * slot_len + tile
    width = features
    plan = make_plan(lengths, deal, tile)

    chunks = Chunks(deal, tile)

    def exchange_in(array):
        return deal.exchanged(gather_slots(plan, array, deal)), chunks.specs(features)

    token_parts = exchange_in(tokens)
    cotangent_parts = exchange_in(cotangent)
    small = jnp.concatenate(
        [
            query_bias, value_bias, out_bias, attention_gain,
            attention_shift, outer_bias, final_gain, final_shift,
        ]
    ).reshape(8, features).astype(F32)
    inner_row = inner_bias.reshape(1, hidden_features).astype(F32)
    wide = 3 * features
    square = features * features
    tiles = Rows(plan, own, rows, tile, own * slot_len // tile)
    attention = Attention(plan, own, slot_len, rows, features)
    qkv_weights = (query_weight, key_weight, value_weight)
    feed_weights = (out_weight, inner_weight, outer_weight)
    feed_size = square + 2 * features * hidden_features
    send = ((deal.total, span, features), BF)

    x1, qkv1 = tiles.call(
        partial(qkv_kernel, own, tile, chunks),
        3 * square,
        [token_parts],
        qkv_weights,
        (small,),
        tiled_out=[(features, BF), (wide, BF)],
        past=1,
    )
    context1, exact1, inverse_sum1, peak1 = attention.forward(qkv1)
    normed1, normed2, inverses, act, slope, qkv2 = tiles.call(
        partial(post_kernel, own, tile, width),
        3 * square + feed_size,
        [context1, x1],
        (*feed_weights, *qkv_weights),
        (small, inner_row),
        tiled_out=[
            (features, F32), (features, F32), (128, F32),
            (hidden_features, BF), (hidden_features, BF), (wide, BF),
        ],
        past=5,
    )
    context2, exact2, inverse_sum2, peak2 = attention.forward(qkv2)

    share_rows = (2 * hidden_features + features) // devices
    feed_grads = [((devices // 2, share_rows, features), BF)] * 2
    sums_out = [((8, features), F32), ((1, hidden_features), F32)]
    stage = [pltpu.VMEM((SLOTS, features, features), BF), pltpu.SemaphoreType.DMA((SLOTS, devices))]
    feed_scratch = [
        pltpu.VMEM((features, hidden_features), F32),
        pltpu.VMEM((hidden_features, features), F32),
        pltpu.VMEM((features, features), F32),
        pltpu.VMEM((8, features), F32),
        pltpu.VMEM((1, hidden_features), F32),
        *stage,
    ]
    dcontext2, dpre2, output_parts, feed_keep2, feed_send2, sums2, inner_sum2 = tiles.call(
        partial(second_kernel, own, tile, chunks, devices, width),
        3 * feed_size,
        [context2, normed2, cotangent_parts],
        feed_weights,
        (small, inner_row),
        tiled_out=[(features, BF), (features, F32)],
        past=0,
        far_out=[send, *feed_grads],
        whole_out=sums_out,
        scratch=[
            *[pltpu.VMEM((tile, hidden_features), BF)] * 2,
            *chunks.scratch(features, BF),
            *feed_scratch,
        ],
    )
    output_parts = deal.exchanged(output_parts)
    dqkv2 = attention.backward(0, attention.pairs, qkv2, exact2, inverse_sum2, peak2, dcontext2)

    qkv_grads = [((devices // 2, 3 * features // devices, features), BF)] * 2
    qkv_scratch = [
        pltpu.VMEM((3, features, features), F32),
        pltpu.VMEM((8, features), F32),
        *stage,
    ]
    dx2, qkv_keep2, qkv_send2, qkv_sums2 = tiles.call(
        partial(qkv_back_kernel, own, tile, None, devices, 1),
        6 * square,
        [*dqkv2, normed2, dpre2],
        qkv_weights,
        (small,),
        tiled_out=[(features, F32)],
        far_out=qkv_grads,
        whole_out=[((8, features), F32)],
        scratch=qkv_scratch,
    )
    output_parts, dx2 = lax.optimization_barrier((output_parts, dx2))
    layer_output = place_slots(plan, lengths, output_parts, deal, BF)
    dcontext1, dpre1, feed_keep, feed_send, sums, inner_sum = tiles.call(
        partial(first_kernel, own, tile, devices, width),
        2 * feed_size,
        [context1, normed1, normed2, inverses, act, slope, dx2],
        feed_weights,
        (small,),
        far=[(feed_keep2, True), (feed_send2, True), (sums2, False), (inner_sum2, False)],
        tiled_out=[(features, BF), (features, F32)],
        past=0,
        far_out=feed_grads,
        whole_out=sums_out,
        scratch=[*feed_scratch, *stage],
    )
    feed_sum = Sum(feed_keep, feed_send)
    sizes = (1, 3, 2) if attention.pairs == 6 else (attention.pairs,)
    steps = (feed_sum.over_core, feed_sum.over_chips, feed_sum.over_both)
    dparts, first, grad1 = [], 0, dcontext1
    for size, step in zip(sizes, steps):
        part = attention.backward(first, size, qkv1, exact1, inverse_sum1, peak1, grad1)
        first += size
        step()
        part, grad1, dpre1 = tied([feed_sum], (part, grad1, dpre1))
        dparts.append(part)
    for step in steps[len(sizes) :]:
        step()
    dqkv1 = [part[i] for i in range(3) for part in dparts]
    groups = len(sizes)
    grad_parts, qkv_keep, qkv_send, qkv_sums = tiles.call(
        partial(qkv_back_kernel, own, tile, chunks, devices, groups),
        6 * square,
        [*dqkv1, x1, dpre1],
        qkv_weights,
        (small,),
        far=[(qkv_keep2, True), (qkv_send2, True), (qkv_sums2, False)],
        far_out=[send, *qkv_grads],
        whole_out=[((8, features), F32)],
        scratch=[*qkv_scratch, *stage, *chunks.scratch(features, BF)],
    )
    each = features // devices
    vectors = jnp.concatenate([qkv_sums[:2], sums[1:7]], 0).reshape(8, devices, each)
    vectors = vectors.transpose(1, 0, 2).reshape(devices, 8 * each)
    vectors = jnp.concatenate([vectors, inner_sum.reshape(devices, hidden_features // devices)], 1)
    filled = vectors.shape[1]
    lines = -(-filled // features)
    lines += -(3 * each + lines) % 64
    vectors = jnp.pad(vectors, ((0, 0), (0, lines * features - filled)))
    vectors = vectors.reshape(devices // 2, 2, lines, features).astype(BF)
    vectors = halved(vectors, "blk", 1, 1)[:, 0]
    feed_sum.over_next()
    qkv_keep, qkv_send, vectors, grad_parts = tied(
        [feed_sum], (qkv_keep, qkv_send, vectors, grad_parts)
    )
    qkv_sum = Sum(qkv_keep, qkv_send, vectors)
    both = [feed_sum, qkv_sum]
    feed_sum.over_rest()
    qkv_sum.over_core()
    qkv_sum.over_chips()
    grad_parts = deal.exchanged(tied(both, grad_parts))
    feed_sum.back_from_rest()
    qkv_sum.over_both()
    qkv_sum.over_next()
    tied(both, ())
    feed_sum.back_from_next()
    qkv_sum.over_rest()
    qkv_sum.back_from_rest()
    tied(both, ())
    qkv_sum.back_from_next()
    total_qkv = qkv_sum.back()
    total_feed = feed_sum.back()
    input_grad = place_slots(plan, lengths, grad_parts, deal, F32)
    vector = total_qkv[3 * each :].reshape(-1)
    query_b, value_b, out_b, gain_a, shift_a, outer_b, gain_f, shift_f = (
        vector[i * each : (i + 1) * each] for i in range(8)
    )
    inner_b = vector[8 * each : filled]
    inner = jnp.concatenate(
        [total_feed[i * each : (i + 1) * each] for i in range(hidden_features // features)], 1
    )
    after = hidden_features // devices
    outer = total_feed[after : 2 * after]
    return (
        layer_output,
        input_grad,
        total_qkv[:each],
        query_b,
        total_qkv[each : 2 * each],
        total_qkv[2 * each : 3 * each],
        value_b,
        total_feed[2 * after :],
        out_b,
        gain_a,
        shift_a,
        inner,
        inner_b,
        outer,
        outer_b,
        gain_f,
        shift_f,
    )


def solution(mesh):
    split = P("dp", "blk", None)
    in_specs = (split, split, P("dp")) + (P(),) * 15
    matrix, vector = P("blk", None), P("blk")
    out_specs = (
        split,
        split,
        matrix,
        vector,
        matrix,
        matrix,
        vector,
        matrix,
        vector,
        vector,
        vector,
        matrix,
        vector,
        matrix,
        vector,
        vector,
        vector,
    )
    return jax.shard_map(
        on_device, mesh=mesh, in_specs=in_specs, out_specs=out_specs, check_vma=False
    )
```

```python
from functools import partial
import math

import jax
import jax.numpy as jnp
from jax import lax
from jax.experimental import pallas as pl
from jax.experimental.pallas import tpu as pltpu
from jax.sharding import PartitionSpec as P

HEAD_DIM = 64
EPSILON = 1e-06
NEGATIVE = -1e30
LOG2E = math.log2(math.e)
LN2 = math.log(2.0)
SCORE_SCALE = HEAD_DIM ** (-0.5)
GELU_C = math.sqrt(2.0 / math.pi)
VMEM_LIMIT = 60 * 2**20
BF = jnp.bfloat16
F32 = jnp.float32
(P_QB, P_VB, P_OB, P_AG, P_AS, P_UB, P_FG, P_FS) = range(8)


def dot_nt(a, b):
    return lax.dot_general(a, b, (((1,), (1,)), ((), ())), preferred_element_type=F32)


def dot_nn(a, b):
    return lax.dot_general(a, b, (((1,), (0,)), ((), ())), preferred_element_type=F32)


def dot_tn(a, b):
    return lax.dot_general(a, b, (((0,), (0,)), ((), ())), preferred_element_type=F32)


def params_of(**extra):
    return pltpu.CompilerParams(vmem_limit_bytes=VMEM_LIMIT, **extra)


def estimate(multiply_adds):
    return pl.CostEstimate(flops=2 * int(multiply_adds), bytes_accessed=1024, transcendentals=0)


class Deal:
    def __init__(self, slots, span):
        self.span = span
        self.blocks = lax.axis_size("blk")
        self.groups = 2 if lax.axis_size("dp") % 2 == 0 else 1
        self.devices = self.groups * self.blocks
        self.turns = -(-slots // self.devices)
        self.own = self.groups * self.turns
        self.total = self.devices * self.turns

    def exchanged(self, parts):
        total, span, features = parts.shape
        parts = parts.reshape(self.devices, self.turns * span, features)
        if self.groups == 1:
            parts = lax.all_to_all(parts, "blk", 0, 0)
        else:
            everyone = lax.axis_size("dp") * self.blocks
            together = [
                list(range(i, i + self.devices)) for i in range(0, everyone, self.devices)
            ]
            parts = lax.all_to_all(parts, ("dp", "blk"), 0, 0, axis_index_groups=together)
        return parts.reshape(total, span, features)


def plan_kernel(deal, tile, len_ref, me_ref, out_ref):
    own, devices, turns = deal.own, deal.devices, deal.turns
    slots = len_ref.shape[0] // deal.groups
    side, place = me_ref[0], me_ref[1]
    me = side * deal.blocks + place
    order = 2 * own + 2
    for r in range(deal.total):
        out_ref[order + r] = -1
    for j in range(own):
        out_ref[2 * j + 1] = 0
    for g in range(deal.groups):
        group = side if g == 0 else 1 - side
        for i in range(slots):
            n = len_ref[g * slots + i]
            rank = jnp.int32(0)
            for j in range(slots):
                if j != i:
                    m = len_ref[g * slots + j]
                    before = (m >= n) if j < i else (m > n)
                    rank = rank + before.astype(jnp.int32)
            turn = lax.div(rank, devices)
            column = lax.rem(rank, devices)
            rising = lax.rem(turn + group, 2) == 1
            owner = jnp.where(rising, devices - 1 - column, column)
            if g == 0:
                out_ref[order + owner * turns + turn] = i

            @pl.when(owner == me)
            def _():
                out_ref[2 * (group * turns + turn) + 1] = n

    start = jnp.int32(0)
    for j in range(own):
        out_ref[2 * j] = start
        start = start + lax.div(out_ref[2 * j + 1] + 127, 128) * 128
    out_ref[2 * own] = jnp.maximum(lax.div(start + tile - 1, tile), 1)
    out_ref[2 * own + 1] = place


def make_plan(lengths, deal, tile):
    place = lax.axis_index("blk")
    side = lax.rem(lax.axis_index("dp"), deal.groups)
    if deal.groups == 2:
        lengths = jnp.concatenate([lengths, swapped(lengths, "dp", 1)])
    return pl.pallas_call(
        partial(plan_kernel, deal, tile),
        in_specs=[pl.BlockSpec(memory_space=pltpu.SMEM)] * 2,
        out_specs=pl.BlockSpec(memory_space=pltpu.SMEM),
        out_shape=jax.ShapeDtypeStruct((2 * deal.own + 2 + deal.total,), jnp.int32),
    )(lengths, jnp.stack([side, place]).astype(jnp.int32))


def gather_kernel(count, first, plan, source, out, held, sems_in, sems_out):
    incoming = [
        pltpu.make_async_copy(
            source.at[jnp.maximum(plan[first + i], 0)], held.at[i], sems_in.at[i]
        )
        for i in range(count)
    ]
    outgoing = [
        pltpu.make_async_copy(held.at[i], out.at[i], sems_out.at[i]) for i in range(count)
    ]
    for copy in incoming:
        copy.start()
    for i in range(count):
        incoming[i].wait()
        outgoing[i].start()
    for copy in outgoing:
        copy.wait()


def gather_slots(plan, source, deal):
    slots, span, features = source.shape
    count = deal.total
    return pl.pallas_call(
        partial(gather_kernel, count, 2 * deal.own + 2),
        grid_spec=pltpu.PrefetchScalarGridSpec(
            num_scalar_prefetch=1,
            grid=(1,),
            in_specs=[pl.BlockSpec(memory_space=pl.ANY)],
            out_specs=pl.BlockSpec(memory_space=pl.ANY),
            scratch_shapes=[
                pltpu.VMEM((count, span, features), source.dtype),
                pltpu.SemaphoreType.DMA((count,)),
                pltpu.SemaphoreType.DMA((count,)),
            ],
        ),
        out_shape=jax.ShapeDtypeStruct((count, span, features), source.dtype),
        compiler_params=params_of(),
    )(plan, source)


class Chunks:
    def __init__(self, deal, tile):
        self.own, self.span, self.tile, self.deal = deal.own, deal.span, tile, deal
        self.chunk = min(128, self.span)
        self.count = tile // self.chunk

    def place(self, plan, step, h):
        row = step * self.tile + h * self.chunk
        base, start, length = jnp.int32(0), plan[0], plan[1]
        turns = self.deal.turns
        for j in range(1, self.own):
            later = row >= plan[2 * j]
            base = jnp.where(later, j // turns * self.deal.blocks * turns + j % turns, base)
            start = jnp.where(later, plan[2 * j], start)
            length = jnp.where(later, plan[2 * j + 1], length)
        at = row - start
        valid = at < length
        at = jnp.where(valid, at, 0)
        block = base + lax.div(at, self.span) * turns
        return block, lax.div(lax.rem(at, self.span), self.chunk), valid

    def specs(self, features):
        def index(h):
            def at(i, plan):
                step = jnp.minimum(i, plan[2 * self.own] - 1)
                block, piece, _ = self.place(plan, step, h)
                return block, piece, 0

            return at

        return [
            pl.BlockSpec((1, self.chunk, features), index(h)) for h in range(self.count)
        ]

    def send(self, plan, step, held, out, sems, action):
        for h in range(self.count):
            block, piece, valid = self.place(plan, step, h)

            @pl.when(valid)
            def _():
                at = pl.multiple_of(piece * self.chunk, self.chunk)
                copy = pltpu.make_async_copy(
                    held.at[pl.ds(h * self.chunk, self.chunk)],
                    out.at[block, pl.ds(at, self.chunk)],
                    sems.at[h],
                )
                action(copy)

    def put(self, plan, step, value, held, out, sems):
        @pl.when(step > 0)
        def _():
            self.send(plan, step - 1, held, out, sems, lambda copy: copy.wait())

        held[...] = value
        self.send(plan, step, held, out, sems, lambda copy: copy.start())

        @pl.when(step == plan[2 * self.own] - 1)
        def _():
            self.send(plan, step, held, out, sems, lambda copy: copy.wait())

    def scratch(self, features, kind):
        return [pltpu.VMEM((self.tile, features), kind), pltpu.SemaphoreType.DMA((self.count,))]


def place_kernel(own, plan, lengths, parts, out):
    total, span, features = parts.shape
    order = 2 * own + 2
    row = lax.broadcasted_iota(jnp.int32, (span, features), 0) + plan[2 * own + 1] * span
    for i in range(total):
        slot = plan[order + i]

        @pl.when(slot >= 0)
        def _():
            keep = row < lengths[slot]
            out[slot] = jnp.where(keep, parts[i].astype(F32), 0.0).astype(out.dtype)


def place_slots(plan, lengths, parts, deal, out_type):
    total, span, features = parts.shape
    slots = lengths.shape[0]
    return pl.pallas_call(
        partial(place_kernel, deal.own),
        grid_spec=pltpu.PrefetchScalarGridSpec(
            num_scalar_prefetch=2,
            grid=(1,),
            in_specs=[pl.BlockSpec((total, span, features), lambda i, *_: (0, 0, 0))],
            out_specs=pl.BlockSpec((slots, span, features), lambda i, *_: (0, 0, 0)),
        ),
        out_shape=jax.ShapeDtypeStruct((slots, span, features), out_type),
        compiler_params=params_of(),
    )(plan, lengths, parts)


def rows_valid(plan, own, tile, shape):
    row = lax.broadcasted_iota(jnp.int32, shape, 0) + pl.program_id(0) * tile
    valid = None
    for j in range(own):
        start = plan[2 * j]
        inside = (row >= start) & (row < start + plan[2 * j + 1])
        valid = inside if valid is None else valid | inside
    return valid


def normed_rows(values):
    center = values - jnp.mean(values, axis=-1, keepdims=True)
    inverse = lax.rsqrt(jnp.mean(center * center, axis=-1, keepdims=True) + EPSILON)
    return center * inverse, inverse


def norm_back(grad_out, normed, inverse, gain):
    scaled = grad_out * gain
    mean_part = jnp.mean(scaled, axis=-1, keepdims=True)
    along_part = jnp.mean(scaled * normed, axis=-1, keepdims=True)
    return inverse * (scaled - mean_part - normed * along_part)


def column_sum(values):
    return jnp.sum(values, axis=0, keepdims=True)


def project_qkv(low, wq, wk, wv, small, out):
    features = low.shape[1]
    out[:, :features] = (
        (dot_nn(low, wq[...]) + small[P_QB : P_QB + 1]) * (SCORE_SCALE * LOG2E)
    ).astype(BF)
    out[:, features : 2 * features] = dot_nn(low, wk[...]).astype(BF)
    out[:, 2 * features :] = (dot_nn(low, wv[...]) + small[P_VB : P_VB + 1]).astype(BF)


SLOTS = 3


class Flush:
    def __init__(self, plan, own, devices, results, stage, sems, earlier, stage_in, sems_in):
        self.last = pl.program_id(0) == plan[2 * own] - 1
        self.core = lax.rem(plan[2 * own + 1], 2)
        self.devices, self.results, self.stage, self.sems = devices, results, stage, sems
        self.earlier, self.stage_in, self.sems_in = earlier, stage_in, sems_in
        self.pieces = []
        self.done = 0

    def plan(self, *pieces):
        self.pieces = pieces
        if self.earlier is not None:

            @pl.when(self.last)
            def _():
                for i in range(min(SLOTS, len(pieces))):
                    self.each_in(i, lambda copy: copy.start())

    def each(self, i, arrays, held, sems, outward, action):
        slot = i % SLOTS
        for same in (0, 1):

            @pl.when(self.core == same)
            def _():
                for n, (row, rows, device, at) in enumerate(self.pieces[i]):
                    far = arrays[int(device % 2 != same)].at[device // 2, pl.ds(at, rows)]
                    near = held.at[slot, pl.ds(row, rows)]
                    source, target = (near, far) if outward else (far, near)
                    action(pltpu.make_async_copy(source, target, sems.at[slot, n]))

    def each_in(self, i, action):
        self.each(i, self.earlier, self.stage_in, self.sems_in, False, action)

    def each_out(self, i, action):
        self.each(i, self.results, self.stage, self.sems, True, action)

    def finish(self, loads):
        @pl.when(self.last)
        def _():
            for i, load in enumerate(loads):
                if i >= SLOTS:
                    self.each_out(i - SLOTS, lambda copy: copy.wait())
                value = load()
                if self.earlier is not None:
                    self.each_in(i, lambda copy: copy.wait())
                    value = value + self.stage_in[i % SLOTS].astype(F32)
                self.stage[i % SLOTS] = value.astype(BF)
                self.each_out(i, lambda copy: copy.start())
                if self.earlier is not None and i + SLOTS < len(loads):
                    self.each_in(i + SLOTS, lambda copy: copy.start())
            for i in range(max(0, len(loads) - SLOTS), len(loads)):
                self.each_out(i, lambda copy: copy.wait())


def share_piece(features, devices, at):
    each = features // devices
    return [(b * each, each, b, at) for b in range(devices)]


def feed_layout(features, hidden_features, devices):
    each, share = features // devices, hidden_features // devices
    pieces = []
    for n, c in enumerate(range(0, hidden_features, features)):
        unit = min(features, share)
        pieces.append(
            [
                (row, unit, (c + row) // share, share + (c + row) % share)
                for row in range(0, features, unit)
            ]
        )
        pieces.append(share_piece(features, devices, n * each))
    pieces.append(share_piece(features, devices, 2 * share))
    return pieces


def qkv_kernel(own, tile, chunks, plan, *refs):
    refs = list(refs)
    parts, refs = refs[: chunks.count], refs[chunks.count :]
    wq, wk, wv, small, x_out, out = refs
    x = jnp.concatenate([part[0] for part in parts], 0)
    x = jnp.where(rows_valid(plan, own, tile, x.shape), x, 0)
    x_out[...] = x
    project_qkv(x, wq, wk, wv, small, out)


def project_qkv(low, wq, wk, wv, small, out):
    features = low.shape[1]
    out[:, :features] = (
        (dot_nn(low, wq[...]) + small[P_QB : P_QB + 1]) * (SCORE_SCALE * LOG2E)
    ).astype(BF)
    out[:, features : 2 * features] = dot_nn(low, wk[...]).astype(BF)
    out[:, 2 * features :] = (dot_nn(low, wv[...]) + small[P_VB : P_VB + 1]).astype(BF)


def gelu_parts(u):
    square = u * u
    t = jnp.tanh(u * (GELU_C + (GELU_C * 0.044715) * square))
    half = 0.5 + 0.5 * t
    slope = half + (0.5 * u) * (1.0 - t * t) * (GELU_C + (3 * GELU_C * 0.044715) * square)
    return u * half, slope


def feed_forward(context, x, wo, wi, wu, small, inner_bias, act, slope, width):
    pre = x + (dot_nn(context, wo[...]) + small[P_OB : P_OB + 1])
    normed1, inverse1 = normed_rows(pre)
    middle = normed1 * small[P_AG : P_AG + 1] + small[P_AS : P_AS + 1]
    low = middle.astype(BF)
    feed = None
    for c in range(0, act.shape[1], width):
        cols = slice(c, c + width)
        hidden = dot_nn(low, wi[:, cols]) + inner_bias[:, cols]
        activated, grad = gelu_parts(hidden)
        activated = activated.astype(BF)
        act[:, cols] = activated
        slope[:, cols] = grad.astype(BF)
        part = dot_nn(activated, wu[cols, :])
        feed = part if feed is None else feed + part
    normed2, inverse2 = normed_rows(middle + (feed + small[P_UB : P_UB + 1]))
    return normed1, inverse1, low, normed2, inverse2


def post_kernel(
    own, tile, width, plan, context, x, wo, wi, wu, wq, wk, wv, small, inner_bias,
    normed1_out, normed2_out, inverse_out, act_out, slope_out, qkv_out,
):
    valid = rows_valid(plan, own, tile, x.shape)
    ctx = jnp.where(valid, context[...], 0)
    normed1, inverse1, _, normed2, inverse2 = feed_forward(
        ctx, x[...].astype(F32), wo, wi, wu, small, inner_bias, act_out, slope_out, width
    )
    normed1_out[...] = normed1
    normed2_out[...] = normed2
    lane = lax.broadcasted_iota(jnp.int32, inverse_out.shape, 1)
    inverse_out[...] = jnp.where(lane < 64, inverse1, inverse2)
    low = (normed2 * small[P_FG : P_FG + 1] + small[P_FS : P_FS + 1]).astype(BF)
    project_qkv(low, wq, wk, wv, small, qkv_out)


def feed_back(
    grad, ctx, low, normed1, inverse1, normed2, inverse2, act, slope, wo, wi, wu, small,
    width, acc_inner, acc_outer, acc_out, sums, inner_sum, flush,
):
    flush.plan(*feed_layout(low.shape[1], act.shape[1], flush.devices))
    sums[5:6] += column_sum(grad * normed2)
    sums[6:7] += column_sum(grad)
    dsum = norm_back(grad, normed2, inverse2, small[P_FG : P_FG + 1])
    dfeed = dsum.astype(BF)
    sums[4:5] += column_sum(dfeed.astype(F32))
    dmiddle = dsum
    for c in range(0, act.shape[1], width):
        cols = slice(c, c + width)
        dactive = dot_nt(dfeed, wu[cols, :])
        acc_outer[cols, :] += dot_tn(act[:, cols], dfeed)
        dhidden = (dactive * slope[:, cols].astype(F32)).astype(BF)
        inner_sum[:, cols] += column_sum(dhidden.astype(F32))
        acc_inner[:, cols] += dot_tn(low, dhidden)
        dmiddle = dmiddle + dot_nt(dhidden, wi[:, cols])
    sums[2:3] += column_sum(dmiddle * normed1)
    sums[3:4] += column_sum(dmiddle)
    dpre = norm_back(dmiddle, normed1, inverse1, small[P_AG : P_AG + 1])
    dbranch = dpre.astype(BF)
    sums[1:2] += column_sum(dbranch.astype(F32))
    acc_out[...] += dot_tn(ctx, dbranch)
    dctx = dot_nt(dbranch, wo[...]).astype(BF)
    return dpre, dctx


def feed_loads(acc_inner, acc_outer, acc_out):
    features = acc_inner.shape[0]
    loads = []
    for c in range(0, acc_inner.shape[1], features):
        cols = slice(c, c + features)
        loads.append(lambda cols=cols: acc_outer[cols, :])
        loads.append(lambda cols=cols: acc_inner[:, cols])
    return [*loads, lambda: acc_out[...]]


def second_kernel(own, tile, chunks, devices, width, plan, context, normed_in, *refs):
    refs = list(refs)
    parts, refs = refs[: chunks.count], refs[chunks.count :]
    wo, wi, wu, small, inner_bias = refs[:5]
    dctx_out, dpre_out, layer_out, keep_out, send_out, sums_out, inner_sum_out = refs[5:12]
    act, slope, held, held_sems = refs[12:16]
    acc_inner, acc_outer, acc_out, sums, inner_sum, stage, sems = refs[16:]
    step = pl.program_id(0)

    @pl.when(step == 0)
    def _():
        for ref in (acc_inner, acc_outer, acc_out, sums, inner_sum):
            ref[...] = jnp.zeros_like(ref)

    valid = rows_valid(plan, own, tile, context.shape)
    ctx = jnp.where(valid, context[...], 0)
    x = normed_in[...] * small[P_FG : P_FG + 1] + small[P_FS : P_FS + 1]
    normed1, inverse1, low, normed2, inverse2 = feed_forward(
        ctx, x, wo, wi, wu, small, inner_bias, act, slope, width
    )
    result = (normed2 * small[P_FG : P_FG + 1] + small[P_FS : P_FS + 1]).astype(BF)
    chunks.put(plan, step, result, held, layer_out, held_sems)
    cotangent = jnp.concatenate([part[0] for part in parts], 0)
    grad = jnp.where(valid, cotangent, 0).astype(F32)
    flush = Flush(plan, own, devices, (keep_out, send_out), stage, sems, None, None, None)
    dpre_out[...], dctx_out[...] = feed_back(
        grad, ctx, low, normed1, inverse1, normed2, inverse2, act, slope, wo, wi, wu, small,
        width, acc_inner, acc_outer, acc_out, sums, inner_sum, flush,
    )
    flush.finish(feed_loads(acc_inner, acc_outer, acc_out))
    sums_out[...] = sums[...]
    inner_sum_out[...] = inner_sum[...]


def first_kernel(
    own, tile, devices, width, plan, context, normed1_in, normed2_in, inverse_in, act, slope, grad,
    wo, wi, wu, small, keep_in, send_in, sums_in, inner_sum_in,
    dctx_out, dpre_out, keep_out, send_out, sums_out, inner_sum_out,
    acc_inner, acc_outer, acc_out, sums, inner_sum, stage, sems, stage_in, sems_in,
):
    step = pl.program_id(0)

    @pl.when(step == 0)
    def _():
        for ref in (acc_inner, acc_outer, acc_out):
            ref[...] = jnp.zeros_like(ref)
        sums[...] = sums_in[...]
        inner_sum[...] = inner_sum_in[...]

    valid = rows_valid(plan, own, tile, context.shape)
    ctx = jnp.where(valid, context[...], 0)
    normed1 = normed1_in[...]
    low = (normed1 * small[P_AG : P_AG + 1] + small[P_AS : P_AS + 1]).astype(BF)
    inverse = inverse_in[...]
    flush = Flush(
        plan, own, devices, (keep_out, send_out), stage, sems, (keep_in, send_in), stage_in, sems_in
    )
    dpre_out[...], dctx_out[...] = feed_back(
        grad[...], ctx, low, normed1, inverse[:, 0:1], normed2_in[...], inverse[:, 64:65],
        act, slope, wo, wi, wu, small, width, acc_inner, acc_outer, acc_out, sums, inner_sum, flush,
    )
    flush.finish(feed_loads(acc_inner, acc_outer, acc_out))
    sums_out[...] = sums[...]
    inner_sum_out[...] = inner_sum[...]


def qkv_back_kernel(own, tile, chunks, devices, groups, plan, *refs):
    refs = list(refs)
    dqkv, refs = refs[: 3 * groups], refs[3 * groups :]
    x, dpre, wq, wk, wv, small = refs[:6]
    if chunks is None:
        earlier, stage_in, sems_in = None, None, None
        dx_out, keep_out, send_out, sums_out = refs[6:10]
        rest = refs[10:]
    else:
        keep_in, send_in, sums_in = refs[6:9]
        earlier = (keep_in, send_in)
        dx_out, keep_out, send_out, sums_out = refs[9:13]
        rest = refs[13:]
    acc, sums, stage, sems = rest[:4]
    if chunks is not None:
        stage_in, sems_in, held, held_sems = rest[4:]
    step = pl.program_id(0)

    @pl.when(step == 0)
    def _():
        acc[...] = jnp.zeros_like(acc)
        sums[...] = jnp.zeros_like(sums) if chunks is None else sums_in[...]

    features = acc.shape[1]
    flush = Flush(plan, own, devices, (keep_out, send_out), stage, sems, earlier, stage_in, sems_in)
    flush.plan(*[share_piece(features, devices, i * (features // devices)) for i in range(3)])
    if chunks is None:
        low = (x[...] * small[P_FG : P_FG + 1] + small[P_FS : P_FS + 1]).astype(BF)
    else:
        low = x[...]
    dx = dpre[...]
    for i, (weight, row) in enumerate(((wq, 0), (wk, None), (wv, 1))):
        grad = jnp.concatenate([ref[...] for ref in dqkv[i * groups : (i + 1) * groups]], 1)
        grad = jnp.where(rows_valid(plan, own, tile, grad.shape), grad, 0)
        acc[i] += dot_tn(low, grad)
        if row is not None:
            sums[row : row + 1] += column_sum(grad.astype(F32))
        dx = dx + dot_nt(grad, weight[...])
    if chunks is None:
        dx_out[...] = dx
    else:
        chunks.put(plan, step, dx.astype(BF), held, dx_out, held_sems)
    flush.finish([lambda i=i: acc[i] for i in range(3)])
    sums_out[...] = sums[...]


class Rows:
    def __init__(self, plan, own, rows, tile, steps):
        self.plan, self.own, self.rows, self.tile, self.steps = plan, own, rows, tile, steps

    def tile_spec(self, width, past=False):
        tiles = 2 * self.own
        beyond = 0 if past else 1
        return pl.BlockSpec((self.tile, width), lambda i, plan: (jnp.minimum(i, plan[tiles] - beyond), 0))

    def call(
        self, kernel, work, tiled, weights, whole, far=(), tiled_out=(), far_out=(), whole_out=(), scratch=(), past=None
    ):
        def whole_spec(shape):
            return pl.BlockSpec(shape, lambda i, *_: (0,) * len(shape))

        operands, in_specs = [], []
        for item in tiled:
            if isinstance(item, tuple):
                operands += [item[0]] * len(item[1])
                in_specs += item[1]
            else:
                operands.append(item)
                in_specs.append(self.tile_spec(item.shape[1]))
        operands += [*weights, *whole, *[array for array, _ in far]]
        in_specs += [
            pl.BlockSpec(array.shape, lambda i, *_: (0, 0), pipeline_mode=pl.Buffered(1))
            for array in weights
        ]
        in_specs += [whole_spec(array.shape) for array in whole]
        in_specs += [
            pl.BlockSpec(memory_space=pl.ANY) if is_far else whole_spec(array.shape)
            for array, is_far in far
        ]
        out_specs = [self.tile_spec(width, i == past) for i, (width, _) in enumerate(tiled_out)]
        out_specs += [pl.BlockSpec(memory_space=pl.ANY) for _ in far_out]
        out_specs += [whole_spec(shape) for shape, _ in whole_out]
        out_shape = [jax.ShapeDtypeStruct((self.rows, width), kind) for width, kind in tiled_out]
        out_shape += [jax.ShapeDtypeStruct(shape, kind) for shape, kind in (*far_out, *whole_out)]

        def guarded(plan, *refs):
            @pl.when(pl.program_id(0) < plan[2 * self.own])
            def _():
                kernel(plan, *refs)

            if past is not None:
                ref = refs[len(operands) + past]

                @pl.when(pl.program_id(0) == plan[2 * self.own])
                def _():
                    ref[...] = jnp.zeros_like(ref)

        return pl.pallas_call(
            guarded,
            grid_spec=pltpu.PrefetchScalarGridSpec(
                num_scalar_prefetch=1,
                grid=(self.steps,),
                in_specs=in_specs,
                out_specs=out_specs,
                scratch_shapes=scratch,
            ),
            out_shape=out_shape,
            compiler_params=params_of(),
            cost_estimate=estimate(work * self.steps * self.tile // 2),
        )(self.plan, *operands)


def lane_mask(rows, first, end):
    lane = lax.broadcasted_iota(jnp.int32, (rows, 128), 1)
    return jnp.where((lane >= first) & (lane < end), 1.0, 0.0).astype(BF)


def halves(rows):
    return lane_mask(rows, 0, 64), lane_mask(rows, 64, 128)


def row_mask(rows, end, inside, outside):
    row = lax.broadcasted_iota(jnp.int32, (rows, 128), 0)
    return jnp.where(row < end, inside, outside).astype(BF)


def by_keys(plan, own, slot_len, step_keys, slot):
    for j in range(own):
        n = plan[2 * j + 1]
        for keys in range(step_keys, slot_len + 1, step_keys):

            @pl.when((n > keys - step_keys) & (n <= keys))
            def _():
                slot(j, keys)


def forward_attention(
    own, slot_len, tq, plan, q_ref, k_ref, v_ref, o_ref, of_ref, li_ref, m_ref, ka, va, bad_ref
):
    low_q = lax.broadcasted_iota(jnp.int32, (tq, 128), 1) < 64
    first_q, second_q = halves(tq)
    one0 = lane_mask(tq, 64, 65)
    one1 = lane_mask(tq, 0, 1)

    def slot(safe, j, keys):
        start = pl.multiple_of(plan[2 * j], 128)
        n = plan[2 * j + 1]
        first, second = halves(keys)
        bias = row_mask(keys, n, 0.0, NEGATIVE)
        k = k_ref[pl.ds(start, keys), :]
        v = v_ref[pl.ds(start, keys), :]
        ka[0, :keys] = k * first + bias * lane_mask(keys, 64, 65)
        ka[1, :keys] = k * second + bias * lane_mask(keys, 0, 1)
        va[0, :keys] = v * first + second
        va[1, :keys] = v * second + first

        def tile(i, c):
            r = pl.multiple_of(start + i * tq, 128)
            q = q_ref[pl.ds(r, tq), :]
            s0 = dot_nt(q * first_q + one0, ka[0, :keys])
            s1 = dot_nt(q * second_q + one1, ka[1, :keys])
            m = jnp.zeros((tq, 128), F32)
            if safe:
                m0 = jnp.max(s0, axis=1, keepdims=True)
                m1 = jnp.max(s1, axis=1, keepdims=True)
                s0, s1 = s0 - m0, s1 - m1
                m = jnp.where(low_q, m0, m1)
            o0 = dot_nn(jnp.exp2(s0).astype(BF), va[0, :keys])
            o1 = dot_nn(jnp.exp2(s1).astype(BF), va[1, :keys])
            total = jnp.where(low_q, pltpu.roll(o0, 64, 1), pltpu.roll(o1, 64, 1))
            li = 1.0 / total
            out = jnp.where(low_q, o0, o1) * li
            o_ref[pl.ds(r, tq), :] = out.astype(BF)
            of_ref[pl.ds(r, tq), :] = out
            li_ref[pl.ds(r, tq), :] = li
            m_ref[pl.ds(r, tq), :] = m
            if not safe:
                good = (total > 2.0**-60) & (total < 2.0**80)
                bad_ref[...] = jnp.where(good, bad_ref[...], 1.0)
            return c

        lax.fori_loop(0, lax.div(n + tq - 1, tq), tile, 0)

    bad_ref[...] = jnp.zeros_like(bad_ref)
    by_keys(plan, own, slot_len, tq, partial(slot, False))

    @pl.when(jnp.max(bad_ref[...]) > 0.0)
    def _():
        by_keys(plan, own, slot_len, tq, partial(slot, True))


def backward_attention(
    own, slot_len, tq, plan, q_ref, k_ref, v_ref, o_ref, do_ref, li_ref, m_ref,
    dq_ref, dk_ref, dv_ref, ka, km, va, dka, dva,
):
    lane_q = lax.broadcasted_iota(jnp.int32, (tq, 128), 1)
    low_q = lane_q < 64
    place = lax.rem(lane_q, 64)
    first_q, second_q = halves(tq)

    def slot(j, keys):
        start = pl.multiple_of(plan[2 * j], 128)
        n = plan[2 * j + 1]
        first, second = halves(keys)
        bias = row_mask(keys, n, 0.0, NEGATIVE)
        k = k_ref[pl.ds(start, keys), :]
        v = v_ref[pl.ds(start, keys), :]
        km[0, :keys] = k * first
        km[1, :keys] = k * second
        ka[0, :keys] = k * first + (bias * lane_mask(keys, 64, 65) + lane_mask(keys, 65, 68))
        ka[1, :keys] = k * second + (bias * lane_mask(keys, 0, 1) + lane_mask(keys, 1, 4))
        va[0, :keys] = v * first + lane_mask(keys, 64, 66)
        va[1, :keys] = v * second + lane_mask(keys, 0, 2)
        dka[:, :keys] = jnp.zeros((128, keys), F32)
        dva[:, :keys] = jnp.zeros((128, keys), F32)

        def tile(i, c):
            r = pl.multiple_of(start + i * tq, 128)
            real_q = lax.broadcasted_iota(jnp.int32, (tq, 128), 0) + i * tq < n
            q = q_ref[pl.ds(r, tq), :] * row_mask(tq, n - i * tq, 1.0, 0.0)
            li = jnp.where(real_q, li_ref[pl.ds(r, tq), :], 0.0)
            m = jnp.where(real_q, m_ref[pl.ds(r, tq), :], 0.0)
            do = (do_ref[pl.ds(r, tq), :].astype(F32) * li).astype(BF)
            product = do.astype(F32) * o_ref[pl.ds(r, tq), :]
            delta0 = -jnp.sum(jnp.where(low_q, product, 0.0), axis=1, keepdims=True)
            delta1 = -jnp.sum(jnp.where(low_q, 0.0, product), axis=1, keepdims=True)
            m_other = -pltpu.roll(m, 64, 1)
            m_high = m_other.astype(BF).astype(F32)
            m_mid = (m_other - m_high).astype(BF).astype(F32)
            m_last = m_other - m_high - m_mid
            beside_q = jnp.where(
                place == 0,
                1.0,
                jnp.where(
                    place == 1, m_high, jnp.where(place == 2, m_mid, jnp.where(place == 3, m_last, 0.0))
                ),
            ).astype(BF)
            delta = jnp.where(low_q, delta1, delta0)
            high = delta.astype(BF).astype(F32)
            beside_do = jnp.where(
                place == 0, high, jnp.where(place == 1, delta - high, 0.0)
            ).astype(BF)
            e0 = jnp.exp2(dot_nt(q * first_q + beside_q * second_q, ka[0, :keys]))
            e1 = jnp.exp2(dot_nt(q * second_q + beside_q * first_q, ka[1, :keys]))
            ds0 = (e0 * dot_nt(do * first_q + beside_do * second_q, va[0, :keys])).astype(BF)
            ds1 = (e1 * dot_nt(do * second_q + beside_do * first_q, va[1, :keys])).astype(BF)
            dq = dot_nn(ds0, km[0, :keys]) + dot_nn(ds1, km[1, :keys])
            dq_ref[pl.ds(r, tq), :] = (dq * SCORE_SCALE).astype(BF)
            q_t = q.T
            do_t = do.T
            dva[:64, :keys] += dot_nn(do_t[:64], e0.astype(BF))
            dva[64:, :keys] += dot_nn(do_t[64:], e1.astype(BF))
            dka[:64, :keys] += dot_nn(q_t[:64], ds0)
            dka[64:, :keys] += dot_nn(q_t[64:], ds1)
            return c

        lax.fori_loop(0, lax.div(n + tq - 1, tq), tile, 0)
        dk_ref[pl.ds(start, keys), :] = (dka[:, :keys].T * LN2).astype(BF)
        dv_ref[pl.ds(start, keys), :] = dva[:, :keys].T.astype(BF)

    by_keys(plan, own, slot_len, tq, slot)


class Attention:
    def __init__(self, plan, own, slot_len, rows, features):
        self.plan, self.own, self.slot_len = plan, own, slot_len
        self.rows, self.features = rows, features
        self.pairs = features // 128
        self.step = min(256, slot_len)

    def spec(self, shift=0):
        return pl.BlockSpec((self.rows, 128), lambda p, *_: (0, p + shift))

    def call(self, kernel, pairs, in_specs, kinds, scratch, work, *args):
        return pl.pallas_call(
            partial(kernel, self.own, self.slot_len, self.step),
            grid_spec=pltpu.PrefetchScalarGridSpec(
                num_scalar_prefetch=1,
                grid=(pairs,),
                in_specs=in_specs,
                out_specs=[self.spec()] * len(kinds),
                scratch_shapes=scratch,
            ),
            out_shape=[jax.ShapeDtypeStruct((self.rows, pairs * 128), kind) for kind in kinds],
            compiler_params=params_of(),
            cost_estimate=estimate(work * pairs * self.own * self.slot_len**2 * 128),
        )(self.plan, *args)

    def qkv_specs(self, first=0):
        return [self.spec(first), self.spec(self.pairs + first), self.spec(2 * self.pairs + first)]

    def forward(self, qkv):
        scratch = [pltpu.VMEM((2, self.slot_len, 128), BF)] * 2
        scratch += [pltpu.VMEM((self.step, 128), F32)]
        return self.call(
            forward_attention, self.pairs, self.qkv_specs(), (BF, F32, F32, F32), scratch, 3, qkv, qkv, qkv
        )

    def backward(self, first, pairs, qkv, out, inverse, peak, grad):
        scratch = [pltpu.VMEM((2, self.slot_len, 128), BF)] * 3
        scratch += [pltpu.VMEM((128, self.slot_len), F32)] * 2
        return self.call(
            backward_attention,
            pairs,
            self.qkv_specs(first) + [self.spec(first)] * 4,
            (BF, BF, BF),
            scratch,
            6,
            qkv,
            qkv,
            qkv,
            out,
            grad,
            inverse,
            peak,
        )


def swapped(array, axis, distance):
    count = lax.axis_size(axis)
    return lax.ppermute(array, axis, [(i, i ^ distance) for i in range(count)])


def my_bit(axis, distance):
    return lax.rem(lax.div(lax.axis_index(axis), distance), 2)


def halved(array, axis, distance, dim=0):
    size = array.shape[dim] // 2
    mine = my_bit(axis, distance) * size
    theirs = size - mine
    received = swapped(lax.dynamic_slice_in_dim(array, theirs, size, dim), axis, distance)
    return lax.dynamic_slice_in_dim(array, mine, size, dim) + received


def doubled(arrays, axis, distance):
    low = my_bit(axis, distance) == 0
    received = swapped(jnp.concatenate(arrays, 0), axis, distance)
    result, at = [], 0
    for array in arrays:
        other = received[at : at + array.shape[0]]
        at += array.shape[0]
        first = jnp.where(low, array, other)
        result.append(jnp.concatenate([first, jnp.where(low, other, array)], 0))
    return result


def bits(count):
    distances = []
    while count > 1:
        count //= 2
        distances.append(count)
    return distances


class Sum:
    def __init__(self, kept, sent, extra=None):
        self.parts = (kept, sent)
        self.extra = extra
        across = lax.axis_size("dp")
        self.near = [distance for distance in bits(across) if distance == 1]
        self.far = sorted(distance for distance in bits(across) if distance > 1)
        self.blocks = [2 * distance for distance in bits(kept.shape[0])]

    def over_core(self):
        kept, sent = self.parts
        total = kept + swapped(sent, "blk", 1)
        if self.extra is not None:
            total = jnp.concatenate([total, self.extra], 1)
        self.parts = (total,)

    def over_chips(self):
        (total,) = self.parts
        half = total.shape[1] // 2
        one, two = total[:, :half], total[:, half:]
        for distance in self.blocks[:1]:
            one = halved(one, "blk", distance)
        for distance in self.near:
            two = halved(two, "dp", distance, 1)
        self.parts = one, two

    def over_both(self):
        one, two = self.parts
        for distance in self.blocks[1:]:
            one = halved(one, "blk", distance)
        one = one[0]
        for distance in self.near:
            one = halved(one, "dp", distance)
        for distance in self.blocks:
            two = halved(two, "blk", distance)
        self.parts = (jnp.stack([one, two[0]]),)

    def over_next(self):
        for distance in self.far[:1]:
            self.parts = (halved(self.parts[0], "dp", distance, 1),)

    def over_rest(self):
        for distance in self.far[1:]:
            self.parts = (halved(self.parts[0], "dp", distance, 1),)
        self.parts = (self.parts[0][0], self.parts[0][1])

    def back_from_rest(self):
        for distance in reversed(self.far[1:]):
            self.parts = tuple(doubled(self.parts, "dp", distance))


def gathered(sums):
    far, near = sums[0].far[:1], sums[0].near
    one, two = ([item.parts[i] for item in sums] for i in (0, 1))
    for distance in far:
        one = doubled(one, "dp", distance)
    for distance in near:
        two = doubled(two, "dp", distance)
    for distance in near:
        one = doubled(one, "dp", distance)
    for distance in far:
        two = doubled(two, "dp", distance)
    if near and far:
        quarters = [jnp.split(part, 4, 0) for part in two]
        two = [jnp.concatenate([a, c, b, d], 0) for a, b, c, d in quarters]
    return [jnp.concatenate(pair, 0).astype(F32) for pair in zip(one, two)]


def tied(sums, others):
    parts, others = lax.optimization_barrier(([item.parts for item in sums], others))
    for item, part in zip(sums, parts):
        item.parts = tuple(part)
    return others


def on_device(
    tokens,
    cotangent,
    lengths,
    query_weight,
    query_bias,
    key_weight,
    value_weight,
    value_bias,
    out_weight,
    out_bias,
    attention_gain,
    attention_shift,
    inner_weight,
    inner_bias,
    outer_weight,
    outer_bias,
    final_gain,
    final_shift,
):
    devices = lax.axis_size("blk")
    slots, span, features = tokens.shape
    hidden_features = inner_weight.shape[1]
    slot_len = devices * span
    deal = Deal(slots, span)
    own = deal.own
    tile = min(256, slot_len)
    rows = own * slot_len + tile
    width = features
    plan = make_plan(lengths, deal, tile)

    chunks = Chunks(deal, tile)

    def exchange_in(array):
        return deal.exchanged(gather_slots(plan, array, deal)), chunks.specs(features)

    token_parts = exchange_in(tokens)
    cotangent_parts = exchange_in(cotangent)
    small = jnp.concatenate(
        [
            query_bias, value_bias, out_bias, attention_gain,
            attention_shift, outer_bias, final_gain, final_shift,
        ]
    ).reshape(8, features).astype(F32)
    inner_row = inner_bias.reshape(1, hidden_features).astype(F32)
    wide = 3 * features
    square = features * features
    tiles = Rows(plan, own, rows, tile, own * slot_len // tile)
    attention = Attention(plan, own, slot_len, rows, features)
    qkv_weights = (query_weight, key_weight, value_weight)
    feed_weights = (out_weight, inner_weight, outer_weight)
    feed_size = square + 2 * features * hidden_features
    send = ((deal.total, span, features), BF)

    x1, qkv1 = tiles.call(
        partial(qkv_kernel, own, tile, chunks),
        3 * square,
        [token_parts],
        qkv_weights,
        (small,),
        tiled_out=[(features, BF), (wide, BF)],
        past=1,
    )
    context1, exact1, inverse_sum1, peak1 = attention.forward(qkv1)
    normed1, normed2, inverses, act, slope, qkv2 = tiles.call(
        partial(post_kernel, own, tile, width),
        3 * square + feed_size,
        [context1, x1],
        (*feed_weights, *qkv_weights),
        (small, inner_row),
        tiled_out=[
            (features, F32), (features, F32), (128, F32),
            (hidden_features, BF), (hidden_features, BF), (wide, BF),
        ],
        past=5,
    )
    context2, exact2, inverse_sum2, peak2 = attention.forward(qkv2)

    unit = 2 * lax.axis_size("dp")
    share_rows = -(-(2 * hidden_features + features) // (devices * unit)) * unit
    feed_grads = [((devices // 2, share_rows, features), BF)] * 2
    sums_out = [((8, features), F32), ((1, hidden_features), F32)]
    stage = [pltpu.VMEM((SLOTS, features, features), BF), pltpu.SemaphoreType.DMA((SLOTS, devices))]
    feed_scratch = [
        pltpu.VMEM((features, hidden_features), F32),
        pltpu.VMEM((hidden_features, features), F32),
        pltpu.VMEM((features, features), F32),
        pltpu.VMEM((8, features), F32),
        pltpu.VMEM((1, hidden_features), F32),
        *stage,
    ]
    dcontext2, dpre2, output_parts, feed_keep2, feed_send2, sums2, inner_sum2 = tiles.call(
        partial(second_kernel, own, tile, chunks, devices, width),
        3 * feed_size,
        [context2, normed2, cotangent_parts],
        feed_weights,
        (small, inner_row),
        tiled_out=[(features, BF), (features, F32)],
        past=0,
        far_out=[send, *feed_grads],
        whole_out=sums_out,
        scratch=[
            *[pltpu.VMEM((tile, hidden_features), BF)] * 2,
            *chunks.scratch(features, BF),
            *feed_scratch,
        ],
    )
    output_parts = deal.exchanged(output_parts)
    dqkv2 = attention.backward(0, attention.pairs, qkv2, exact2, inverse_sum2, peak2, dcontext2)

    qkv_grads = [((devices // 2, 3 * features // devices, features), BF)] * 2
    qkv_scratch = [
        pltpu.VMEM((3, features, features), F32),
        pltpu.VMEM((8, features), F32),
        *stage,
    ]
    dx2, qkv_keep2, qkv_send2, qkv_sums2 = tiles.call(
        partial(qkv_back_kernel, own, tile, None, devices, 1),
        6 * square,
        [*dqkv2, normed2, dpre2],
        qkv_weights,
        (small,),
        tiled_out=[(features, F32)],
        far_out=qkv_grads,
        whole_out=[((8, features), F32)],
        scratch=qkv_scratch,
    )
    output_parts, dx2 = lax.optimization_barrier((output_parts, dx2))
    layer_output = place_slots(plan, lengths, output_parts, deal, BF)
    dcontext1, dpre1, feed_keep, feed_send, sums, inner_sum = tiles.call(
        partial(first_kernel, own, tile, devices, width),
        2 * feed_size,
        [context1, normed1, normed2, inverses, act, slope, dx2],
        feed_weights,
        (small,),
        far=[(feed_keep2, True), (feed_send2, True), (sums2, False), (inner_sum2, False)],
        tiled_out=[(features, BF), (features, F32)],
        past=0,
        far_out=feed_grads,
        whole_out=sums_out,
        scratch=[*feed_scratch, *stage],
    )
    feed_sum = Sum(feed_keep, feed_send)
    sizes = (1, 3, 2) if attention.pairs == 6 else (attention.pairs,)
    steps = (feed_sum.over_core, feed_sum.over_chips, feed_sum.over_both)
    dparts, first, grad1 = [], 0, dcontext1
    for size, step in zip(sizes, steps):
        part = attention.backward(first, size, qkv1, exact1, inverse_sum1, peak1, grad1)
        first += size
        step()
        part, grad1, dpre1 = tied([feed_sum], (part, grad1, dpre1))
        dparts.append(part)
    for step in steps[len(sizes) :]:
        step()
    dqkv1 = [part[i] for i in range(3) for part in dparts]
    groups = len(sizes)
    grad_parts, qkv_keep, qkv_send, qkv_sums = tiles.call(
        partial(qkv_back_kernel, own, tile, chunks, devices, groups),
        6 * square,
        [*dqkv1, x1, dpre1],
        qkv_weights,
        (small,),
        far=[(qkv_keep2, True), (qkv_send2, True), (qkv_sums2, False)],
        far_out=[send, *qkv_grads],
        whole_out=[((8, features), F32)],
        scratch=[*qkv_scratch, *stage, *chunks.scratch(features, BF)],
    )
    each = features // devices
    vectors = jnp.concatenate([qkv_sums[:2], sums[1:7]], 0).reshape(8, devices, each)
    vectors = vectors.transpose(1, 0, 2).reshape(devices, 8 * each)
    vectors = jnp.concatenate([vectors, inner_sum.reshape(devices, hidden_features // devices)], 1)
    filled = vectors.shape[1]
    lines = -(-filled // features)
    lines += -(3 * each + lines) % max(64, unit)
    vectors = jnp.pad(vectors, ((0, 0), (0, lines * features - filled)))
    vectors = vectors.reshape(devices // 2, 2, lines, features).astype(BF)
    vectors = halved(vectors, "blk", 1, 1)[:, 0]
    feed_sum.over_next()
    qkv_sum = Sum(qkv_keep, qkv_send, vectors)
    both = [feed_sum, qkv_sum]
    feed_sum.over_rest()
    qkv_sum.over_core()
    qkv_sum.over_chips()
    qkv_sum.over_both()
    grad_parts = deal.exchanged(tied(both, grad_parts))
    feed_sum.back_from_rest()
    qkv_sum.over_next()
    qkv_sum.over_rest()
    tied(both, ())
    qkv_sum.back_from_rest()
    grad_parts = tied(both, grad_parts)
    total_feed, total_qkv = gathered(both)
    input_grad = place_slots(plan, lengths, grad_parts, deal, F32)
    vector = total_qkv[3 * each :].reshape(-1)
    query_b, value_b, out_b, gain_a, shift_a, outer_b, gain_f, shift_f = (
        vector[i * each : (i + 1) * each] for i in range(8)
    )
    inner_b = vector[8 * each : filled]
    inner = jnp.concatenate(
        [total_feed[i * each : (i + 1) * each] for i in range(hidden_features // features)], 1
    )
    after = hidden_features // devices
    outer = total_feed[after : 2 * after]
    return (
        layer_output,
        input_grad,
        total_qkv[:each],
        query_b,
        total_qkv[each : 2 * each],
        total_qkv[2 * each : 3 * each],
        value_b,
        total_feed[2 * after : 2 * after + each],
        out_b,
        gain_a,
        shift_a,
        inner,
        inner_b,
        outer,
        outer_b,
        gain_f,
        shift_f,
    )


def solution(mesh):
    split = P("dp", "blk", None)
    in_specs = (split, split, P("dp")) + (P(),) * 15
    matrix, vector = P("blk", None), P("blk")
    out_specs = (
        split,
        split,
        matrix,
        vector,
        matrix,
        matrix,
        vector,
        matrix,
        vector,
        vector,
        vector,
        matrix,
        vector,
        matrix,
        vector,
        vector,
        vector,
    )
    return jax.shard_map(
        on_device, mesh=mesh, in_specs=in_specs, out_specs=out_specs, check_vma=False
    )
```

```python
from functools import partial
import math

import jax
import jax.numpy as jnp
from jax import lax
from jax.experimental import pallas as pl
from jax.experimental.pallas import tpu as pltpu
from jax.sharding import PartitionSpec as P

HEAD_DIM = 64
EPSILON = 1e-06
NEGATIVE = -1e30
LOG2E = math.log2(math.e)
LN2 = math.log(2.0)
SCORE_SCALE = HEAD_DIM ** (-0.5)
GELU_C = math.sqrt(2.0 / math.pi)
VMEM_LIMIT = 60 * 2**20
BF = jnp.bfloat16
F32 = jnp.float32
(P_QB, P_VB, P_OB, P_AG, P_AS, P_UB, P_FG, P_FS) = range(8)


def dot_nt(a, b):
    return lax.dot_general(a, b, (((1,), (1,)), ((), ())), preferred_element_type=F32)


def dot_nn(a, b):
    return lax.dot_general(a, b, (((1,), (0,)), ((), ())), preferred_element_type=F32)


def dot_tn(a, b):
    return lax.dot_general(a, b, (((0,), (0,)), ((), ())), preferred_element_type=F32)


def params_of(**extra):
    return pltpu.CompilerParams(vmem_limit_bytes=VMEM_LIMIT, **extra)


def estimate(multiply_adds):
    return pl.CostEstimate(flops=2 * int(multiply_adds), bytes_accessed=1024, transcendentals=0)


class Deal:
    def __init__(self, slots, span):
        self.span = span
        self.blocks = lax.axis_size("blk")
        self.groups = 2 if lax.axis_size("dp") % 2 == 0 else 1
        self.devices = self.groups * self.blocks
        self.turns = -(-slots // self.devices)
        self.own = self.groups * self.turns
        self.total = self.devices * self.turns

    def exchanged(self, parts):
        total, span, features = parts.shape
        parts = parts.reshape(self.devices, self.turns * span, features)
        if self.groups == 1:
            parts = lax.all_to_all(parts, "blk", 0, 0)
        else:
            everyone = lax.axis_size("dp") * self.blocks
            together = [
                list(range(i, i + self.devices)) for i in range(0, everyone, self.devices)
            ]
            parts = lax.all_to_all(parts, ("dp", "blk"), 0, 0, axis_index_groups=together)
        return parts.reshape(total, span, features)


def plan_kernel(deal, tile, len_ref, me_ref, out_ref):
    own, devices, turns = deal.own, deal.devices, deal.turns
    slots = len_ref.shape[0] // deal.groups
    side, place = me_ref[0], me_ref[1]
    me = side * deal.blocks + place
    order = 2 * own + 2
    for r in range(deal.total):
        out_ref[order + r] = -1
    for j in range(own):
        out_ref[2 * j + 1] = 0
    for g in range(deal.groups):
        group = side if g == 0 else 1 - side
        for i in range(slots):
            n = len_ref[g * slots + i]
            rank = jnp.int32(0)
            for j in range(slots):
                if j != i:
                    m = len_ref[g * slots + j]
                    before = (m >= n) if j < i else (m > n)
                    rank = rank + before.astype(jnp.int32)
            turn = lax.div(rank, devices)
            column = lax.rem(rank, devices)
            rising = lax.rem(turn + group, 2) == 1
            owner = jnp.where(rising, devices - 1 - column, column)
            if g == 0:
                out_ref[order + owner * turns + turn] = i

            @pl.when(owner == me)
            def _():
                out_ref[2 * (group * turns + turn) + 1] = n

    start = jnp.int32(0)
    for j in range(own):
        out_ref[2 * j] = start
        start = start + lax.div(out_ref[2 * j + 1] + 127, 128) * 128
    out_ref[2 * own] = jnp.maximum(lax.div(start + tile - 1, tile), 1)
    out_ref[2 * own + 1] = place


def make_plan(lengths, deal, tile):
    place = lax.axis_index("blk")
    side = lax.rem(lax.axis_index("dp"), deal.groups)
    if deal.groups == 2:
        lengths = jnp.concatenate([lengths, swapped(lengths, "dp", 1)])
    return pl.pallas_call(
        partial(plan_kernel, deal, tile),
        in_specs=[pl.BlockSpec(memory_space=pltpu.SMEM)] * 2,
        out_specs=pl.BlockSpec(memory_space=pltpu.SMEM),
        out_shape=jax.ShapeDtypeStruct((2 * deal.own + 2 + deal.total,), jnp.int32),
    )(lengths, jnp.stack([side, place]).astype(jnp.int32))


def gather_kernel(count, first, plan, source, out, held, sems_in, sems_out):
    incoming = [
        pltpu.make_async_copy(
            source.at[jnp.maximum(plan[first + i], 0)], held.at[i], sems_in.at[i]
        )
        for i in range(count)
    ]
    outgoing = [
        pltpu.make_async_copy(held.at[i], out.at[i], sems_out.at[i]) for i in range(count)
    ]
    for copy in incoming:
        copy.start()
    for i in range(count):
        incoming[i].wait()
        outgoing[i].start()
    for copy in outgoing:
        copy.wait()


def gather_slots(plan, source, deal):
    slots, span, features = source.shape
    count = deal.total
    return pl.pallas_call(
        partial(gather_kernel, count, 2 * deal.own + 2),
        grid_spec=pltpu.PrefetchScalarGridSpec(
            num_scalar_prefetch=1,
            grid=(1,),
            in_specs=[pl.BlockSpec(memory_space=pl.ANY)],
            out_specs=pl.BlockSpec(memory_space=pl.ANY),
            scratch_shapes=[
                pltpu.VMEM((count, span, features), source.dtype),
                pltpu.SemaphoreType.DMA((count,)),
                pltpu.SemaphoreType.DMA((count,)),
            ],
        ),
        out_shape=jax.ShapeDtypeStruct((count, span, features), source.dtype),
        compiler_params=params_of(),
    )(plan, source)


class Chunks:
    def __init__(self, deal, tile):
        self.own, self.span, self.tile, self.deal = deal.own, deal.span, tile, deal
        self.chunk = min(128, self.span)
        self.count = tile // self.chunk

    def place(self, plan, step, h):
        row = step * self.tile + h * self.chunk
        base, start, length = jnp.int32(0), plan[0], plan[1]
        turns = self.deal.turns
        for j in range(1, self.own):
            later = row >= plan[2 * j]
            base = jnp.where(later, j // turns * self.deal.blocks * turns + j % turns, base)
            start = jnp.where(later, plan[2 * j], start)
            length = jnp.where(later, plan[2 * j + 1], length)
        at = row - start
        valid = at < length
        at = jnp.where(valid, at, 0)
        block = base + lax.div(at, self.span) * turns
        return block, lax.div(lax.rem(at, self.span), self.chunk), valid

    def specs(self, features):
        def index(h):
            def at(i, plan):
                step = jnp.minimum(i, plan[2 * self.own] - 1)
                block, piece, _ = self.place(plan, step, h)
                return block, piece, 0

            return at

        return [
            pl.BlockSpec((1, self.chunk, features), index(h)) for h in range(self.count)
        ]

    def send(self, plan, step, held, out, sems, action):
        for h in range(self.count):
            block, piece, valid = self.place(plan, step, h)

            @pl.when(valid)
            def _():
                at = pl.multiple_of(piece * self.chunk, self.chunk)
                copy = pltpu.make_async_copy(
                    held.at[pl.ds(h * self.chunk, self.chunk)],
                    out.at[block, pl.ds(at, self.chunk)],
                    sems.at[h],
                )
                action(copy)

    def put(self, plan, step, value, held, out, sems):
        @pl.when(step > 0)
        def _():
            self.send(plan, step - 1, held, out, sems, lambda copy: copy.wait())

        held[...] = value
        self.send(plan, step, held, out, sems, lambda copy: copy.start())

        @pl.when(step == plan[2 * self.own] - 1)
        def _():
            self.send(plan, step, held, out, sems, lambda copy: copy.wait())

    def scratch(self, features, kind):
        return [pltpu.VMEM((self.tile, features), kind), pltpu.SemaphoreType.DMA((self.count,))]


def place_kernel(own, plan, lengths, parts, out):
    total, span, features = parts.shape
    order = 2 * own + 2
    row = lax.broadcasted_iota(jnp.int32, (span, features), 0) + plan[2 * own + 1] * span
    for i in range(total):
        slot = plan[order + i]

        @pl.when(slot >= 0)
        def _():
            keep = row < lengths[slot]
            out[slot] = jnp.where(keep, parts[i].astype(F32), 0.0).astype(out.dtype)


def place_slots(plan, lengths, parts, deal, out_type):
    total, span, features = parts.shape
    slots = lengths.shape[0]
    return pl.pallas_call(
        partial(place_kernel, deal.own),
        grid_spec=pltpu.PrefetchScalarGridSpec(
            num_scalar_prefetch=2,
            grid=(1,),
            in_specs=[pl.BlockSpec((total, span, features), lambda i, *_: (0, 0, 0))],
            out_specs=pl.BlockSpec((slots, span, features), lambda i, *_: (0, 0, 0)),
        ),
        out_shape=jax.ShapeDtypeStruct((slots, span, features), out_type),
        compiler_params=params_of(),
    )(plan, lengths, parts)


def rows_valid(plan, own, tile, shape):
    row = lax.broadcasted_iota(jnp.int32, shape, 0) + pl.program_id(0) * tile
    valid = None
    for j in range(own):
        start = plan[2 * j]
        inside = (row >= start) & (row < start + plan[2 * j + 1])
        valid = inside if valid is None else valid | inside
    return valid


def normed_rows(values):
    center = values - jnp.mean(values, axis=-1, keepdims=True)
    inverse = lax.rsqrt(jnp.mean(center * center, axis=-1, keepdims=True) + EPSILON)
    return center * inverse, inverse


def norm_back(grad_out, normed, inverse, gain):
    scaled = grad_out * gain
    mean_part = jnp.mean(scaled, axis=-1, keepdims=True)
    along_part = jnp.mean(scaled * normed, axis=-1, keepdims=True)
    return inverse * (scaled - mean_part - normed * along_part)


def column_sum(values):
    return jnp.sum(values, axis=0, keepdims=True)


def project_qkv(low, wq, wk, wv, small, out):
    features = low.shape[1]
    out[:, :features] = (
        (dot_nn(low, wq[...]) + small[P_QB : P_QB + 1]) * (SCORE_SCALE * LOG2E)
    ).astype(BF)
    out[:, features : 2 * features] = dot_nn(low, wk[...]).astype(BF)
    out[:, 2 * features :] = (dot_nn(low, wv[...]) + small[P_VB : P_VB + 1]).astype(BF)


SLOTS = 3


class Flush:
    def __init__(self, plan, own, devices, results, stage, sems, earlier, stage_in, sems_in):
        self.last = pl.program_id(0) == plan[2 * own] - 1
        self.core = lax.rem(plan[2 * own + 1], 2)
        self.devices, self.results, self.stage, self.sems = devices, results, stage, sems
        self.earlier, self.stage_in, self.sems_in = earlier, stage_in, sems_in
        self.pieces = []
        self.done = 0

    def plan(self, *pieces):
        self.pieces = pieces
        if self.earlier is not None:

            @pl.when(self.last)
            def _():
                for i in range(min(SLOTS, len(pieces))):
                    self.each_in(i, lambda copy: copy.start())

    def each(self, i, arrays, held, sems, outward, action):
        slot = i % SLOTS
        for same in (0, 1):

            @pl.when(self.core == same)
            def _():
                for n, (row, rows, device, at) in enumerate(self.pieces[i]):
                    far = arrays[int(device % 2 != same)].at[device // 2, pl.ds(at, rows)]
                    near = held.at[slot, pl.ds(row, rows)]
                    source, target = (near, far) if outward else (far, near)
                    action(pltpu.make_async_copy(source, target, sems.at[slot, n]))

    def each_in(self, i, action):
        self.each(i, self.earlier, self.stage_in, self.sems_in, False, action)

    def each_out(self, i, action):
        self.each(i, self.results, self.stage, self.sems, True, action)

    def finish(self, loads):
        @pl.when(self.last)
        def _():
            for i, load in enumerate(loads):
                if i >= SLOTS:
                    self.each_out(i - SLOTS, lambda copy: copy.wait())
                value = load()
                if self.earlier is not None:
                    self.each_in(i, lambda copy: copy.wait())
                    value = value + self.stage_in[i % SLOTS].astype(F32)
                self.stage[i % SLOTS] = value.astype(BF)
                self.each_out(i, lambda copy: copy.start())
                if self.earlier is not None and i + SLOTS < len(loads):
                    self.each_in(i + SLOTS, lambda copy: copy.start())
            for i in range(max(0, len(loads) - SLOTS), len(loads)):
                self.each_out(i, lambda copy: copy.wait())


def share_piece(features, devices, at):
    each = features // devices
    return [(b * each, each, b, at) for b in range(devices)]


def feed_layout(features, hidden_features, devices):
    each, share = features // devices, hidden_features // devices
    pieces = []
    for n, c in enumerate(range(0, hidden_features, features)):
        unit = min(features, share)
        pieces.append(
            [
                (row, unit, (c + row) // share, share + (c + row) % share)
                for row in range(0, features, unit)
            ]
        )
        pieces.append(share_piece(features, devices, n * each))
    pieces.append(share_piece(features, devices, 2 * share))
    return pieces


def qkv_kernel(own, tile, chunks, plan, *refs):
    refs = list(refs)
    parts, refs = refs[: chunks.count], refs[chunks.count :]
    wq, wk, wv, small, x_out, out = refs
    x = jnp.concatenate([part[0] for part in parts], 0)
    x = jnp.where(rows_valid(plan, own, tile, x.shape), x, 0)
    x_out[...] = x
    project_qkv(x, wq, wk, wv, small, out)


def project_qkv(low, wq, wk, wv, small, out):
    features = low.shape[1]
    out[:, :features] = (
        (dot_nn(low, wq[...]) + small[P_QB : P_QB + 1]) * (SCORE_SCALE * LOG2E)
    ).astype(BF)
    out[:, features : 2 * features] = dot_nn(low, wk[...]).astype(BF)
    out[:, 2 * features :] = (dot_nn(low, wv[...]) + small[P_VB : P_VB + 1]).astype(BF)


def gelu_parts(u):
    square = u * u
    t = jnp.tanh(u * (GELU_C + (GELU_C * 0.044715) * square))
    half = 0.5 + 0.5 * t
    slope = half + (0.5 * u) * (1.0 - t * t) * (GELU_C + (3 * GELU_C * 0.044715) * square)
    return u * half, slope


def feed_forward(context, x, wo, wi, wu, small, inner_bias, act, slope, width):
    pre = x + (dot_nn(context, wo[...]) + small[P_OB : P_OB + 1])
    normed1, inverse1 = normed_rows(pre)
    middle = normed1 * small[P_AG : P_AG + 1] + small[P_AS : P_AS + 1]
    low = middle.astype(BF)
    feed = None
    for c in range(0, act.shape[1], width):
        cols = slice(c, c + width)
        hidden = dot_nn(low, wi[:, cols]) + inner_bias[:, cols]
        activated, grad = gelu_parts(hidden)
        activated = activated.astype(BF)
        act[:, cols] = activated
        slope[:, cols] = grad.astype(BF)
        part = dot_nn(activated, wu[cols, :])
        feed = part if feed is None else feed + part
    normed2, inverse2 = normed_rows(middle + (feed + small[P_UB : P_UB + 1]))
    return normed1, inverse1, low, normed2, inverse2


def post_kernel(
    own, tile, width, plan, context, x, wo, wi, wu, wq, wk, wv, small, inner_bias,
    normed1_out, normed2_out, inverse_out, act_out, slope_out, qkv_out,
):
    valid = rows_valid(plan, own, tile, x.shape)
    ctx = jnp.where(valid, context[...], 0)
    normed1, inverse1, _, normed2, inverse2 = feed_forward(
        ctx, x[...].astype(F32), wo, wi, wu, small, inner_bias, act_out, slope_out, width
    )
    normed1_out[...] = normed1
    normed2_out[...] = normed2
    lane = lax.broadcasted_iota(jnp.int32, inverse_out.shape, 1)
    inverse_out[...] = jnp.where(lane < 64, inverse1, inverse2)
    low = (normed2 * small[P_FG : P_FG + 1] + small[P_FS : P_FS + 1]).astype(BF)
    project_qkv(low, wq, wk, wv, small, qkv_out)


def feed_back(
    grad, ctx, low, normed1, inverse1, normed2, inverse2, act, slope, wo, wi, wu, small,
    width, acc_inner, acc_outer, acc_out, sums, inner_sum, flush,
):
    flush.plan(*feed_layout(low.shape[1], act.shape[1], flush.devices))
    sums[5:6] += column_sum(grad * normed2)
    sums[6:7] += column_sum(grad)
    dsum = norm_back(grad, normed2, inverse2, small[P_FG : P_FG + 1])
    dfeed = dsum.astype(BF)
    sums[4:5] += column_sum(dfeed.astype(F32))
    dmiddle = dsum
    for c in range(0, act.shape[1], width):
        cols = slice(c, c + width)
        dactive = dot_nt(dfeed, wu[cols, :])
        acc_outer[cols, :] += dot_tn(act[:, cols], dfeed)
        dhidden = (dactive * slope[:, cols].astype(F32)).astype(BF)
        inner_sum[:, cols] += column_sum(dhidden.astype(F32))
        acc_inner[:, cols] += dot_tn(low, dhidden)
        dmiddle = dmiddle + dot_nt(dhidden, wi[:, cols])
    sums[2:3] += column_sum(dmiddle * normed1)
    sums[3:4] += column_sum(dmiddle)
    dpre = norm_back(dmiddle, normed1, inverse1, small[P_AG : P_AG + 1])
    dbranch = dpre.astype(BF)
    sums[1:2] += column_sum(dbranch.astype(F32))
    acc_out[...] += dot_tn(ctx, dbranch)
    dctx = dot_nt(dbranch, wo[...]).astype(BF)
    return dpre, dctx


def feed_loads(acc_inner, acc_outer, acc_out):
    features = acc_inner.shape[0]
    loads = []
    for c in range(0, acc_inner.shape[1], features):
        cols = slice(c, c + features)
        loads.append(lambda cols=cols: acc_outer[cols, :])
        loads.append(lambda cols=cols: acc_inner[:, cols])
    return [*loads, lambda: acc_out[...]]


def second_kernel(own, tile, chunks, devices, width, plan, context, normed_in, *refs):
    refs = list(refs)
    parts, refs = refs[: chunks.count], refs[chunks.count :]
    wo, wi, wu, small, inner_bias = refs[:5]
    dctx_out, dpre_out, layer_out, keep_out, send_out, sums_out, inner_sum_out = refs[5:12]
    act, slope, held, held_sems = refs[12:16]
    acc_inner, acc_outer, acc_out, sums, inner_sum, stage, sems = refs[16:]
    step = pl.program_id(0)

    @pl.when(step == 0)
    def _():
        for ref in (acc_inner, acc_outer, acc_out, sums, inner_sum):
            ref[...] = jnp.zeros_like(ref)

    valid = rows_valid(plan, own, tile, context.shape)
    ctx = jnp.where(valid, context[...], 0)
    x = normed_in[...] * small[P_FG : P_FG + 1] + small[P_FS : P_FS + 1]
    normed1, inverse1, low, normed2, inverse2 = feed_forward(
        ctx, x, wo, wi, wu, small, inner_bias, act, slope, width
    )
    result = (normed2 * small[P_FG : P_FG + 1] + small[P_FS : P_FS + 1]).astype(BF)
    chunks.put(plan, step, result, held, layer_out, held_sems)
    cotangent = jnp.concatenate([part[0] for part in parts], 0)
    grad = jnp.where(valid, cotangent, 0).astype(F32)
    flush = Flush(plan, own, devices, (keep_out, send_out), stage, sems, None, None, None)
    dpre_out[...], dctx_out[...] = feed_back(
        grad, ctx, low, normed1, inverse1, normed2, inverse2, act, slope, wo, wi, wu, small,
        width, acc_inner, acc_outer, acc_out, sums, inner_sum, flush,
    )
    flush.finish(feed_loads(acc_inner, acc_outer, acc_out))
    sums_out[...] = sums[...]
    inner_sum_out[...] = inner_sum[...]


def first_kernel(
    own, tile, devices, width, plan, context, normed1_in, normed2_in, inverse_in, act, slope, grad,
    wo, wi, wu, small, keep_in, send_in, sums_in, inner_sum_in,
    dctx_out, dpre_out, keep_out, send_out, sums_out, inner_sum_out,
    acc_inner, acc_outer, acc_out, sums, inner_sum, stage, sems, stage_in, sems_in,
):
    step = pl.program_id(0)

    @pl.when(step == 0)
    def _():
        for ref in (acc_inner, acc_outer, acc_out):
            ref[...] = jnp.zeros_like(ref)
        sums[...] = sums_in[...]
        inner_sum[...] = inner_sum_in[...]

    valid = rows_valid(plan, own, tile, context.shape)
    ctx = jnp.where(valid, context[...], 0)
    normed1 = normed1_in[...]
    low = (normed1 * small[P_AG : P_AG + 1] + small[P_AS : P_AS + 1]).astype(BF)
    inverse = inverse_in[...]
    flush = Flush(
        plan, own, devices, (keep_out, send_out), stage, sems, (keep_in, send_in), stage_in, sems_in
    )
    dpre_out[...], dctx_out[...] = feed_back(
        grad[...], ctx, low, normed1, inverse[:, 0:1], normed2_in[...], inverse[:, 64:65],
        act, slope, wo, wi, wu, small, width, acc_inner, acc_outer, acc_out, sums, inner_sum, flush,
    )
    flush.finish(feed_loads(acc_inner, acc_outer, acc_out))
    sums_out[...] = sums[...]
    inner_sum_out[...] = inner_sum[...]


def qkv_back_kernel(own, tile, chunks, devices, groups, plan, *refs):
    refs = list(refs)
    dqkv, refs = refs[: 3 * groups], refs[3 * groups :]
    x, dpre, wq, wk, wv, small = refs[:6]
    if chunks is None:
        earlier, stage_in, sems_in = None, None, None
        dx_out, keep_out, send_out, sums_out = refs[6:10]
        rest = refs[10:]
    else:
        keep_in, send_in, sums_in = refs[6:9]
        earlier = (keep_in, send_in)
        dx_out, keep_out, send_out, sums_out = refs[9:13]
        rest = refs[13:]
    acc, sums, stage, sems = rest[:4]
    if chunks is not None:
        stage_in, sems_in, held, held_sems = rest[4:]
    step = pl.program_id(0)

    @pl.when(step == 0)
    def _():
        acc[...] = jnp.zeros_like(acc)
        sums[...] = jnp.zeros_like(sums) if chunks is None else sums_in[...]

    features = acc.shape[1]
    flush = Flush(plan, own, devices, (keep_out, send_out), stage, sems, earlier, stage_in, sems_in)
    flush.plan(*[share_piece(features, devices, i * (features // devices)) for i in range(3)])
    if chunks is None:
        low = (x[...] * small[P_FG : P_FG + 1] + small[P_FS : P_FS + 1]).astype(BF)
    else:
        low = x[...]
    dx = dpre[...]
    for i, (weight, row) in enumerate(((wq, 0), (wk, None), (wv, 1))):
        grad = jnp.concatenate([ref[...] for ref in dqkv[i * groups : (i + 1) * groups]], 1)
        grad = jnp.where(rows_valid(plan, own, tile, grad.shape), grad, 0)
        acc[i] += dot_tn(low, grad)
        if row is not None:
            sums[row : row + 1] += column_sum(grad.astype(F32))
        dx = dx + dot_nt(grad, weight[...])
    if chunks is None:
        dx_out[...] = dx
    else:
        chunks.put(plan, step, dx.astype(BF), held, dx_out, held_sems)
    flush.finish([lambda i=i: acc[i] for i in range(3)])
    sums_out[...] = sums[...]


class Rows:
    def __init__(self, plan, own, rows, tile, steps):
        self.plan, self.own, self.rows, self.tile, self.steps = plan, own, rows, tile, steps

    def tile_spec(self, width, past=False):
        tiles = 2 * self.own
        beyond = 0 if past else 1
        return pl.BlockSpec((self.tile, width), lambda i, plan: (jnp.minimum(i, plan[tiles] - beyond), 0))

    def call(
        self, kernel, work, tiled, weights, whole, far=(), tiled_out=(), far_out=(), whole_out=(), scratch=(), past=None
    ):
        def whole_spec(shape):
            return pl.BlockSpec(shape, lambda i, *_: (0,) * len(shape))

        operands, in_specs = [], []
        for item in tiled:
            if isinstance(item, tuple):
                operands += [item[0]] * len(item[1])
                in_specs += item[1]
            else:
                operands.append(item)
                in_specs.append(self.tile_spec(item.shape[1]))
        operands += [*weights, *whole, *[array for array, _ in far]]
        in_specs += [
            pl.BlockSpec(array.shape, lambda i, *_: (0, 0), pipeline_mode=pl.Buffered(1))
            for array in weights
        ]
        in_specs += [whole_spec(array.shape) for array in whole]
        in_specs += [
            pl.BlockSpec(memory_space=pl.ANY) if is_far else whole_spec(array.shape)
            for array, is_far in far
        ]
        out_specs = [self.tile_spec(width, i == past) for i, (width, _) in enumerate(tiled_out)]
        out_specs += [pl.BlockSpec(memory_space=pl.ANY) for _ in far_out]
        out_specs += [whole_spec(shape) for shape, _ in whole_out]
        out_shape = [jax.ShapeDtypeStruct((self.rows, width), kind) for width, kind in tiled_out]
        out_shape += [jax.ShapeDtypeStruct(shape, kind) for shape, kind in (*far_out, *whole_out)]

        def guarded(plan, *refs):
            @pl.when(pl.program_id(0) < plan[2 * self.own])
            def _():
                kernel(plan, *refs)

            if past is not None:
                ref = refs[len(operands) + past]

                @pl.when(pl.program_id(0) == plan[2 * self.own])
                def _():
                    ref[...] = jnp.zeros_like(ref)

        return pl.pallas_call(
            guarded,
            grid_spec=pltpu.PrefetchScalarGridSpec(
                num_scalar_prefetch=1,
                grid=(self.steps,),
                in_specs=in_specs,
                out_specs=out_specs,
                scratch_shapes=scratch,
            ),
            out_shape=out_shape,
            compiler_params=params_of(),
            cost_estimate=estimate(work * self.steps * self.tile // 2),
        )(self.plan, *operands)


def lane_mask(rows, first, end):
    lane = lax.broadcasted_iota(jnp.int32, (rows, 128), 1)
    return jnp.where((lane >= first) & (lane < end), 1.0, 0.0).astype(BF)


def halves(rows):
    return lane_mask(rows, 0, 64), lane_mask(rows, 64, 128)


def row_mask(rows, end, inside, outside):
    row = lax.broadcasted_iota(jnp.int32, (rows, 128), 0)
    return jnp.where(row < end, inside, outside).astype(BF)


def by_keys(plan, own, slot_len, step_keys, slot):
    for j in range(own):
        n = plan[2 * j + 1]
        for keys in range(step_keys, slot_len + 1, step_keys):

            @pl.when((n > keys - step_keys) & (n <= keys))
            def _():
                slot(j, keys)


def forward_attention(
    own, slot_len, tq, plan, q_ref, k_ref, v_ref, o_ref, of_ref, li_ref, m_ref, ka, va, bad_ref
):
    low_q = lax.broadcasted_iota(jnp.int32, (tq, 128), 1) < 64
    first_q, second_q = halves(tq)
    one0 = lane_mask(tq, 64, 65)
    one1 = lane_mask(tq, 0, 1)

    def slot(safe, j, keys):
        start = pl.multiple_of(plan[2 * j], 128)
        n = plan[2 * j + 1]
        first, second = halves(keys)
        bias = row_mask(keys, n, 0.0, NEGATIVE)
        k = k_ref[pl.ds(start, keys), :]
        v = v_ref[pl.ds(start, keys), :]
        ka[0, :keys] = k * first + bias * lane_mask(keys, 64, 65)
        ka[1, :keys] = k * second + bias * lane_mask(keys, 0, 1)
        va[0, :keys] = v * first + second
        va[1, :keys] = v * second + first

        def tile(i, c):
            r = pl.multiple_of(start + i * tq, 128)
            q = q_ref[pl.ds(r, tq), :]
            s0 = dot_nt(q * first_q + one0, ka[0, :keys])
            s1 = dot_nt(q * second_q + one1, ka[1, :keys])
            m = jnp.zeros((tq, 128), F32)
            if safe:
                m0 = jnp.max(s0, axis=1, keepdims=True)
                m1 = jnp.max(s1, axis=1, keepdims=True)
                s0, s1 = s0 - m0, s1 - m1
                m = jnp.where(low_q, m0, m1)
            o0 = dot_nn(jnp.exp2(s0).astype(BF), va[0, :keys])
            o1 = dot_nn(jnp.exp2(s1).astype(BF), va[1, :keys])
            total = jnp.where(low_q, pltpu.roll(o0, 64, 1), pltpu.roll(o1, 64, 1))
            li = 1.0 / total
            out = jnp.where(low_q, o0, o1) * li
            o_ref[pl.ds(r, tq), :] = out.astype(BF)
            of_ref[pl.ds(r, tq), :] = out
            li_ref[pl.ds(r, tq), :] = li
            m_ref[pl.ds(r, tq), :] = m
            if not safe:
                good = (total > 2.0**-60) & (total < 2.0**80)
                bad_ref[...] = jnp.where(good, bad_ref[...], 1.0)
            return c

        lax.fori_loop(0, lax.div(n + tq - 1, tq), tile, 0)

    bad_ref[...] = jnp.zeros_like(bad_ref)
    by_keys(plan, own, slot_len, tq, partial(slot, False))

    @pl.when(jnp.max(bad_ref[...]) > 0.0)
    def _():
        by_keys(plan, own, slot_len, tq, partial(slot, True))


def backward_attention(
    own, slot_len, tq, plan, q_ref, k_ref, v_ref, o_ref, do_ref, li_ref, m_ref,
    dq_ref, dk_ref, dv_ref, ka, km, va, dka, dva,
):
    lane_q = lax.broadcasted_iota(jnp.int32, (tq, 128), 1)
    low_q = lane_q < 64
    place = lax.rem(lane_q, 64)
    first_q, second_q = halves(tq)

    def slot(j, keys):
        start = pl.multiple_of(plan[2 * j], 128)
        n = plan[2 * j + 1]
        first, second = halves(keys)
        bias = row_mask(keys, n, 0.0, NEGATIVE)
        k = k_ref[pl.ds(start, keys), :]
        v = v_ref[pl.ds(start, keys), :]
        km[0, :keys] = k * first
        km[1, :keys] = k * second
        ka[0, :keys] = k * first + (bias * lane_mask(keys, 64, 65) + lane_mask(keys, 65, 68))
        ka[1, :keys] = k * second + (bias * lane_mask(keys, 0, 1) + lane_mask(keys, 1, 4))
        va[0, :keys] = v * first + lane_mask(keys, 64, 66)
        va[1, :keys] = v * second + lane_mask(keys, 0, 2)
        dka[:, :keys] = jnp.zeros((128, keys), F32)
        dva[:, :keys] = jnp.zeros((128, keys), F32)

        def tile(i, c):
            r = pl.multiple_of(start + i * tq, 128)
            real_q = lax.broadcasted_iota(jnp.int32, (tq, 128), 0) + i * tq < n
            q = q_ref[pl.ds(r, tq), :] * row_mask(tq, n - i * tq, 1.0, 0.0)
            li = jnp.where(real_q, li_ref[pl.ds(r, tq), :], 0.0)
            m = jnp.where(real_q, m_ref[pl.ds(r, tq), :], 0.0)
            do = (do_ref[pl.ds(r, tq), :].astype(F32) * li).astype(BF)
            product = do.astype(F32) * o_ref[pl.ds(r, tq), :]
            delta0 = -jnp.sum(jnp.where(low_q, product, 0.0), axis=1, keepdims=True)
            delta1 = -jnp.sum(jnp.where(low_q, 0.0, product), axis=1, keepdims=True)
            m_other = -pltpu.roll(m, 64, 1)
            m_high = m_other.astype(BF).astype(F32)
            m_mid = (m_other - m_high).astype(BF).astype(F32)
            m_last = m_other - m_high - m_mid
            beside_q = jnp.where(
                place == 0,
                1.0,
                jnp.where(
                    place == 1, m_high, jnp.where(place == 2, m_mid, jnp.where(place == 3, m_last, 0.0))
                ),
            ).astype(BF)
            delta = jnp.where(low_q, delta1, delta0)
            high = delta.astype(BF).astype(F32)
            beside_do = jnp.where(
                place == 0, high, jnp.where(place == 1, delta - high, 0.0)
            ).astype(BF)
            e0 = jnp.exp2(dot_nt(q * first_q + beside_q * second_q, ka[0, :keys]))
            e1 = jnp.exp2(dot_nt(q * second_q + beside_q * first_q, ka[1, :keys]))
            ds0 = (e0 * dot_nt(do * first_q + beside_do * second_q, va[0, :keys])).astype(BF)
            ds1 = (e1 * dot_nt(do * second_q + beside_do * first_q, va[1, :keys])).astype(BF)
            dq = dot_nn(ds0, km[0, :keys]) + dot_nn(ds1, km[1, :keys])
            dq_ref[pl.ds(r, tq), :] = (dq * SCORE_SCALE).astype(BF)
            q_t = q.T
            do_t = do.T
            dva[:64, :keys] += dot_nn(do_t[:64], e0.astype(BF))
            dva[64:, :keys] += dot_nn(do_t[64:], e1.astype(BF))
            dka[:64, :keys] += dot_nn(q_t[:64], ds0)
            dka[64:, :keys] += dot_nn(q_t[64:], ds1)
            return c

        lax.fori_loop(0, lax.div(n + tq - 1, tq), tile, 0)
        dk_ref[pl.ds(start, keys), :] = (dka[:, :keys].T * LN2).astype(BF)
        dv_ref[pl.ds(start, keys), :] = dva[:, :keys].T.astype(BF)

    by_keys(plan, own, slot_len, tq, slot)


class Attention:
    def __init__(self, plan, own, slot_len, rows, features):
        self.plan, self.own, self.slot_len = plan, own, slot_len
        self.rows, self.features = rows, features
        self.pairs = features // 128
        self.step = min(256, slot_len)

    def spec(self, shift=0):
        return pl.BlockSpec((self.rows, 128), lambda p, *_: (0, p + shift))

    def call(self, kernel, pairs, in_specs, kinds, scratch, work, *args):
        return pl.pallas_call(
            partial(kernel, self.own, self.slot_len, self.step),
            grid_spec=pltpu.PrefetchScalarGridSpec(
                num_scalar_prefetch=1,
                grid=(pairs,),
                in_specs=in_specs,
                out_specs=[self.spec()] * len(kinds),
                scratch_shapes=scratch,
            ),
            out_shape=[jax.ShapeDtypeStruct((self.rows, pairs * 128), kind) for kind in kinds],
            compiler_params=params_of(),
            cost_estimate=estimate(work * pairs * self.own * self.slot_len**2 * 128),
        )(self.plan, *args)

    def qkv_specs(self, first=0):
        return [self.spec(first), self.spec(self.pairs + first), self.spec(2 * self.pairs + first)]

    def forward(self, qkv):
        scratch = [pltpu.VMEM((2, self.slot_len, 128), BF)] * 2
        scratch += [pltpu.VMEM((self.step, 128), F32)]
        return self.call(
            forward_attention, self.pairs, self.qkv_specs(), (BF, F32, F32, F32), scratch, 3, qkv, qkv, qkv
        )

    def backward(self, first, pairs, qkv, out, inverse, peak, grad):
        scratch = [pltpu.VMEM((2, self.slot_len, 128), BF)] * 3
        scratch += [pltpu.VMEM((128, self.slot_len), F32)] * 2
        return self.call(
            backward_attention,
            pairs,
            self.qkv_specs(first) + [self.spec(first)] * 4,
            (BF, BF, BF),
            scratch,
            6,
            qkv,
            qkv,
            qkv,
            out,
            grad,
            inverse,
            peak,
        )


def swapped(array, axis, distance):
    count = lax.axis_size(axis)
    return lax.ppermute(array, axis, [(i, i ^ distance) for i in range(count)])


def my_bit(axis, distance):
    return lax.rem(lax.div(lax.axis_index(axis), distance), 2)


def halved(array, axis, distance, dim=0):
    size = array.shape[dim] // 2
    mine = my_bit(axis, distance) * size
    theirs = size - mine
    received = swapped(lax.dynamic_slice_in_dim(array, theirs, size, dim), axis, distance)
    return lax.dynamic_slice_in_dim(array, mine, size, dim) + received


def doubled(arrays, axis, distance):
    low = my_bit(axis, distance) == 0
    received = swapped(jnp.concatenate(arrays, 0), axis, distance)
    result, at = [], 0
    for array in arrays:
        other = received[at : at + array.shape[0]]
        at += array.shape[0]
        first = jnp.where(low, array, other)
        result.append(jnp.concatenate([first, jnp.where(low, other, array)], 0))
    return result


def bits(count):
    distances = []
    while count > 1:
        count //= 2
        distances.append(count)
    return distances


class Sum:
    def __init__(self, kept, sent, extra=None):
        self.parts = (kept, sent)
        self.extra = extra
        across = lax.axis_size("dp")
        self.near = [distance for distance in bits(across) if distance == 1]
        self.far = sorted(distance for distance in bits(across) if distance > 1)
        self.blocks = [2 * distance for distance in bits(kept.shape[0])]

    def over_core(self):
        kept, sent = self.parts
        total = kept + swapped(sent, "blk", 1)
        if self.extra is not None:
            total = jnp.concatenate([total, self.extra], 1)
        self.parts = (total,)

    def over_chips(self):
        (total,) = self.parts
        half = total.shape[1] // 2
        one, two = total[:, :half], total[:, half:]
        for distance in self.blocks[:1]:
            one = halved(one, "blk", distance)
        for distance in self.near:
            two = halved(two, "dp", distance, 1)
        self.parts = one, two

    def over_both(self):
        one, two = self.parts
        for distance in self.blocks[1:]:
            one = halved(one, "blk", distance)
        one = one[0]
        for distance in self.near:
            one = halved(one, "dp", distance)
        for distance in self.blocks:
            two = halved(two, "blk", distance)
        self.parts = (jnp.stack([one, two[0]]),)

    def over_next(self):
        for distance in self.far[:1]:
            self.parts = (halved(self.parts[0], "dp", distance, 1),)

    def over_rest(self):
        for distance in self.far[1:]:
            self.parts = (halved(self.parts[0], "dp", distance, 1),)
        self.parts = (self.parts[0][0], self.parts[0][1])

    def back_from_rest(self):
        for distance in reversed(self.far[1:]):
            self.parts = tuple(doubled(self.parts, "dp", distance))


def gathered(sums):
    far, near = sums[0].far[:1], sums[0].near
    one, two = ([item.parts[i] for item in sums] for i in (0, 1))
    for distance in far:
        one = doubled(one, "dp", distance)
    for distance in near:
        two = doubled(two, "dp", distance)
    for distance in near:
        one = doubled(one, "dp", distance)
    for distance in far:
        two = doubled(two, "dp", distance)
    if near and far:
        quarters = [jnp.split(part, 4, 0) for part in two]
        two = [jnp.concatenate([a, c, b, d], 0) for a, b, c, d in quarters]
    return [jnp.concatenate(pair, 0).astype(F32) for pair in zip(one, two)]


def tied(sums, others):
    parts, others = lax.optimization_barrier(([item.parts for item in sums], others))
    for item, part in zip(sums, parts):
        item.parts = tuple(part)
    return others


def on_device(
    tokens,
    cotangent,
    lengths,
    query_weight,
    query_bias,
    key_weight,
    value_weight,
    value_bias,
    out_weight,
    out_bias,
    attention_gain,
    attention_shift,
    inner_weight,
    inner_bias,
    outer_weight,
    outer_bias,
    final_gain,
    final_shift,
):
    devices = lax.axis_size("blk")
    slots, span, features = tokens.shape
    hidden_features = inner_weight.shape[1]
    slot_len = devices * span
    deal = Deal(slots, span)
    own = deal.own
    tile = min(256, slot_len)
    rows = own * slot_len + tile
    width = features
    plan = make_plan(lengths, deal, tile)

    chunks = Chunks(deal, tile)

    def exchange_in(array):
        return deal.exchanged(gather_slots(plan, array, deal)), chunks.specs(features)

    token_parts = exchange_in(tokens)
    cotangent_parts = exchange_in(cotangent)
    small = jnp.concatenate(
        [
            query_bias, value_bias, out_bias, attention_gain,
            attention_shift, outer_bias, final_gain, final_shift,
        ]
    ).reshape(8, features).astype(F32)
    inner_row = inner_bias.reshape(1, hidden_features).astype(F32)
    wide = 3 * features
    square = features * features
    tiles = Rows(plan, own, rows, tile, own * slot_len // tile)
    attention = Attention(plan, own, slot_len, rows, features)
    qkv_weights = (query_weight, key_weight, value_weight)
    feed_weights = (out_weight, inner_weight, outer_weight)
    feed_size = square + 2 * features * hidden_features
    send = ((deal.total, span, features), BF)

    x1, qkv1 = tiles.call(
        partial(qkv_kernel, own, tile, chunks),
        3 * square,
        [token_parts],
        qkv_weights,
        (small,),
        tiled_out=[(features, BF), (wide, BF)],
        past=1,
    )
    context1, exact1, inverse_sum1, peak1 = attention.forward(qkv1)
    normed1, normed2, inverses, act, slope, qkv2 = tiles.call(
        partial(post_kernel, own, tile, width),
        3 * square + feed_size,
        [context1, x1],
        (*feed_weights, *qkv_weights),
        (small, inner_row),
        tiled_out=[
            (features, F32), (features, F32), (128, F32),
            (hidden_features, BF), (hidden_features, BF), (wide, BF),
        ],
        past=5,
    )
    context2, exact2, inverse_sum2, peak2 = attention.forward(qkv2)

    unit = 2 * lax.axis_size("dp")
    share_rows = -(-(2 * hidden_features + features) // (devices * unit)) * unit
    feed_grads = [((devices // 2, share_rows, features), BF)] * 2
    sums_out = [((8, features), F32), ((1, hidden_features), F32)]
    stage = [pltpu.VMEM((SLOTS, features, features), BF), pltpu.SemaphoreType.DMA((SLOTS, devices))]
    feed_scratch = [
        pltpu.VMEM((features, hidden_features), F32),
        pltpu.VMEM((hidden_features, features), F32),
        pltpu.VMEM((features, features), F32),
        pltpu.VMEM((8, features), F32),
        pltpu.VMEM((1, hidden_features), F32),
        *stage,
    ]
    dcontext2, dpre2, output_parts, feed_keep2, feed_send2, sums2, inner_sum2 = tiles.call(
        partial(second_kernel, own, tile, chunks, devices, width),
        3 * feed_size,
        [context2, normed2, cotangent_parts],
        feed_weights,
        (small, inner_row),
        tiled_out=[(features, BF), (features, F32)],
        past=0,
        far_out=[send, *feed_grads],
        whole_out=sums_out,
        scratch=[
            *[pltpu.VMEM((tile, hidden_features), BF)] * 2,
            *chunks.scratch(features, BF),
            *feed_scratch,
        ],
    )
    output_parts = deal.exchanged(output_parts)
    dqkv2 = attention.backward(0, attention.pairs, qkv2, exact2, inverse_sum2, peak2, dcontext2)

    qkv_grads = [((devices // 2, 3 * features // devices, features), BF)] * 2
    qkv_scratch = [
        pltpu.VMEM((3, features, features), F32),
        pltpu.VMEM((8, features), F32),
        *stage,
    ]
    dx2, qkv_keep2, qkv_send2, qkv_sums2 = tiles.call(
        partial(qkv_back_kernel, own, tile, None, devices, 1),
        6 * square,
        [*dqkv2, normed2, dpre2],
        qkv_weights,
        (small,),
        tiled_out=[(features, F32)],
        far_out=qkv_grads,
        whole_out=[((8, features), F32)],
        scratch=qkv_scratch,
    )
    output_parts, dx2 = lax.optimization_barrier((output_parts, dx2))
    layer_output = place_slots(plan, lengths, output_parts, deal, BF)
    dcontext1, dpre1, feed_keep, feed_send, sums, inner_sum = tiles.call(
        partial(first_kernel, own, tile, devices, width),
        2 * feed_size,
        [context1, normed1, normed2, inverses, act, slope, dx2],
        feed_weights,
        (small,),
        far=[(feed_keep2, True), (feed_send2, True), (sums2, False), (inner_sum2, False)],
        tiled_out=[(features, BF), (features, F32)],
        past=0,
        far_out=feed_grads,
        whole_out=sums_out,
        scratch=[*feed_scratch, *stage],
    )
    feed_sum = Sum(feed_keep, feed_send)
    sizes = (1, 3, 2) if attention.pairs == 6 else (attention.pairs,)
    steps = (feed_sum.over_core, feed_sum.over_chips, feed_sum.over_both)
    dparts, first, grad1 = [], 0, dcontext1
    for size, step in zip(sizes, steps):
        part = attention.backward(first, size, qkv1, exact1, inverse_sum1, peak1, grad1)
        first += size
        step()
        part, grad1, dpre1 = tied([feed_sum], (part, grad1, dpre1))
        dparts.append(part)
    for step in steps[len(sizes) :]:
        step()
    dqkv1 = [part[i] for i in range(3) for part in dparts]
    groups = len(sizes)
    grad_parts, qkv_keep, qkv_send, qkv_sums = tiles.call(
        partial(qkv_back_kernel, own, tile, chunks, devices, groups),
        6 * square,
        [*dqkv1, x1, dpre1],
        qkv_weights,
        (small,),
        far=[(qkv_keep2, True), (qkv_send2, True), (qkv_sums2, False)],
        far_out=[send, *qkv_grads],
        whole_out=[((8, features), F32)],
        scratch=[*qkv_scratch, *stage, *chunks.scratch(features, BF)],
    )
    feed_sum.over_next()
    grad_parts, qkv_keep, qkv_send, qkv_sums = tied(
        [feed_sum], (grad_parts, qkv_keep, qkv_send, qkv_sums)
    )

    each = features // devices
    vectors = jnp.concatenate([qkv_sums[:2], sums[1:7]], 0).reshape(8, devices, each)
    vectors = vectors.transpose(1, 0, 2).reshape(devices, 8 * each)
    vectors = jnp.concatenate([vectors, inner_sum.reshape(devices, hidden_features // devices)], 1)
    filled = vectors.shape[1]
    lines = -(-filled // features)
    lines += -(3 * each + lines) % max(64, unit)
    vectors = jnp.pad(vectors, ((0, 0), (0, lines * features - filled)))
    vectors = vectors.reshape(devices // 2, 2, lines, features).astype(BF)
    vectors = halved(vectors, "blk", 1, 1)[:, 0]
    qkv_sum = Sum(qkv_keep, qkv_send, vectors)
    both = [feed_sum, qkv_sum]
    feed_sum.over_rest()
    qkv_sum.over_core()
    qkv_sum.over_chips()
    qkv_sum.over_both()
    grad_parts = deal.exchanged(tied(both, grad_parts))
    feed_sum.back_from_rest()
    qkv_sum.over_next()
    qkv_sum.over_rest()
    tied(both, ())
    qkv_sum.back_from_rest()
    grad_parts = tied(both, grad_parts)
    total_feed, total_qkv = gathered(both)
    input_grad = place_slots(plan, lengths, grad_parts, deal, F32)
    vector = total_qkv[3 * each :].reshape(-1)
    query_b, value_b, out_b, gain_a, shift_a, outer_b, gain_f, shift_f = (
        vector[i * each : (i + 1) * each] for i in range(8)
    )
    inner_b = vector[8 * each : filled]
    inner = jnp.concatenate(
        [total_feed[i * each : (i + 1) * each] for i in range(hidden_features // features)], 1
    )
    after = hidden_features // devices
    outer = total_feed[after : 2 * after]
    return (
        layer_output,
        input_grad,
        total_qkv[:each],
        query_b,
        total_qkv[each : 2 * each],
        total_qkv[2 * each : 3 * each],
        value_b,
        total_feed[2 * after : 2 * after + each],
        out_b,
        gain_a,
        shift_a,
        inner,
        inner_b,
        outer,
        outer_b,
        gain_f,
        shift_f,
    )


def solution(mesh):
    split = P("dp", "blk", None)
    in_specs = (split, split, P("dp")) + (P(),) * 15
    matrix, vector = P("blk", None), P("blk")
    out_specs = (
        split,
        split,
        matrix,
        vector,
        matrix,
        matrix,
        vector,
        matrix,
        vector,
        vector,
        vector,
        matrix,
        vector,
        matrix,
        vector,
        vector,
        vector,
    )
    return jax.shard_map(
        on_device, mesh=mesh, in_specs=in_specs, out_specs=out_specs, check_vma=False
    )
```

```python
from functools import partial
import math

import jax
import jax.numpy as jnp
from jax import lax
from jax.experimental import pallas as pl
from jax.experimental.pallas import tpu as pltpu
from jax.sharding import PartitionSpec as P

HEAD_DIM = 64
EPSILON = 1e-06
NEGATIVE = -1e30
LOG2E = math.log2(math.e)
LN2 = math.log(2.0)
SCORE_SCALE = HEAD_DIM ** (-0.5)
GELU_C = math.sqrt(2.0 / math.pi)
VMEM_LIMIT = 60 * 2**20
BF = jnp.bfloat16
F32 = jnp.float32
(P_QB, P_VB, P_OB, P_AG, P_AS, P_UB, P_FG, P_FS) = range(8)


def dot_nt(a, b):
    return lax.dot_general(a, b, (((1,), (1,)), ((), ())), preferred_element_type=F32)


def dot_nn(a, b):
    return lax.dot_general(a, b, (((1,), (0,)), ((), ())), preferred_element_type=F32)


def dot_tn(a, b):
    return lax.dot_general(a, b, (((0,), (0,)), ((), ())), preferred_element_type=F32)


def params_of(**extra):
    return pltpu.CompilerParams(vmem_limit_bytes=VMEM_LIMIT, **extra)


def estimate(multiply_adds):
    return pl.CostEstimate(flops=2 * int(multiply_adds), bytes_accessed=1024, transcendentals=0)


class Deal:
    def __init__(self, slots, span):
        self.span = span
        self.blocks = lax.axis_size("blk")
        self.groups = 2 if lax.axis_size("dp") % 2 == 0 else 1
        self.devices = self.groups * self.blocks
        self.turns = -(-slots // self.devices)
        self.own = self.groups * self.turns
        self.total = self.devices * self.turns

    def exchanged(self, parts):
        total, span, features = parts.shape
        parts = parts.reshape(self.devices, self.turns * span, features)
        if self.groups == 1:
            parts = lax.all_to_all(parts, "blk", 0, 0)
        else:
            everyone = lax.axis_size("dp") * self.blocks
            together = [
                list(range(i, i + self.devices)) for i in range(0, everyone, self.devices)
            ]
            parts = lax.all_to_all(parts, ("dp", "blk"), 0, 0, axis_index_groups=together)
        return parts.reshape(total, span, features)


def plan_kernel(deal, tile, len_ref, me_ref, out_ref):
    own, devices, turns = deal.own, deal.devices, deal.turns
    slots = len_ref.shape[0] // deal.groups
    side, place = me_ref[0], me_ref[1]
    me = side * deal.blocks + place
    order = 2 * own + 2
    for r in range(deal.total):
        out_ref[order + r] = -1
    for j in range(own):
        out_ref[2 * j + 1] = 0
    for g in range(deal.groups):
        group = side if g == 0 else 1 - side
        for i in range(slots):
            n = len_ref[g * slots + i]
            rank = jnp.int32(0)
            for j in range(slots):
                if j != i:
                    m = len_ref[g * slots + j]
                    before = (m >= n) if j < i else (m > n)
                    rank = rank + before.astype(jnp.int32)
            turn = lax.div(rank, devices)
            column = lax.rem(rank, devices)
            rising = lax.rem(turn + group, 2) == 1
            owner = jnp.where(rising, devices - 1 - column, column)
            if g == 0:
                out_ref[order + owner * turns + turn] = i

            @pl.when(owner == me)
            def _():
                out_ref[2 * (group * turns + turn) + 1] = n

    start = jnp.int32(0)
    for j in range(own):
        out_ref[2 * j] = start
        start = start + lax.div(out_ref[2 * j + 1] + 127, 128) * 128
    out_ref[2 * own] = jnp.maximum(lax.div(start + tile - 1, tile), 1)
    out_ref[2 * own + 1] = place


def make_plan(lengths, deal, tile):
    place = lax.axis_index("blk")
    side = lax.rem(lax.axis_index("dp"), deal.groups)
    if deal.groups == 2:
        lengths = jnp.concatenate([lengths, swapped(lengths, "dp", 1)])
    return pl.pallas_call(
        partial(plan_kernel, deal, tile),
        in_specs=[pl.BlockSpec(memory_space=pltpu.SMEM)] * 2,
        out_specs=pl.BlockSpec(memory_space=pltpu.SMEM),
        out_shape=jax.ShapeDtypeStruct((2 * deal.own + 2 + deal.total,), jnp.int32),
    )(lengths, jnp.stack([side, place]).astype(jnp.int32))


def gather_kernel(count, first, plan, source, out, held, sems_in, sems_out):
    incoming = [
        pltpu.make_async_copy(
            source.at[jnp.maximum(plan[first + i], 0)], held.at[i], sems_in.at[i]
        )
        for i in range(count)
    ]
    outgoing = [
        pltpu.make_async_copy(held.at[i], out.at[i], sems_out.at[i]) for i in range(count)
    ]
    for copy in incoming:
        copy.start()
    for i in range(count):
        incoming[i].wait()
        outgoing[i].start()
    for copy in outgoing:
        copy.wait()


def gather_slots(plan, source, deal):
    slots, span, features = source.shape
    count = deal.total
    return pl.pallas_call(
        partial(gather_kernel, count, 2 * deal.own + 2),
        grid_spec=pltpu.PrefetchScalarGridSpec(
            num_scalar_prefetch=1,
            grid=(1,),
            in_specs=[pl.BlockSpec(memory_space=pl.ANY)],
            out_specs=pl.BlockSpec(memory_space=pl.ANY),
            scratch_shapes=[
                pltpu.VMEM((count, span, features), source.dtype),
                pltpu.SemaphoreType.DMA((count,)),
                pltpu.SemaphoreType.DMA((count,)),
            ],
        ),
        out_shape=jax.ShapeDtypeStruct((count, span, features), source.dtype),
        compiler_params=params_of(),
    )(plan, source)


class Chunks:
    def __init__(self, deal, tile):
        self.own, self.span, self.tile, self.deal = deal.own, deal.span, tile, deal
        self.chunk = min(128, self.span)
        self.count = tile // self.chunk

    def place(self, plan, step, h):
        row = step * self.tile + h * self.chunk
        base, start, length = jnp.int32(0), plan[0], plan[1]
        turns = self.deal.turns
        for j in range(1, self.own):
            later = row >= plan[2 * j]
            base = jnp.where(later, j // turns * self.deal.blocks * turns + j % turns, base)
            start = jnp.where(later, plan[2 * j], start)
            length = jnp.where(later, plan[2 * j + 1], length)
        at = row - start
        valid = at < length
        at = jnp.where(valid, at, 0)
        block = base + lax.div(at, self.span) * turns
        return block, lax.div(lax.rem(at, self.span), self.chunk), valid

    def specs(self, features):
        def index(h):
            def at(i, plan):
                step = jnp.minimum(i, plan[2 * self.own] - 1)
                block, piece, _ = self.place(plan, step, h)
                return block, piece, 0

            return at

        return [
            pl.BlockSpec((1, self.chunk, features), index(h)) for h in range(self.count)
        ]

    def send(self, plan, step, held, out, sems, action):
        for h in range(self.count):
            block, piece, valid = self.place(plan, step, h)

            @pl.when(valid)
            def _():
                at = pl.multiple_of(piece * self.chunk, self.chunk)
                copy = pltpu.make_async_copy(
                    held.at[pl.ds(h * self.chunk, self.chunk)],
                    out.at[block, pl.ds(at, self.chunk)],
                    sems.at[h],
                )
                action(copy)

    def put(self, plan, step, value, held, out, sems):
        @pl.when(step > 0)
        def _():
            self.send(plan, step - 1, held, out, sems, lambda copy: copy.wait())

        held[...] = value
        self.send(plan, step, held, out, sems, lambda copy: copy.start())

        @pl.when(step == plan[2 * self.own] - 1)
        def _():
            self.send(plan, step, held, out, sems, lambda copy: copy.wait())

    def scratch(self, features, kind):
        return [pltpu.VMEM((self.tile, features), kind), pltpu.SemaphoreType.DMA((self.count,))]


def place_kernel(own, plan, lengths, parts, out):
    total, span, features = parts.shape
    order = 2 * own + 2
    row = lax.broadcasted_iota(jnp.int32, (span, features), 0) + plan[2 * own + 1] * span
    for i in range(total):
        slot = plan[order + i]

        @pl.when(slot >= 0)
        def _():
            keep = row < lengths[slot]
            out[slot] = jnp.where(keep, parts[i].astype(F32), 0.0).astype(out.dtype)


def place_slots(plan, lengths, parts, deal, out_type):
    total, span, features = parts.shape
    slots = lengths.shape[0]
    return pl.pallas_call(
        partial(place_kernel, deal.own),
        grid_spec=pltpu.PrefetchScalarGridSpec(
            num_scalar_prefetch=2,
            grid=(1,),
            in_specs=[pl.BlockSpec((total, span, features), lambda i, *_: (0, 0, 0))],
            out_specs=pl.BlockSpec((slots, span, features), lambda i, *_: (0, 0, 0)),
        ),
        out_shape=jax.ShapeDtypeStruct((slots, span, features), out_type),
        compiler_params=params_of(),
    )(plan, lengths, parts)


def rows_valid(plan, own, tile, shape):
    row = lax.broadcasted_iota(jnp.int32, shape, 0) + pl.program_id(0) * tile
    valid = None
    for j in range(own):
        start = plan[2 * j]
        inside = (row >= start) & (row < start + plan[2 * j + 1])
        valid = inside if valid is None else valid | inside
    return valid


def normed_rows(values):
    center = values - jnp.mean(values, axis=-1, keepdims=True)
    inverse = lax.rsqrt(jnp.mean(center * center, axis=-1, keepdims=True) + EPSILON)
    return center * inverse, inverse


def norm_back(grad_out, normed, inverse, gain):
    scaled = grad_out * gain
    mean_part = jnp.mean(scaled, axis=-1, keepdims=True)
    along_part = jnp.mean(scaled * normed, axis=-1, keepdims=True)
    return inverse * (scaled - mean_part - normed * along_part)


def column_sum(values):
    return jnp.sum(values, axis=0, keepdims=True)


def project_qkv(low, wq, wk, wv, small, out):
    features = low.shape[1]
    out[:, :features] = (
        (dot_nn(low, wq[...]) + small[P_QB : P_QB + 1]) * (SCORE_SCALE * LOG2E)
    ).astype(BF)
    out[:, features : 2 * features] = dot_nn(low, wk[...]).astype(BF)
    out[:, 2 * features :] = (dot_nn(low, wv[...]) + small[P_VB : P_VB + 1]).astype(BF)


SLOTS = 3


class Flush:
    def __init__(self, plan, own, devices, results, stage, sems, earlier, stage_in, sems_in):
        self.last = pl.program_id(0) == plan[2 * own] - 1
        self.core = lax.rem(plan[2 * own + 1], 2)
        self.devices, self.results, self.stage, self.sems = devices, results, stage, sems
        self.earlier, self.stage_in, self.sems_in = earlier, stage_in, sems_in
        self.pieces = []
        self.done = 0

    def plan(self, *pieces):
        self.pieces = pieces
        if self.earlier is not None:

            @pl.when(self.last)
            def _():
                for i in range(min(SLOTS, len(pieces))):
                    self.each_in(i, lambda copy: copy.start())

    def each(self, i, arrays, held, sems, outward, action):
        slot = i % SLOTS
        for same in (0, 1):

            @pl.when(self.core == same)
            def _():
                for n, (row, rows, device, at) in enumerate(self.pieces[i]):
                    far = arrays[int(device % 2 != same)].at[device // 2, pl.ds(at, rows)]
                    near = held.at[slot, pl.ds(row, rows)]
                    source, target = (near, far) if outward else (far, near)
                    action(pltpu.make_async_copy(source, target, sems.at[slot, n]))

    def each_in(self, i, action):
        self.each(i, self.earlier, self.stage_in, self.sems_in, False, action)

    def each_out(self, i, action):
        self.each(i, self.results, self.stage, self.sems, True, action)

    def finish(self, loads):
        @pl.when(self.last)
        def _():
            for i, load in enumerate(loads):
                if i >= SLOTS:
                    self.each_out(i - SLOTS, lambda copy: copy.wait())
                value = load()
                if self.earlier is not None:
                    self.each_in(i, lambda copy: copy.wait())
                    value = value + self.stage_in[i % SLOTS].astype(F32)
                self.stage[i % SLOTS] = value.astype(BF)
                self.each_out(i, lambda copy: copy.start())
                if self.earlier is not None and i + SLOTS < len(loads):
                    self.each_in(i + SLOTS, lambda copy: copy.start())
            for i in range(max(0, len(loads) - SLOTS), len(loads)):
                self.each_out(i, lambda copy: copy.wait())


def share_piece(features, devices, at):
    each = features // devices
    return [(b * each, each, b, at) for b in range(devices)]


def feed_layout(features, hidden_features, devices):
    each, share = features // devices, hidden_features // devices
    pieces = []
    for n, c in enumerate(range(0, hidden_features, features)):
        unit = min(features, share)
        pieces.append(
            [
                (row, unit, (c + row) // share, share + (c + row) % share)
                for row in range(0, features, unit)
            ]
        )
        pieces.append(share_piece(features, devices, n * each))
    pieces.append(share_piece(features, devices, 2 * share))
    return pieces


def qkv_kernel(own, tile, chunks, plan, *refs):
    refs = list(refs)
    parts, refs = refs[: chunks.count], refs[chunks.count :]
    wq, wk, wv, small, x_out, out = refs
    x = jnp.concatenate([part[0] for part in parts], 0)
    x = jnp.where(rows_valid(plan, own, tile, x.shape), x, 0)
    x_out[...] = x
    project_qkv(x, wq, wk, wv, small, out)


def project_qkv(low, wq, wk, wv, small, out):
    features = low.shape[1]
    out[:, :features] = (
        (dot_nn(low, wq[...]) + small[P_QB : P_QB + 1]) * (SCORE_SCALE * LOG2E)
    ).astype(BF)
    out[:, features : 2 * features] = dot_nn(low, wk[...]).astype(BF)
    out[:, 2 * features :] = (dot_nn(low, wv[...]) + small[P_VB : P_VB + 1]).astype(BF)


def gelu_parts(u):
    square = u * u
    t = jnp.tanh(u * (GELU_C + (GELU_C * 0.044715) * square))
    half = 0.5 + 0.5 * t
    slope = half + (0.5 * u) * (1.0 - t * t) * (GELU_C + (3 * GELU_C * 0.044715) * square)
    return u * half, slope


def feed_forward(context, x, wo, wi, wu, small, inner_bias, act, slope, width):
    pre = x + (dot_nn(context, wo[...]) + small[P_OB : P_OB + 1])
    normed1, inverse1 = normed_rows(pre)
    middle = normed1 * small[P_AG : P_AG + 1] + small[P_AS : P_AS + 1]
    low = middle.astype(BF)
    feed = None
    for c in range(0, act.shape[1], width):
        cols = slice(c, c + width)
        hidden = dot_nn(low, wi[:, cols]) + inner_bias[:, cols]
        activated, grad = gelu_parts(hidden)
        activated = activated.astype(BF)
        act[:, cols] = activated
        slope[:, cols] = grad.astype(BF)
        part = dot_nn(activated, wu[cols, :])
        feed = part if feed is None else feed + part
    normed2, inverse2 = normed_rows(middle + (feed + small[P_UB : P_UB + 1]))
    return normed1, inverse1, low, normed2, inverse2


def post_kernel(
    own, tile, width, plan, context, x, wo, wi, wu, wq, wk, wv, small, inner_bias,
    normed1_out, normed2_out, inverse_out, act_out, slope_out, qkv_out,
):
    valid = rows_valid(plan, own, tile, x.shape)
    ctx = jnp.where(valid, context[...], 0)
    normed1, inverse1, _, normed2, inverse2 = feed_forward(
        ctx, x[...].astype(F32), wo, wi, wu, small, inner_bias, act_out, slope_out, width
    )
    normed1_out[...] = normed1
    normed2_out[...] = normed2
    lane = lax.broadcasted_iota(jnp.int32, inverse_out.shape, 1)
    inverse_out[...] = jnp.where(lane < 64, inverse1, inverse2)
    low = (normed2 * small[P_FG : P_FG + 1] + small[P_FS : P_FS + 1]).astype(BF)
    project_qkv(low, wq, wk, wv, small, qkv_out)


def feed_back(
    grad, ctx, low, normed1, inverse1, normed2, inverse2, act, slope, wo, wi, wu, small,
    width, acc_inner, acc_outer, acc_out, sums, inner_sum, flush,
):
    flush.plan(*feed_layout(low.shape[1], act.shape[1], flush.devices))
    sums[5:6] += column_sum(grad * normed2)
    sums[6:7] += column_sum(grad)
    dsum = norm_back(grad, normed2, inverse2, small[P_FG : P_FG + 1])
    dfeed = dsum.astype(BF)
    sums[4:5] += column_sum(dfeed.astype(F32))
    dmiddle = dsum
    for c in range(0, act.shape[1], width):
        cols = slice(c, c + width)
        dactive = dot_nt(dfeed, wu[cols, :])
        acc_outer[cols, :] += dot_tn(act[:, cols], dfeed)
        dhidden = (dactive * slope[:, cols].astype(F32)).astype(BF)
        inner_sum[:, cols] += column_sum(dhidden.astype(F32))
        acc_inner[:, cols] += dot_tn(low, dhidden)
        dmiddle = dmiddle + dot_nt(dhidden, wi[:, cols])
    sums[2:3] += column_sum(dmiddle * normed1)
    sums[3:4] += column_sum(dmiddle)
    dpre = norm_back(dmiddle, normed1, inverse1, small[P_AG : P_AG + 1])
    dbranch = dpre.astype(BF)
    sums[1:2] += column_sum(dbranch.astype(F32))
    acc_out[...] += dot_tn(ctx, dbranch)
    dctx = dot_nt(dbranch, wo[...]).astype(BF)
    return dpre, dctx


def feed_loads(acc_inner, acc_outer, acc_out):
    features = acc_inner.shape[0]
    loads = []
    for c in range(0, acc_inner.shape[1], features):
        cols = slice(c, c + features)
        loads.append(lambda cols=cols: acc_outer[cols, :])
        loads.append(lambda cols=cols: acc_inner[:, cols])
    return [*loads, lambda: acc_out[...]]


def second_kernel(own, tile, chunks, devices, width, plan, context, normed_in, *refs):
    refs = list(refs)
    parts, refs = refs[: chunks.count], refs[chunks.count :]
    wo, wi, wu, small, inner_bias = refs[:5]
    dctx_out, dpre_out, layer_out, keep_out, send_out, sums_out, inner_sum_out = refs[5:12]
    act, slope, held, held_sems = refs[12:16]
    acc_inner, acc_outer, acc_out, sums, inner_sum, stage, sems = refs[16:]
    step = pl.program_id(0)

    @pl.when(step == 0)
    def _():
        for ref in (acc_inner, acc_outer, acc_out, sums, inner_sum):
            ref[...] = jnp.zeros_like(ref)

    valid = rows_valid(plan, own, tile, context.shape)
    ctx = jnp.where(valid, context[...], 0)
    x = normed_in[...] * small[P_FG : P_FG + 1] + small[P_FS : P_FS + 1]
    normed1, inverse1, low, normed2, inverse2 = feed_forward(
        ctx, x, wo, wi, wu, small, inner_bias, act, slope, width
    )
    result = (normed2 * small[P_FG : P_FG + 1] + small[P_FS : P_FS + 1]).astype(BF)
    chunks.put(plan, step, result, held, layer_out, held_sems)
    cotangent = jnp.concatenate([part[0] for part in parts], 0)
    grad = jnp.where(valid, cotangent, 0).astype(F32)
    flush = Flush(plan, own, devices, (keep_out, send_out), stage, sems, None, None, None)
    dpre_out[...], dctx_out[...] = feed_back(
        grad, ctx, low, normed1, inverse1, normed2, inverse2, act, slope, wo, wi, wu, small,
        width, acc_inner, acc_outer, acc_out, sums, inner_sum, flush,
    )
    flush.finish(feed_loads(acc_inner, acc_outer, acc_out))
    sums_out[...] = sums[...]
    inner_sum_out[...] = inner_sum[...]


def first_kernel(
    own, tile, devices, width, plan, context, normed1_in, normed2_in, inverse_in, act, slope, grad,
    wo, wi, wu, small, keep_in, send_in, sums_in, inner_sum_in,
    dctx_out, dpre_out, keep_out, send_out, sums_out, inner_sum_out,
    acc_inner, acc_outer, acc_out, sums, inner_sum, stage, sems, stage_in, sems_in,
):
    step = pl.program_id(0)

    @pl.when(step == 0)
    def _():
        for ref in (acc_inner, acc_outer, acc_out):
            ref[...] = jnp.zeros_like(ref)
        sums[...] = sums_in[...]
        inner_sum[...] = inner_sum_in[...]

    valid = rows_valid(plan, own, tile, context.shape)
    ctx = jnp.where(valid, context[...], 0)
    normed1 = normed1_in[...]
    low = (normed1 * small[P_AG : P_AG + 1] + small[P_AS : P_AS + 1]).astype(BF)
    inverse = inverse_in[...]
    flush = Flush(
        plan, own, devices, (keep_out, send_out), stage, sems, (keep_in, send_in), stage_in, sems_in
    )
    dpre_out[...], dctx_out[...] = feed_back(
        grad[...], ctx, low, normed1, inverse[:, 0:1], normed2_in[...], inverse[:, 64:65],
        act, slope, wo, wi, wu, small, width, acc_inner, acc_outer, acc_out, sums, inner_sum, flush,
    )
    flush.finish(feed_loads(acc_inner, acc_outer, acc_out))
    sums_out[...] = sums[...]
    inner_sum_out[...] = inner_sum[...]


def qkv_back_kernel(own, tile, chunks, devices, groups, plan, *refs):
    refs = list(refs)
    dqkv, refs = refs[: 3 * groups], refs[3 * groups :]
    x, dpre, wq, wk, wv, small = refs[:6]
    if chunks is None:
        earlier, stage_in, sems_in = None, None, None
        dx_out, keep_out, send_out, sums_out = refs[6:10]
        rest = refs[10:]
    else:
        keep_in, send_in, sums_in = refs[6:9]
        earlier = (keep_in, send_in)
        dx_out, keep_out, send_out, sums_out = refs[9:13]
        rest = refs[13:]
    acc, sums, stage, sems = rest[:4]
    if chunks is not None:
        stage_in, sems_in, held, held_sems = rest[4:]
    step = pl.program_id(0)

    @pl.when(step == 0)
    def _():
        acc[...] = jnp.zeros_like(acc)
        sums[...] = jnp.zeros_like(sums) if chunks is None else sums_in[...]

    features = acc.shape[1]
    flush = Flush(plan, own, devices, (keep_out, send_out), stage, sems, earlier, stage_in, sems_in)
    flush.plan(*[share_piece(features, devices, i * (features // devices)) for i in range(3)])
    if chunks is None:
        low = (x[...] * small[P_FG : P_FG + 1] + small[P_FS : P_FS + 1]).astype(BF)
    else:
        low = x[...]
    dx = dpre[...]
    for i, (weight, row) in enumerate(((wq, 0), (wk, None), (wv, 1))):
        grad = jnp.concatenate([ref[...] for ref in dqkv[i * groups : (i + 1) * groups]], 1)
        grad = jnp.where(rows_valid(plan, own, tile, grad.shape), grad, 0)
        acc[i] += dot_tn(low, grad)
        if row is not None:
            sums[row : row + 1] += column_sum(grad.astype(F32))
        dx = dx + dot_nt(grad, weight[...])
    if chunks is None:
        dx_out[...] = dx
    else:
        chunks.put(plan, step, dx.astype(BF), held, dx_out, held_sems)
    flush.finish([lambda i=i: acc[i] for i in range(3)])
    sums_out[...] = sums[...]


class Rows:
    def __init__(self, plan, own, rows, tile, steps):
        self.plan, self.own, self.rows, self.tile, self.steps = plan, own, rows, tile, steps

    def tile_spec(self, width, past=False):
        tiles = 2 * self.own
        beyond = 0 if past else 1
        return pl.BlockSpec((self.tile, width), lambda i, plan: (jnp.minimum(i, plan[tiles] - beyond), 0))

    def call(
        self, kernel, work, tiled, weights, whole, far=(), tiled_out=(), far_out=(), whole_out=(), scratch=(), past=None
    ):
        def whole_spec(shape):
            return pl.BlockSpec(shape, lambda i, *_: (0,) * len(shape))

        operands, in_specs = [], []
        for item in tiled:
            if isinstance(item, tuple):
                operands += [item[0]] * len(item[1])
                in_specs += item[1]
            else:
                operands.append(item)
                in_specs.append(self.tile_spec(item.shape[1]))
        operands += [*weights, *whole, *[array for array, _ in far]]
        in_specs += [
            pl.BlockSpec(array.shape, lambda i, *_: (0, 0), pipeline_mode=pl.Buffered(1))
            for array in weights
        ]
        in_specs += [whole_spec(array.shape) for array in whole]
        in_specs += [
            pl.BlockSpec(memory_space=pl.ANY) if is_far else whole_spec(array.shape)
            for array, is_far in far
        ]
        out_specs = [self.tile_spec(width, i == past) for i, (width, _) in enumerate(tiled_out)]
        out_specs += [pl.BlockSpec(memory_space=pl.ANY) for _ in far_out]
        out_specs += [whole_spec(shape) for shape, _ in whole_out]
        out_shape = [jax.ShapeDtypeStruct((self.rows, width), kind) for width, kind in tiled_out]
        out_shape += [jax.ShapeDtypeStruct(shape, kind) for shape, kind in (*far_out, *whole_out)]

        def guarded(plan, *refs):
            @pl.when(pl.program_id(0) < plan[2 * self.own])
            def _():
                kernel(plan, *refs)

            if past is not None:
                ref = refs[len(operands) + past]

                @pl.when(pl.program_id(0) == plan[2 * self.own])
                def _():
                    ref[...] = jnp.zeros_like(ref)

        return pl.pallas_call(
            guarded,
            grid_spec=pltpu.PrefetchScalarGridSpec(
                num_scalar_prefetch=1,
                grid=(self.steps,),
                in_specs=in_specs,
                out_specs=out_specs,
                scratch_shapes=scratch,
            ),
            out_shape=out_shape,
            compiler_params=params_of(),
            cost_estimate=estimate(work * self.steps * self.tile // 2),
        )(self.plan, *operands)


def lane_mask(rows, first, end):
    lane = lax.broadcasted_iota(jnp.int32, (rows, 128), 1)
    return jnp.where((lane >= first) & (lane < end), 1.0, 0.0).astype(BF)


def halves(rows):
    return lane_mask(rows, 0, 64), lane_mask(rows, 64, 128)


def row_mask(rows, end, inside, outside):
    row = lax.broadcasted_iota(jnp.int32, (rows, 128), 0)
    return jnp.where(row < end, inside, outside).astype(BF)


def by_keys(plan, own, slot_len, step_keys, slot):
    for j in range(own):
        n = plan[2 * j + 1]
        for keys in range(step_keys, slot_len + 1, step_keys):

            @pl.when((n > keys - step_keys) & (n <= keys))
            def _():
                slot(j, keys)


def forward_attention(
    own, slot_len, tq, plan, q_ref, k_ref, v_ref, o_ref, of_ref, li_ref, m_ref, ka, va, bad_ref
):
    low_q = lax.broadcasted_iota(jnp.int32, (tq, 128), 1) < 64
    first_q, second_q = halves(tq)
    one0 = lane_mask(tq, 64, 65)
    one1 = lane_mask(tq, 0, 1)

    def slot(safe, j, keys):
        start = pl.multiple_of(plan[2 * j], 128)
        n = plan[2 * j + 1]
        first, second = halves(keys)
        bias = row_mask(keys, n, 0.0, NEGATIVE)
        k = k_ref[pl.ds(start, keys), :]
        v = v_ref[pl.ds(start, keys), :]
        ka[0, :keys] = k * first + bias * lane_mask(keys, 64, 65)
        ka[1, :keys] = k * second + bias * lane_mask(keys, 0, 1)
        va[0, :keys] = v * first + second
        va[1, :keys] = v * second + first

        def tile(i, c):
            r = pl.multiple_of(start + i * tq, 128)
            q = q_ref[pl.ds(r, tq), :]
            s0 = dot_nt(q * first_q + one0, ka[0, :keys])
            s1 = dot_nt(q * second_q + one1, ka[1, :keys])
            m = jnp.zeros((tq, 128), F32)
            if safe:
                m0 = jnp.max(s0, axis=1, keepdims=True)
                m1 = jnp.max(s1, axis=1, keepdims=True)
                s0, s1 = s0 - m0, s1 - m1
                m = jnp.where(low_q, m0, m1)
            o0 = dot_nn(jnp.exp2(s0).astype(BF), va[0, :keys])
            o1 = dot_nn(jnp.exp2(s1).astype(BF), va[1, :keys])
            total = jnp.where(low_q, pltpu.roll(o0, 64, 1), pltpu.roll(o1, 64, 1))
            li = 1.0 / total
            out = jnp.where(low_q, o0, o1) * li
            o_ref[pl.ds(r, tq), :] = out.astype(BF)
            of_ref[pl.ds(r, tq), :] = out
            li_ref[pl.ds(r, tq), :] = li
            m_ref[pl.ds(r, tq), :] = m
            if not safe:
                good = (total > 2.0**-60) & (total < 2.0**80)
                bad_ref[...] = jnp.where(good, bad_ref[...], 1.0)
            return c

        lax.fori_loop(0, lax.div(n + tq - 1, tq), tile, 0)

    bad_ref[...] = jnp.zeros_like(bad_ref)
    by_keys(plan, own, slot_len, tq, partial(slot, False))

    @pl.when(jnp.max(bad_ref[...]) > 0.0)
    def _():
        by_keys(plan, own, slot_len, tq, partial(slot, True))


def backward_attention(
    own, slot_len, tq, plan, q_ref, k_ref, v_ref, o_ref, do_ref, li_ref, m_ref,
    dq_ref, dk_ref, dv_ref, ka, km, va, dka, dva,
):
    lane_q = lax.broadcasted_iota(jnp.int32, (tq, 128), 1)
    low_q = lane_q < 64
    place = lax.rem(lane_q, 64)
    first_q, second_q = halves(tq)

    def slot(j, keys):
        start = pl.multiple_of(plan[2 * j], 128)
        n = plan[2 * j + 1]
        first, second = halves(keys)
        bias = row_mask(keys, n, 0.0, NEGATIVE)
        k = k_ref[pl.ds(start, keys), :]
        v = v_ref[pl.ds(start, keys), :]
        km[0, :keys] = k * first
        km[1, :keys] = k * second
        ka[0, :keys] = k * first + (bias * lane_mask(keys, 64, 65) + lane_mask(keys, 65, 68))
        ka[1, :keys] = k * second + (bias * lane_mask(keys, 0, 1) + lane_mask(keys, 1, 4))
        va[0, :keys] = v * first + lane_mask(keys, 64, 66)
        va[1, :keys] = v * second + lane_mask(keys, 0, 2)
        dka[:, :keys] = jnp.zeros((128, keys), F32)
        dva[:, :keys] = jnp.zeros((128, keys), F32)

        def tile(i, c):
            r = pl.multiple_of(start + i * tq, 128)
            real_q = lax.broadcasted_iota(jnp.int32, (tq, 128), 0) + i * tq < n
            q = q_ref[pl.ds(r, tq), :] * row_mask(tq, n - i * tq, 1.0, 0.0)
            li = jnp.where(real_q, li_ref[pl.ds(r, tq), :], 0.0)
            m = jnp.where(real_q, m_ref[pl.ds(r, tq), :], 0.0)
            do = (do_ref[pl.ds(r, tq), :].astype(F32) * li).astype(BF)
            product = do.astype(F32) * o_ref[pl.ds(r, tq), :]
            delta0 = -jnp.sum(jnp.where(low_q, product, 0.0), axis=1, keepdims=True)
            delta1 = -jnp.sum(jnp.where(low_q, 0.0, product), axis=1, keepdims=True)
            m_other = -pltpu.roll(m, 64, 1)
            m_high = m_other.astype(BF).astype(F32)
            m_mid = (m_other - m_high).astype(BF).astype(F32)
            m_last = m_other - m_high - m_mid
            beside_q = jnp.where(
                place == 0,
                1.0,
                jnp.where(
                    place == 1, m_high, jnp.where(place == 2, m_mid, jnp.where(place == 3, m_last, 0.0))
                ),
            ).astype(BF)
            delta = jnp.where(low_q, delta1, delta0)
            high = delta.astype(BF).astype(F32)
            beside_do = jnp.where(
                place == 0, high, jnp.where(place == 1, delta - high, 0.0)
            ).astype(BF)
            e0 = jnp.exp2(dot_nt(q * first_q + beside_q * second_q, ka[0, :keys]))
            e1 = jnp.exp2(dot_nt(q * second_q + beside_q * first_q, ka[1, :keys]))
            ds0 = (e0 * dot_nt(do * first_q + beside_do * second_q, va[0, :keys])).astype(BF)
            ds1 = (e1 * dot_nt(do * second_q + beside_do * first_q, va[1, :keys])).astype(BF)
            dq = dot_nn(ds0, km[0, :keys]) + dot_nn(ds1, km[1, :keys])
            dq_ref[pl.ds(r, tq), :] = (dq * SCORE_SCALE).astype(BF)
            q_t = q.T
            do_t = do.T
            dva[:64, :keys] += dot_nn(do_t[:64], e0.astype(BF))
            dva[64:, :keys] += dot_nn(do_t[64:], e1.astype(BF))
            dka[:64, :keys] += dot_nn(q_t[:64], ds0)
            dka[64:, :keys] += dot_nn(q_t[64:], ds1)
            return c

        lax.fori_loop(0, lax.div(n + tq - 1, tq), tile, 0)
        dk_ref[pl.ds(start, keys), :] = (dka[:, :keys].T * LN2).astype(BF)
        dv_ref[pl.ds(start, keys), :] = dva[:, :keys].T.astype(BF)

    by_keys(plan, own, slot_len, tq, slot)


class Attention:
    def __init__(self, plan, own, slot_len, rows, features):
        self.plan, self.own, self.slot_len = plan, own, slot_len
        self.rows, self.features = rows, features
        self.pairs = features // 128
        self.step = min(256, slot_len)

    def spec(self, shift=0):
        return pl.BlockSpec((self.rows, 128), lambda p, *_: (0, p + shift))

    def call(self, kernel, pairs, in_specs, kinds, scratch, work, *args):
        return pl.pallas_call(
            partial(kernel, self.own, self.slot_len, self.step),
            grid_spec=pltpu.PrefetchScalarGridSpec(
                num_scalar_prefetch=1,
                grid=(pairs,),
                in_specs=in_specs,
                out_specs=[self.spec()] * len(kinds),
                scratch_shapes=scratch,
            ),
            out_shape=[jax.ShapeDtypeStruct((self.rows, pairs * 128), kind) for kind in kinds],
            compiler_params=params_of(),
            cost_estimate=estimate(work * pairs * self.own * self.slot_len**2 * 128),
        )(self.plan, *args)

    def qkv_specs(self, first=0):
        return [self.spec(first), self.spec(self.pairs + first), self.spec(2 * self.pairs + first)]

    def forward(self, qkv):
        scratch = [pltpu.VMEM((2, self.slot_len, 128), BF)] * 2
        scratch += [pltpu.VMEM((self.step, 128), F32)]
        return self.call(
            forward_attention, self.pairs, self.qkv_specs(), (BF, F32, F32, F32), scratch, 3, qkv, qkv, qkv
        )

    def backward(self, first, pairs, qkv, out, inverse, peak, grad):
        scratch = [pltpu.VMEM((2, self.slot_len, 128), BF)] * 3
        scratch += [pltpu.VMEM((128, self.slot_len), F32)] * 2
        return self.call(
            backward_attention,
            pairs,
            self.qkv_specs(first) + [self.spec(first)] * 4,
            (BF, BF, BF),
            scratch,
            6,
            qkv,
            qkv,
            qkv,
            out,
            grad,
            inverse,
            peak,
        )


def swapped(array, axis, distance):
    count = lax.axis_size(axis)
    return lax.ppermute(array, axis, [(i, i ^ distance) for i in range(count)])


def my_bit(axis, distance):
    return lax.rem(lax.div(lax.axis_index(axis), distance), 2)


def halved(array, axis, distance, dim=0):
    size = array.shape[dim] // 2
    mine = my_bit(axis, distance) * size
    theirs = size - mine
    received = swapped(lax.dynamic_slice_in_dim(array, theirs, size, dim), axis, distance)
    return lax.dynamic_slice_in_dim(array, mine, size, dim) + received


def doubled(arrays, axis, distance):
    low = my_bit(axis, distance) == 0
    received = swapped(jnp.concatenate(arrays, 0), axis, distance)
    result, at = [], 0
    for array in arrays:
        other = received[at : at + array.shape[0]]
        at += array.shape[0]
        first = jnp.where(low, array, other)
        result.append(jnp.concatenate([first, jnp.where(low, other, array)], 0))
    return result


def bits(count):
    distances = []
    while count > 1:
        count //= 2
        distances.append(count)
    return distances


class Sum:
    def __init__(self, kept, sent, extra=None):
        self.parts = (kept, sent)
        self.extra = extra
        across = lax.axis_size("dp")
        self.near = [distance for distance in bits(across) if distance == 1]
        self.far = sorted(distance for distance in bits(across) if distance > 1)
        self.blocks = [2 * distance for distance in bits(kept.shape[0])]

    def over_core(self):
        kept, sent = self.parts
        total = kept + swapped(sent, "blk", 1)
        if self.extra is not None:
            total = jnp.concatenate([total, self.extra], 1)
        self.parts = (total,)

    def over_chips(self):
        (total,) = self.parts
        half = total.shape[1] // 2
        one, two = total[:, :half], total[:, half:]
        for distance in self.blocks[:1]:
            one = halved(one, "blk", distance)
        for distance in self.near:
            two = halved(two, "dp", distance, 1)
        self.parts = one, two

    def over_both(self):
        one, two = self.parts
        for distance in self.blocks[1:]:
            one = halved(one, "blk", distance)
        one = one[0]
        for distance in self.near:
            one = halved(one, "dp", distance)
        for distance in self.blocks:
            two = halved(two, "blk", distance)
        self.parts = (jnp.stack([one, two[0]]),)

    def over_next(self):
        for distance in self.far[:1]:
            self.parts = (halved(self.parts[0], "dp", distance, 1),)

    def over_rest(self):
        for distance in self.far[1:]:
            self.parts = (halved(self.parts[0], "dp", distance, 1),)
        self.parts = (self.parts[0][0], self.parts[0][1])

    def back_from_rest(self):
        for distance in reversed(self.far[1:]):
            self.parts = tuple(doubled(self.parts, "dp", distance))


def gathered(sums):
    far, near = sums[0].far[:1], sums[0].near
    one, two = ([item.parts[i] for item in sums] for i in (0, 1))
    for distance in far:
        one = doubled(one, "dp", distance)
    for distance in near:
        two = doubled(two, "dp", distance)
    for distance in near:
        one = doubled(one, "dp", distance)
    for distance in far:
        two = doubled(two, "dp", distance)
    if near and far:
        quarters = [jnp.split(part, 4, 0) for part in two]
        two = [jnp.concatenate([a, c, b, d], 0) for a, b, c, d in quarters]
    return [jnp.concatenate(pair, 0) for pair in zip(one, two)]


def tied(sums, others):
    parts, others = lax.optimization_barrier(([item.parts for item in sums], others))
    for item, part in zip(sums, parts):
        item.parts = tuple(part)
    return others


def on_device(
    tokens,
    cotangent,
    lengths,
    query_weight,
    query_bias,
    key_weight,
    value_weight,
    value_bias,
    out_weight,
    out_bias,
    attention_gain,
    attention_shift,
    inner_weight,
    inner_bias,
    outer_weight,
    outer_bias,
    final_gain,
    final_shift,
):
    devices = lax.axis_size("blk")
    slots, span, features = tokens.shape
    hidden_features = inner_weight.shape[1]
    slot_len = devices * span
    deal = Deal(slots, span)
    own = deal.own
    tile = min(256, slot_len)
    rows = own * slot_len + tile
    width = features
    plan = make_plan(lengths, deal, tile)

    chunks = Chunks(deal, tile)

    def exchange_in(array):
        return deal.exchanged(gather_slots(plan, array, deal)), chunks.specs(features)

    token_parts = exchange_in(tokens)
    cotangent_parts = exchange_in(cotangent)
    small = jnp.concatenate(
        [
            query_bias, value_bias, out_bias, attention_gain,
            attention_shift, outer_bias, final_gain, final_shift,
        ]
    ).reshape(8, features).astype(F32)
    inner_row = inner_bias.reshape(1, hidden_features).astype(F32)
    wide = 3 * features
    square = features * features
    tiles = Rows(plan, own, rows, tile, own * slot_len // tile)
    attention = Attention(plan, own, slot_len, rows, features)
    qkv_weights = (query_weight, key_weight, value_weight)
    feed_weights = (out_weight, inner_weight, outer_weight)
    feed_size = square + 2 * features * hidden_features
    send = ((deal.total, span, features), BF)

    x1, qkv1 = tiles.call(
        partial(qkv_kernel, own, tile, chunks),
        3 * square,
        [token_parts],
        qkv_weights,
        (small,),
        tiled_out=[(features, BF), (wide, BF)],
        past=1,
    )
    context1, exact1, inverse_sum1, peak1 = attention.forward(qkv1)
    normed1, normed2, inverses, act, slope, qkv2 = tiles.call(
        partial(post_kernel, own, tile, width),
        3 * square + feed_size,
        [context1, x1],
        (*feed_weights, *qkv_weights),
        (small, inner_row),
        tiled_out=[
            (features, F32), (features, F32), (128, F32),
            (hidden_features, BF), (hidden_features, BF), (wide, BF),
        ],
        past=5,
    )
    context2, exact2, inverse_sum2, peak2 = attention.forward(qkv2)

    unit = 2 * lax.axis_size("dp")
    share_rows = -(-(2 * hidden_features + features) // (devices * unit)) * unit
    feed_grads = [((devices // 2, share_rows, features), BF)] * 2
    sums_out = [((8, features), F32), ((1, hidden_features), F32)]
    stage = [pltpu.VMEM((SLOTS, features, features), BF), pltpu.SemaphoreType.DMA((SLOTS, devices))]
    feed_scratch = [
        pltpu.VMEM((features, hidden_features), F32),
        pltpu.VMEM((hidden_features, features), F32),
        pltpu.VMEM((features, features), F32),
        pltpu.VMEM((8, features), F32),
        pltpu.VMEM((1, hidden_features), F32),
        *stage,
    ]
    dcontext2, dpre2, output_parts, feed_keep2, feed_send2, sums2, inner_sum2 = tiles.call(
        partial(second_kernel, own, tile, chunks, devices, width),
        3 * feed_size,
        [context2, normed2, cotangent_parts],
        feed_weights,
        (small, inner_row),
        tiled_out=[(features, BF), (features, F32)],
        past=0,
        far_out=[send, *feed_grads],
        whole_out=sums_out,
        scratch=[
            *[pltpu.VMEM((tile, hidden_features), BF)] * 2,
            *chunks.scratch(features, BF),
            *feed_scratch,
        ],
    )
    output_parts = deal.exchanged(output_parts)
    dqkv2 = attention.backward(0, attention.pairs, qkv2, exact2, inverse_sum2, peak2, dcontext2)

    qkv_grads = [((devices // 2, 3 * features // devices, features), BF)] * 2
    qkv_scratch = [
        pltpu.VMEM((3, features, features), F32),
        pltpu.VMEM((8, features), F32),
        *stage,
    ]
    dx2, qkv_keep2, qkv_send2, qkv_sums2 = tiles.call(
        partial(qkv_back_kernel, own, tile, None, devices, 1),
        6 * square,
        [*dqkv2, normed2, dpre2],
        qkv_weights,
        (small,),
        tiled_out=[(features, F32)],
        far_out=qkv_grads,
        whole_out=[((8, features), F32)],
        scratch=qkv_scratch,
    )
    output_parts, dx2 = lax.optimization_barrier((output_parts, dx2))
    layer_output = place_slots(plan, lengths, output_parts, deal, BF)
    dcontext1, dpre1, feed_keep, feed_send, sums, inner_sum = tiles.call(
        partial(first_kernel, own, tile, devices, width),
        2 * feed_size,
        [context1, normed1, normed2, inverses, act, slope, dx2],
        feed_weights,
        (small,),
        far=[(feed_keep2, True), (feed_send2, True), (sums2, False), (inner_sum2, False)],
        tiled_out=[(features, BF), (features, F32)],
        past=0,
        far_out=feed_grads,
        whole_out=sums_out,
        scratch=[*feed_scratch, *stage],
    )
    feed_sum = Sum(feed_keep, feed_send)
    sizes = (1, 3, 2) if attention.pairs == 6 else (attention.pairs,)
    steps = (feed_sum.over_core, feed_sum.over_chips, feed_sum.over_both)
    dparts, first, grad1 = [], 0, dcontext1
    for size, step in zip(sizes, steps):
        part = attention.backward(first, size, qkv1, exact1, inverse_sum1, peak1, grad1)
        first += size
        step()
        part, grad1, dpre1 = tied([feed_sum], (part, grad1, dpre1))
        dparts.append(part)
    for step in steps[len(sizes) :]:
        step()
    dqkv1 = [part[i] for i in range(3) for part in dparts]
    groups = len(sizes)
    grad_parts, qkv_keep, qkv_send, qkv_sums = tiles.call(
        partial(qkv_back_kernel, own, tile, chunks, devices, groups),
        6 * square,
        [*dqkv1, x1, dpre1],
        qkv_weights,
        (small,),
        far=[(qkv_keep2, True), (qkv_send2, True), (qkv_sums2, False)],
        far_out=[send, *qkv_grads],
        whole_out=[((8, features), F32)],
        scratch=[*qkv_scratch, *stage, *chunks.scratch(features, BF)],
    )
    feed_sum.over_next()
    grad_parts, qkv_keep, qkv_send, qkv_sums = tied(
        [feed_sum], (grad_parts, qkv_keep, qkv_send, qkv_sums)
    )

    each = features // devices
    vectors = jnp.concatenate([qkv_sums[:2], sums[1:7]], 0).reshape(8, devices, each)
    vectors = vectors.transpose(1, 0, 2).reshape(devices, 8 * each)
    vectors = jnp.concatenate([vectors, inner_sum.reshape(devices, hidden_features // devices)], 1)
    filled = vectors.shape[1]
    lines = -(-filled // features)
    lines += -(3 * each + lines) % max(64, unit)
    vectors = jnp.pad(vectors, ((0, 0), (0, lines * features - filled)))
    vectors = vectors.reshape(devices // 2, 2, lines, features).astype(BF)
    vectors = halved(vectors, "blk", 1, 1)[:, 0]
    qkv_sum = Sum(qkv_keep, qkv_send, vectors)
    both = [feed_sum, qkv_sum]
    feed_sum.over_rest()
    qkv_sum.over_core()
    qkv_sum.over_chips()
    qkv_sum.over_both()
    grad_parts = deal.exchanged(tied(both, grad_parts))
    feed_sum.back_from_rest()
    qkv_sum.over_next()
    qkv_sum.over_rest()
    tied(both, ())
    qkv_sum.back_from_rest()
    grad_parts = tied(both, grad_parts)
    total_feed, total_qkv = gathered(both)
    input_grad = place_slots(plan, lengths, grad_parts, deal, F32)
    used = -(-filled // features)
    vector = total_qkv[3 * each : 3 * each + used].reshape(-1).astype(F32)
    query_b, value_b, out_b, gain_a, shift_a, outer_b, gain_f, shift_f = (
        vector[i * each : (i + 1) * each] for i in range(8)
    )
    inner_b = vector[8 * each : filled]
    inner = jnp.concatenate(
        [total_feed[i * each : (i + 1) * each] for i in range(hidden_features // features)], 1
    ).astype(F32)
    after = hidden_features // devices
    outer = total_feed[after : 2 * after].astype(F32)
    return (
        layer_output,
        input_grad,
        total_qkv[:each].astype(F32),
        query_b,
        total_qkv[each : 2 * each].astype(F32),
        total_qkv[2 * each : 3 * each].astype(F32),
        value_b,
        total_feed[2 * after : 2 * after + each].astype(F32),
        out_b,
        gain_a,
        shift_a,
        inner,
        inner_b,
        outer,
        outer_b,
        gain_f,
        shift_f,
    )


def solution(mesh):
    split = P("dp", "blk", None)
    in_specs = (split, split, P("dp")) + (P(),) * 15
    matrix, vector = P("blk", None), P("blk")
    out_specs = (
        split,
        split,
        matrix,
        vector,
        matrix,
        matrix,
        vector,
        matrix,
        vector,
        vector,
        vector,
        matrix,
        vector,
        matrix,
        vector,
        vector,
        vector,
    )
    return jax.shard_map(
        on_device, mesh=mesh, in_specs=in_specs, out_specs=out_specs, check_vma=False
    )
```
